32 devices in a mesh: groups: 2 (over x), tile: 16 (over z, y, core).
Axes of the slice: x: 2, y: 2, z: 4, core: 2. Of those that a mesh axis runs over, the one named last changes fastest.
Arguments:
- observations: bfloat16 [2048, 64, 256], P(('groups', 'tile')), parts along dimension 0, may hold values from -6 to 6
- pixel_geometry: float32 [2048, 8, 256], P(('groups', 'tile')), parts along dimension 0, as said below
- block_counts: int32 [2048], P(('groups', 'tile')), parts along dimension 0, may hold values from 1 to 256, as said below
- block_tiles: int32 [2048], P(('groups', 'tile')), parts along dimension 0, may hold values from 0 to 511, as said below
- cutoff_lists: int32 [512, 3], replicated, may hold values from 0 to 127, as said below
- patch_geometry: float32 [4, 32768], replicated, as said below
- stress: bfloat16 [64, 65536], P(None, ('groups', 'tile')), parts along dimension 1, may hold values from -3 to 3
- screens: bfloat16 [1024, 64, 256], P(('groups', 'tile')), parts along dimension 0, may hold values from -3 to 3
Outputs:
- stress_gradient: float32 [64, 65536], P(None, ('groups', 'tile')), parts along dimension 1
- screen_gradient: float32 [1024, 64, 256], P(('groups', 'tile')), parts along dimension 0
The draws below stay inside these ranges and needn't reach their ends.
There are 2 independent parts, one for each index of `groups`. The reference program is written for one: setup_inputs(seed, part) draws one part's arguments, and reference() takes and returns one part's arrays. A program takes and returns all parts, laid end to end along the dimension named above; an argument that names none is the same for every part. Nothing has to cross between parts.
Inputs may be any that keep to these rules, and one draw needn't show every extreme that they name: `block_tiles`: the owner of tile t is index t // 32 of tile. Among the 64 blocks of one device at most 8 belong to the tiles of one owner, and some owner gets exactly 8 from every device. The live pixels of a block are its first block_counts pixels. `cutoff_lists`: the 3 entries of a row are different patch blocks. `patch_geometry`: depths are 1 or more; compliances are positive. `pixel_geometry`: u and v lie within 0 to 15; weights are positive.
All inputs are finite; a program needn't handle non-finite values.
Results may differ from the reference program's by a relative error of at most 0.0037.
Values may be sent and summed in bfloat16 or wider, within the bound.
No kernel may reach another device: no remote copies, remote signals or barrier semaphores. Data moves between devices by JAX's collectives and lax.ppermute only.
A program may use at most 128 MiB of HBM per device.

```python
import math
import jax
import jax.numpy as jnp
from jax import lax

P_SIZE = 32768
PBLK = 256
PIX = 256
NEAR = 3
E = 64
SG = 16
TILES_DEV = 32
BLK_DEV = 64
BLOCKS = 1024
NT = 512
CAP = 8
SG2 = 256
N_TILE = 16


REGION = 16.0


def draw_pixel_geometry(key, part):
    key = jax.random.fold_in(key, 3)
    keys = jax.random.split(key, 8)
    shape = (BLOCKS, PIX)
    east = jax.random.uniform(keys[0], shape, jnp.float32, 0.0, REGION)
    north = jax.random.uniform(keys[1], shape, jnp.float32, 0.0, REGION)
    along_u = jax.random.uniform(keys[2], shape, jnp.float32, 0.0, SG - 1.0)
    along_v = jax.random.uniform(keys[3], shape, jnp.float32, 0.0, SG - 1.0)
    sight_east = jax.random.uniform(keys[4], shape, jnp.float32, -0.6, 0.6)
    sight_north = jax.random.uniform(keys[5], shape, jnp.float32, -0.6, 0.6)
    sight_up = jax.random.uniform(keys[6], shape, jnp.float32, 0.6, 0.95)
    weight = jnp.exp(jax.random.uniform(keys[7], shape, jnp.float32, math.log(0.03), math.log(0.3)))
    return jnp.stack([east, north, along_u, along_v, sight_east, sight_north, sight_up, weight], axis=1)


def draw_patch_geometry(key, part):
    key = jax.random.fold_in(key, 5)
    keys = jax.random.split(key, 4)
    east = jax.random.uniform(keys[0], (P_SIZE,), jnp.float32, 0.0, REGION)
    north = jax.random.uniform(keys[1], (P_SIZE,), jnp.float32, 0.0, REGION)
    depth = jax.random.uniform(keys[2], (P_SIZE,), jnp.float32, 1.0, 4.0)
    compliance = jnp.exp(jax.random.uniform(keys[3], (P_SIZE,), jnp.float32, math.log(0.3), math.log(3.0)))
    return jnp.stack([east, north, depth, compliance], axis=0)


def draw_block_counts(key, part):
    key = jax.random.fold_in(key, 7)
    first, second = jax.random.split(key)
    counts = jax.random.randint(first, (BLOCKS,), 1, PIX + 1, jnp.int32)
    chosen = jax.random.randint(second, (), 0, BLOCKS, jnp.int32)
    other = (chosen + BLOCKS // 2) % BLOCKS
    return counts.at[chosen].set(PIX).at[other].set(1)


def draw_block_tiles(key, part):
    key = jax.random.fold_in(key, 11)
    keys = jax.random.split(key, 5)
    slots = N_TILE * CAP
    owner_of_slot = jnp.arange(slots, dtype=jnp.int32) // CAP
    level = jax.random.randint(keys[0], (N_TILE,), 0, 4, jnp.int32)
    favored = jax.random.randint(keys[1], (), 0, N_TILE, jnp.int32)
    level = level.at[favored].set(4)
    noise = jax.random.randint(keys[2], (N_TILE, slots), 0, 4096, jnp.int32)
    score = level[owner_of_slot][None, :] * 4096 + noise
    chosen = jnp.argsort(-score, axis=1, stable=True)[:, :BLK_DEV]
    owners = owner_of_slot[chosen]
    shuffle = jnp.argsort(jax.random.randint(keys[3], (N_TILE, BLK_DEV), 0, 1 << 20, jnp.int32), axis=1, stable=True)
    owners = jnp.take_along_axis(owners, shuffle, axis=1)
    inner = jax.random.randint(keys[4], (N_TILE, BLK_DEV), 0, TILES_DEV, jnp.int32)
    return (owners * TILES_DEV + inner).reshape(BLOCKS).astype(jnp.int32)


def draw_cutoff_lists(key, part):
    key = jax.random.fold_in(key, 13)
    scores = jax.random.randint(key, (NT, P_SIZE // PBLK), 0, 1 << 20, jnp.int32)
    return jnp.argsort(scores, axis=1, stable=True)[:, :NEAR].astype(jnp.int32)


def levels(stream_key, shape, pieces, low, top_value):
    level = 1.0
    for axis_at, shards_of in pieces:
        steps = jax.random.uniform(jax.random.fold_in(jax.random.fold_in(stream_key, 6), axis_at), (shards_of,), jnp.float32, low / len(pieces), top_value / len(pieces))
        level = level * jnp.repeat(jnp.exp(steps), shape[axis_at] // shards_of).reshape((-1,) + (1,) * (len(shape) - 1 - axis_at))
    return level


def centred(key, extent, deviation, reach, shards=(), kind=jnp.bfloat16):
    level = levels(key, extent, shards, -0.22, 0.18) if shards else 1.0
    entries = jax.random.normal(key, extent, jnp.float32) * deviation * level
    return jnp.minimum(jnp.maximum(entries, -reach), reach).astype(kind)


def setup_inputs(seed: int = 0, part: int = 0) -> dict:
    key_of = jax.random.split(jax.random.key(seed), 9)
    part_splits = jax.random.split(jax.random.fold_in(key_of[8], part), 9)
    observations = centred(part_splits[0], (BLOCKS, E, PIX), 1.0, 6.0, ((0, 16),))
    pixel_geometry = draw_pixel_geometry(jax.random.fold_in(jax.random.fold_in(key_of[8], part), 71), part)
    block_counts = draw_block_counts(jax.random.fold_in(jax.random.fold_in(key_of[8], part), 71), part)
    block_tiles = draw_block_tiles(jax.random.fold_in(jax.random.fold_in(key_of[8], part), 71), part)
    cutoff_lists = draw_cutoff_lists(jax.random.fold_in(key_of[8], 71), part)
    patch_geometry = draw_patch_geometry(jax.random.fold_in(key_of[8], 71), part)
    stress = centred(part_splits[6], (E, P_SIZE), 0.5, 3.0, ((1, 16),))
    screens = centred(part_splits[7], (NT, E, SG2), 0.5, 3.0, ((0, 16),))
    return dict(observations=observations, pixel_geometry=pixel_geometry, block_counts=block_counts, block_tiles=block_tiles, cutoff_lists=cutoff_lists, patch_geometry=patch_geometry, stress=stress, screens=screens)


def green_block(pixels, patches):
    east = pixels[0][:, None] - patches[0][None, :]
    north = pixels[1][:, None] - patches[1][None, :]
    depth = patches[2][None, :]
    radius = east * east + north * north + depth * depth
    inverse = lax.rsqrt(radius)
    along = pixels[4][:, None] * east + pixels[5][:, None] * north + pixels[6][:, None] * depth
    return (patches[3][None, :] * depth * depth * along * inverse * inverse * inverse).astype(jnp.bfloat16)

def hat_block(pixels, nodes):
    grid = jnp.arange(nodes).astype(jnp.float32)
    across = jnp.maximum(0.0, 1.0 - jnp.abs(pixels[2][:, None] - grid[None, :]))
    upward = jnp.maximum(0.0, 1.0 - jnp.abs(pixels[3][:, None] - grid[None, :]))
    return (across[:, :, None] * upward[:, None, :]).reshape(pixels.shape[1], nodes * nodes).astype(jnp.bfloat16)

def near_pieces(tile, cutoff_lists, patch_blocks, stress_blocks):
    near = cutoff_lists[tile]
    patches = patch_blocks[:, near].reshape(patch_blocks.shape[0], -1)
    stress_near = stress_blocks[:, near].reshape(stress_blocks.shape[0], -1)
    return (near, patches, stress_near)

def predict(green, stress_near):
    return lax.dot_general(stress_near, green, (((1,), (1,)), ((), ())), preferred_element_type=jnp.float32)

def weigh(prediction, screen, hats, observed, pixels, count):
    correction = lax.dot_general(screen, hats, (((1,), (1,)), ((), ())), preferred_element_type=jnp.float32)
    live = jnp.arange(pixels.shape[1]) < count
    scale = jnp.where(live, pixels[7], 0.0)
    return ((prediction + correction - observed.astype(jnp.float32)) * scale[None, :]).astype(jnp.bfloat16)

def reference(observations, pixel_geometry, block_counts, block_tiles, cutoff_lists, patch_geometry, stress, screens):
    blocks = observations.shape[0]
    patch_blocks = patch_geometry.reshape(4, P_SIZE // PBLK, PBLK)
    stress_blocks = stress.reshape(E, P_SIZE // PBLK, PBLK)
    group = 16

    def one(observed, pixels, count, tile):
        near, patches, stress_near = near_pieces(tile, cutoff_lists, patch_blocks, stress_blocks)
        green = green_block(pixels, patches)
        hats = hat_block(pixels, SG)
        weighted = weigh(predict(green, stress_near), screens[tile], hats, observed, pixels, count)
        terms = jnp.dot(weighted, green, preferred_element_type=jnp.float32).reshape(E, NEAR, PBLK)
        return (near, terms, jnp.dot(weighted, hats, preferred_element_type=jnp.float32))

    def step(index, carry):
        grad, screen_grad = carry
        start = (index * group).astype(jnp.int32)
        observed = lax.dynamic_slice_in_dim(observations, start, group, 0)
        pixels = lax.dynamic_slice_in_dim(pixel_geometry, start, group, 0)
        counts = lax.dynamic_slice_in_dim(block_counts, start, group, 0)
        tiles = lax.dynamic_slice_in_dim(block_tiles, start, group, 0)
        near, terms, screen_terms = jax.vmap(one)(observed, pixels, counts, tiles)
        grad = grad.at[:, near.reshape(-1)].add(jnp.moveaxis(terms, 0, 1).reshape(E, group * NEAR, PBLK))
        screen_grad = screen_grad.at[tiles].add(screen_terms)
        return (grad, screen_grad)
    start_grad = jnp.zeros((E, P_SIZE // PBLK, PBLK), jnp.float32)
    start_screen = jnp.zeros(screens.shape, jnp.float32)
    grad, screen_grad = lax.fori_loop(0, blocks // group, step, (start_grad, start_screen))
    return (grad.reshape(E, P_SIZE), screen_grad)
```

```python
import functools

import jax
import jax.numpy as jnp
from jax import lax
from jax.experimental import pallas as pl
from jax.experimental.pallas import tpu as pltpu
from jax.sharding import PartitionSpec as P

PBLK = 256
NEAR = 3
SG = 16
CHUNK = 128
PARTS = 2
NARROW = 3
MIB = 1 << 20


def pack_kernel(local_tiles, parts, each, tiles, counts, obs, pix, *rest):
    obs_out, pix_out = rest[:parts], rest[parts : 2 * parts]
    meta, fill, sems = rest[2 * parts :]
    per = each // parts

    def clear_meta(i, _):
        meta[i] = 0
        return 0

    def clear_fill(i, _):
        fill[i] = 0
        return 0

    lax.fori_loop(0, meta.shape[0], clear_meta, 0)
    lax.fori_loop(0, fill.shape[0], clear_fill, 0)

    def send(b, _):
        tile = tiles[b]
        owner = lax.div(tile, local_tiles)
        rank = fill[owner]
        fill[owner] = rank + 1
        slot = owner * each + rank
        meta[2 * slot] = counts[b]
        meta[2 * slot + 1] = tile
        part = lax.div(rank, per)
        place = owner * per + lax.rem(rank, per)
        for c in range(parts):

            @pl.when(part == c)
            def _():
                pltpu.make_async_copy(obs.at[b], obs_out[c].at[place], sems.at[0]).start()
                pltpu.make_async_copy(pix.at[b], pix_out[c].at[place], sems.at[1]).start()

        return 0

    lax.fori_loop(0, obs.shape[0], send, 0)
    pltpu.make_async_copy(obs, obs, sems.at[0]).wait()
    pltpu.make_async_copy(pix, pix, sems.at[1]).wait()


def pack(observations, pixel_geometry, block_counts, block_tiles, devices, local_tiles, parts):
    blocks = observations.shape[0]
    each = 2 * blocks // devices
    per = each // parts
    smem = pl.BlockSpec(memory_space=pltpu.SMEM)
    hbm = pl.BlockSpec(memory_space=pl.ANY)
    out = pl.pallas_call(
        functools.partial(pack_kernel, local_tiles, parts, each),
        in_specs=[smem, smem, hbm, hbm],
        out_specs=[hbm] * (2 * parts) + [smem],
        out_shape=[
            jax.ShapeDtypeStruct((devices * per,) + observations.shape[1:], observations.dtype)
        ]
        * parts
        + [jax.ShapeDtypeStruct((devices * per,) + pixel_geometry.shape[1:], jnp.float32)] * parts
        + [jax.ShapeDtypeStruct((devices * each * 2,), jnp.int32)],
        scratch_shapes=[pltpu.SMEM((devices,), jnp.int32), pltpu.SemaphoreType.DMA((2,))],
        name="pack",
    )(block_tiles, block_counts, observations, pixel_geometry)
    return out[:parts], out[parts : 2 * parts], out[2 * parts]


def fit_kernel(
    first,
    counts,
    tiles,
    cutoffs,
    places,
    obs,
    pix,
    screens,
    stress,
    patches,
    *rest,
):
    if first:
        grad, screen_grad, items, sems = rest
        grad[...] = jnp.zeros_like(grad)
        screen_grad[...] = jnp.zeros_like(screen_grad)
    else:
        grad_in, screen_in, grad, screen_grad, items, sems = rest
        copies = [
            pltpu.make_async_copy(grad_in, grad, sems.at[0]),
            pltpu.make_async_copy(screen_in, screen_grad, sems.at[1]),
        ]
        for copy in copies:
            copy.start()
        for copy in copies:
            copy.wait()
    width = obs.shape[2]
    local_tiles = screens.shape[0]

    def list_slot(s, total):
        live = lax.div(counts[s] + CHUNK - 1, CHUNK)

        def put(c, at):
            items[at] = s * (width // CHUNK) + c
            return at + 1

        return lax.fori_loop(0, live, put, total)

    total = lax.fori_loop(0, obs.shape[0], list_slot, 0)

    def step(i, _):
        item = items[i]
        slot = lax.div(item, width // CHUNK)
        start = pl.multiple_of(lax.rem(item, width // CHUNK) * CHUNK, CHUNK)
        tile = tiles[slot]
        local = lax.rem(tile, local_tiles)
        rows = pix[slot, :, pl.ds(start, CHUNK)]
        columns = rows.T
        east, north = columns[:, 0:1], columns[:, 1:2]
        le, ln, lu = columns[:, 4:5], columns[:, 5:6], columns[:, 6:7]
        greens, nears = [], []
        prediction = jnp.zeros((obs.shape[1], CHUNK), jnp.float32)
        for k in range(NEAR):
            near = cutoffs[tile * NEAR + k]
            patch = patches[near]
            dx = east - patch[0:1]
            dy = north - patch[1:2]
            inverse = lax.rsqrt(dx * dx + dy * dy + patch[3:4])
            along = le * dx + ln * dy + lu * patch[2:3]
            green = (patch[4:5] * along * inverse * inverse * inverse).astype(jnp.bfloat16)
            prediction += lax.dot_general(
                stress[near], green, (((1,), (1,)), ((), ())), preferred_element_type=jnp.float32
            )
            greens.append(green)
            nears.append(near)
        node = lax.broadcasted_iota(jnp.int32, (SG, CHUNK), 0).astype(jnp.float32)
        across = jnp.maximum(0.0, 1.0 - jnp.abs(rows[2:3] - node))
        upward = jnp.maximum(0.0, 1.0 - jnp.abs(rows[3:4] - node))
        hats = jnp.concatenate(
            [(across[a : a + 1] * upward).astype(jnp.bfloat16) for a in range(SG)], axis=0
        )
        correction = jnp.dot(screens[local], hats, preferred_element_type=jnp.float32)
        lane = lax.broadcasted_iota(jnp.int32, (1, CHUNK), 1) + start
        scale = jnp.where(lane < counts[slot], rows[7:8], 0.0)
        observed = obs[slot, :, pl.ds(start, CHUNK)].astype(jnp.float32)
        weighted = ((prediction + correction - observed) * scale).astype(jnp.bfloat16)
        for near, green in zip(nears, greens):
            place = places[near]
            grad[place] += jnp.dot(weighted, green, preferred_element_type=jnp.float32)
        screen_grad[local] += lax.dot_general(
            weighted, hats, (((1,), (1,)), ((), ())), preferred_element_type=jnp.float32
        )
        return 0

    lax.fori_loop(0, total, step, 0)


def fit(counts, tiles, cutoffs, places, obs, pix, screens, stress, patches, state):
    first = state is None
    blocks, epochs = stress.shape[0], stress.shape[1]
    slots, width = obs.shape[0], obs.shape[2]
    vmem = pl.BlockSpec(memory_space=pltpu.VMEM)
    smem = pl.BlockSpec(memory_space=pltpu.SMEM)
    hbm = pl.BlockSpec(memory_space=pl.ANY)
    extra = () if first else tuple(state)
    return pl.pallas_call(
        functools.partial(fit_kernel, first),
        in_specs=[smem] * 4 + [vmem] * 5 + [hbm] * len(extra),
        out_specs=[vmem, vmem],
        out_shape=[
            jax.ShapeDtypeStruct((blocks, epochs, PBLK), jnp.float32),
            jax.ShapeDtypeStruct(screens.shape, jnp.float32),
        ],
        scratch_shapes=[
            pltpu.SMEM((slots * (width // CHUNK),), jnp.int32),
            pltpu.SemaphoreType.DMA((2,)),
        ],
        compiler_params=pltpu.CompilerParams(vmem_limit_bytes=56 * MIB),
        cost_estimate=pl.CostEstimate(
            flops=slots * 4 * epochs * width * (NEAR + 1) * PBLK,
            bytes_accessed=40 * MIB,
            transcendentals=slots * width * NEAR * PBLK,
        ),
        name="fit",
    )(counts, tiles, cutoffs, places, obs, pix, screens, stress, patches, *extra)


def reduce_scatter(grad, devices):
    stages = devices.bit_length() - 1
    for bit in range(stages):
        half = grad.shape[0] // 2
        kept, given = grad[:half], grad[half:]
        if stages - bit <= NARROW:
            given = given.astype(jnp.bfloat16)
        pairs = [(i, i ^ (1 << bit)) for i in range(devices)]
        grad = kept + lax.ppermute(given, "tile", pairs).astype(jnp.float32)
    return grad


def on_device(
    observations,
    pixel_geometry,
    block_counts,
    block_tiles,
    cutoff_lists,
    patch_geometry,
    stress,
    screens,
):
    devices = lax.axis_size("tile")
    here = lax.axis_index("tile")
    local_tiles = screens.shape[0]
    blocks, epochs, width = observations.shape
    each = 2 * blocks // devices
    parts = min(PARTS, each)
    per = each // parts
    local = stress.shape[1] // PBLK
    mine = jnp.swapaxes(stress.reshape(epochs, local, PBLK), 0, 1)
    full = lax.all_gather(mine, "tile", axis=0, tiled=True)
    patch_blocks = full.shape[0]
    east, north, depth, compliance = patch_geometry
    patches = jnp.stack(
        [east, north, depth, depth * depth, compliance * depth * depth] + [depth] * 3
    )
    patches = jnp.swapaxes(patches.reshape(8, patch_blocks, PBLK), 0, 1)
    stages = devices.bit_length() - 1
    block = jnp.arange(patch_blocks)
    other = (block // local) ^ here
    turned = sum(((other >> b) & 1) << (stages - 1 - b) for b in range(stages))
    places = (turned * local + block % local).astype(jnp.int32)

    obs_parts, pix_parts, meta = pack(
        observations, pixel_geometry, block_counts, block_tiles, devices, local_tiles, parts
    )

    def swap(values):
        split = values.reshape((devices, -1) + values.shape[1:])
        got = lax.all_to_all(split, "tile", split_axis=0, concat_axis=0, tiled=True)
        return got.reshape(values.shape)

    info = swap(meta).reshape(devices, each, 2)
    cutoffs = cutoff_lists.reshape(-1)
    state = None
    for part, (obs, pix) in enumerate(zip(obs_parts, pix_parts)):
        here_info = info[:, part * per : (part + 1) * per].reshape(devices * per, 2)
        state = fit(
            here_info[:, 0],
            here_info[:, 1],
            cutoffs,
            places,
            swap(obs),
            swap(pix),
            screens,
            full,
            patches,
            state,
        )
    grad, screen_gradient = state
    grad = reduce_scatter(grad, devices)
    return (jnp.swapaxes(grad, 0, 1).reshape(epochs, local * PBLK), screen_gradient)


def solution(mesh):
    return jax.shard_map(
        on_device,
        mesh=mesh,
        in_specs=(
            P(("groups", "tile"), None, None),
            P(("groups", "tile"), None, None),
            P(("groups", "tile")),
            P(("groups", "tile")),
            P(),
            P(),
            P(None, ("groups", "tile")),
            P(("groups", "tile"), None, None),
        ),
        out_specs=(P(None, ("groups", "tile")), P(("groups", "tile"), None, None)),
        check_vma=False,
    )
```

```python
import functools

import jax
import jax.numpy as jnp
from jax import lax
from jax.experimental import pallas as pl
from jax.experimental.pallas import tpu as pltpu
from jax.sharding import PartitionSpec as P

PBLK = 256
NEAR = 3
SG = 16
CHUNK = 128
LAYER = 4
PAIR = 2
NARROW = 3
MIB = 1 << 20


def pack_kernel(local_tiles, layers, each, here, tiles, counts, obs, pix, *rest):
    obs_out, pix_out = rest[: 2 * layers], rest[2 * layers : 3 * layers]
    obs_all, pix_all, fill, sems = rest[3 * layers :]
    my_layer, my_seat = lax.div(here[0], LAYER), lax.rem(here[0], LAYER)
    width = pix.shape[2]

    def clear(i, _):
        fill[i] = 0
        return 0

    lax.fori_loop(0, fill.shape[0], clear, 0)
    for x in range(layers):
        pix_all[x, LAYER * each] = jnp.zeros((8, width), jnp.float32)
    lane = lax.broadcasted_iota(jnp.int32, (8, width), 1)
    row = lax.broadcasted_iota(jnp.int32, (8, width), 0)

    def put(b, _):
        tile = tiles[b]
        owner = lax.div(tile, local_tiles)
        rank = fill[owner]
        fill[owner] = rank + 1
        x = lax.div(owner, LAYER) ^ my_layer
        seat = lax.rem(owner, LAYER) ^ my_seat
        half = 1 - lax.div(seat, PAIR)
        place = ((half * layers + x) * PAIR + lax.rem(seat, PAIR)) * each + rank
        slot = seat * each + rank
        obs_all[place] = obs[b]
        pix_all[x, slot] = pix[b]
        entry = jnp.where(row == 0, counts[b], tile).astype(jnp.float32)
        info = pix_all[x, LAYER * each]
        pix_all[x, LAYER * each] = jnp.where((lane == slot) & (row < 2), entry, info)
        return 0

    lax.fori_loop(0, obs.shape[0], put, 0)
    span = PAIR * each
    copies = [
        pltpu.make_async_copy(pix_all.at[x], pix_out[x], sems.at[x]) for x in range(layers)
    ] + [
        pltpu.make_async_copy(obs_all.at[pl.ds(i * span, span)], obs_out[i], sems.at[layers + i])
        for i in range(2 * layers)
    ]
    for copy in copies:
        copy.start()
    for copy in copies:
        copy.wait()


def pack(observations, pixel_geometry, block_counts, block_tiles, here, devices, local_tiles):
    blocks, epochs, width = observations.shape
    each = 2 * blocks // devices
    layers = devices // LAYER
    smem = pl.BlockSpec(memory_space=pltpu.SMEM)
    vmem = pl.BlockSpec(memory_space=pltpu.VMEM)
    hbm = pl.BlockSpec(memory_space=pl.ANY)
    obs_part = jax.ShapeDtypeStruct((PAIR * each, epochs, width), observations.dtype)
    pix_part = jax.ShapeDtypeStruct((LAYER * each + 1, 8, width), jnp.float32)
    out = pl.pallas_call(
        functools.partial(pack_kernel, local_tiles, layers, each),
        in_specs=[smem, smem, smem, vmem, vmem],
        out_specs=[hbm] * (3 * layers),
        out_shape=[obs_part] * (2 * layers) + [pix_part] * layers,
        scratch_shapes=[
            pltpu.VMEM((devices * each, epochs, width), observations.dtype),
            pltpu.VMEM((layers,) + pix_part.shape, jnp.float32),
            pltpu.SMEM((devices,), jnp.int32),
            pltpu.SemaphoreType.DMA((3 * layers,)),
        ],
        compiler_params=pltpu.CompilerParams(vmem_limit_bytes=24 * MIB),
        name="pack",
    )(here, block_tiles, block_counts, observations, pixel_geometry)
    return out[:layers], out[layers : 2 * layers], out[2 * layers :]


def fit_kernel(first, layers, each, *refs):
    info, cutoffs, places = refs[:3]
    obs_in, pix_in = refs[3 : 3 + layers], refs[3 + layers : 3 + 2 * layers]
    rest = refs[3 + 2 * layers :]
    screen_in, stress_in, patches_in = rest[:2], rest[2], rest[3]
    if first:
        grad_out, screen_out = rest[4:5], rest[5:7]
        rest = rest[7:]
    else:
        grad_in, grad_out, screen_out = rest[4], rest[5:7], rest[7:9]
        rest = rest[9:]
    obs, pix, screens, stress, patches, grad, screen_grad = rest[:7]
    green_a, hats_a, green_b, hats_b, items, sems = rest[7:]
    span = PAIR * each
    base = span if first else 0
    local_tiles = screens.shape[0] // 2
    width = obs.shape[2]
    chunks = width // CHUNK

    loads = [
        (stress_in, stress),
        (patches_in, patches),
        (screen_in[0], screens.at[pl.ds(0, local_tiles)]),
        (screen_in[1], screens.at[pl.ds(local_tiles, local_tiles)]),
    ]
    for x in range(layers):
        loads.append((pix_in[x].at[pl.ds(base, span)], pix.at[pl.ds(x * span, span)]))
        loads.append((obs_in[x], obs.at[pl.ds(x * span, span)]))
    if not first:
        loads.append((grad_in, grad))
    loads = [pltpu.make_async_copy(a, b, sems.at[i]) for i, (a, b) in enumerate(loads)]
    for copy in loads:
        copy.start()
    screen_grad[...] = jnp.zeros_like(screen_grad)
    if first:
        grad[...] = jnp.zeros_like(grad)

    def count_of(slot):
        return info[lax.div(slot, span) * 2 * LAYER * each + base + lax.rem(slot, span)]

    def tile_of(slot):
        return info[(lax.div(slot, span) * 2 + 1) * LAYER * each + base + lax.rem(slot, span)]

    def list_slot(slot, total):
        live = lax.div(count_of(slot) + CHUNK - 1, CHUNK)

        def put(c, at):
            items[at] = slot * chunks + c
            return at + 1

        return lax.fori_loop(0, live, put, total)

    total = lax.fori_loop(0, layers * span, list_slot, 0)
    for copy in loads:
        copy.wait()

    def item_of(i):
        item = items[jnp.minimum(i, total - 1)]
        slot = lax.div(item, chunks)
        start = pl.multiple_of(lax.rem(item, chunks) * CHUNK, CHUNK)
        return slot, start, tile_of(slot)

    def make(i, green, hats):
        slot, start, tile = item_of(i)
        rows = pix[slot, :, pl.ds(start, CHUNK)]
        columns = rows.T
        near = [cutoffs[tile * NEAR + k] for k in range(NEAR)]
        for low in range(0, CHUNK, 16):
            strips = [[] for _ in range(NEAR)]
            for at in (low, low + 8):
                east, north, le, ln, lu = (
                    jnp.broadcast_to(columns[at : at + 8, c : c + 1], (8, PBLK))
                    for c in (0, 1, 4, 5, 6)
                )
                for k in range(NEAR):
                    patch = patches.at[near[k]]
                    dx = east - patch[0]
                    dy = north - patch[1]
                    inverse = lax.rsqrt(dx * dx + dy * dy + patch[3])
                    along = le * dx + ln * dy + lu * patch[2]
                    strips[k].append(patch[4] * along * inverse * inverse * inverse)
            for k in range(NEAR):
                green[low : low + 16, k * PBLK : (k + 1) * PBLK] = jnp.concatenate(
                    strips[k], axis=0
                ).astype(jnp.bfloat16)
        node = lax.broadcasted_iota(jnp.int32, (SG, CHUNK), 0).astype(jnp.float32)
        across = jnp.maximum(0.0, 1.0 - jnp.abs(rows[2:3] - node))
        upward = jnp.maximum(0.0, 1.0 - jnp.abs(rows[3:4] - node))
        for a in range(SG):
            hats[a * SG : (a + 1) * SG] = (across[a : a + 1] * upward).astype(jnp.bfloat16)

    def use(i, green, hats):
        slot, start, tile = item_of(i)
        near = [cutoffs[tile * NEAR + k] for k in range(NEAR)]
        screen = lax.div(lax.rem(slot, span), each) * local_tiles + lax.rem(tile, local_tiles)
        model = jnp.dot(screens[screen], hats[...], preferred_element_type=jnp.float32)
        for k in range(NEAR):
            model += lax.dot_general(
                stress[near[k]],
                green[:, k * PBLK : (k + 1) * PBLK],
                (((1,), (1,)), ((), ())),
                preferred_element_type=jnp.float32,
            )
        live = jnp.where(i < total, count_of(slot), 0) - start
        lane = lax.broadcasted_iota(jnp.int32, (1, CHUNK), 1)
        scale = jnp.where(lane < live, pix[slot, 7:8, pl.ds(start, CHUNK)], 0.0)
        observed = obs[slot, :, pl.ds(start, CHUNK)].astype(jnp.float32)
        weighted = ((model - observed) * scale).astype(jnp.bfloat16)
        for k in range(NEAR):
            grad[places[near[k]]] += jnp.dot(
                weighted,
                green[:, k * PBLK : (k + 1) * PBLK],
                preferred_element_type=jnp.float32,
            )
        screen_grad[screen] += lax.dot_general(
            weighted, hats[...], (((1,), (1,)), ((), ())), preferred_element_type=jnp.float32
        )

    @pl.when(total > 0)
    def _():
        make(0, green_a, hats_a)

        def step(j, _):
            use(2 * j, green_a, hats_a)
            make(2 * j + 1, green_b, hats_b)
            use(2 * j + 1, green_b, hats_b)
            make(2 * j + 2, green_a, hats_a)
            return 0

        lax.fori_loop(0, lax.div(total + 1, 2), step, 0)

    part = grad.shape[0] // len(grad_out)
    stores = [(grad.at[pl.ds(i * part, part)], out) for i, out in enumerate(grad_out)] + [
        (screen_grad.at[pl.ds(i * local_tiles, local_tiles)], out)
        for i, out in enumerate(screen_out)
    ]
    stores = [pltpu.make_async_copy(a, b, sems.at[i]) for i, (a, b) in enumerate(stores)]
    for copy in stores:
        copy.start()
    for copy in stores:
        copy.wait()


def fit(info, cutoffs, places, obs, pix, screens, stress, patches, grad):
    first = grad is None
    layers = len(obs)
    blocks, epochs = stress.shape[0], stress.shape[1]
    span, width = obs[0].shape[0], obs[0].shape[2]
    slots = layers * span
    local_tiles = screens[0].shape[0]
    smem = pl.BlockSpec(memory_space=pltpu.SMEM)
    hbm = pl.BlockSpec(memory_space=pl.ANY)
    extra = () if first else (grad,)
    pieces = 1 if first else 2
    grad_part = jax.ShapeDtypeStruct((blocks // pieces, epochs, PBLK), jnp.float32)
    screen_part = jax.ShapeDtypeStruct(screens[0].shape, jnp.float32)
    out = pl.pallas_call(
        functools.partial(fit_kernel, first, layers, span // PAIR),
        in_specs=[smem] * 3 + [hbm] * (2 * layers + 4 + len(extra)),
        out_specs=[hbm] * (pieces + 2),
        out_shape=[grad_part] * pieces + [screen_part] * 2,
        scratch_shapes=[
            pltpu.VMEM((slots, epochs, width), obs[0].dtype),
            pltpu.VMEM((slots, 8, width), jnp.float32),
            pltpu.VMEM((2 * local_tiles,) + screens[0].shape[1:], screens[0].dtype),
            pltpu.VMEM(stress.shape, stress.dtype),
            pltpu.VMEM(patches.shape, patches.dtype),
            pltpu.VMEM((blocks, epochs, PBLK), jnp.float32),
            pltpu.VMEM((2 * local_tiles,) + screens[0].shape[1:], jnp.float32),
        ]
        + [
            pltpu.VMEM((CHUNK, NEAR * PBLK), jnp.bfloat16),
            pltpu.VMEM((SG * SG, CHUNK), jnp.bfloat16),
        ]
        * 2
        + [
            pltpu.SMEM((slots * (width // CHUNK),), jnp.int32),
            pltpu.SemaphoreType.DMA((5 + 2 * layers,)),
        ],
        compiler_params=pltpu.CompilerParams(vmem_limit_bytes=40 * MIB),
        cost_estimate=pl.CostEstimate(
            flops=slots * 4 * epochs * width * (NEAR + 1) * PBLK,
            bytes_accessed=40 * MIB,
            transcendentals=slots * width * NEAR * PBLK,
        ),
        name="fit",
    )(info, cutoffs, places, *obs, *pix, *screens, stress, patches, *extra)
    return out[:pieces], out[pieces:]


def partner(values, devices, distance):
    return lax.ppermute(values, "tile", [(i, i ^ distance) for i in range(devices)])


def orders(devices):
    stages = devices.bit_length() - 1
    high = list(range(stages - 1, 1, -1))
    return [1] + high, high + [1]


def block_places(devices, here, blocks, local):
    block = jnp.arange(blocks)
    other = (block // local) ^ here
    seat = block % local
    half = local // 2
    spots = []
    for order in orders(devices):
        spot = 0
        for bit in order:
            spot = spot * 2 + ((other >> bit) & 1)
        spots.append(spot)
    chips = devices // 2
    upper = seat // half
    spot = jnp.where(upper == 0, spots[0], spots[1])
    place = (((other & 1) * 2 + upper) * chips + spot) * half + seat % half
    return place.astype(jnp.int32)


def halve(kept, given, devices):
    total = kept + partner(given, devices, 1)
    middle = total.shape[0] // 2
    parts = [total[:middle], total[middle:]]
    both = orders(devices)
    stages = len(both[0])
    for stage in range(stages):
        for side in range(2):
            size = parts[side].shape[0] // 2
            given = parts[side][size:]
            if stages - stage <= NARROW:
                given = given.astype(jnp.bfloat16)
            got = partner(given, devices, 1 << both[side][stage])
            parts[side] = parts[side][:size] + got.astype(jnp.float32)
    return jnp.concatenate(parts, axis=0)


def on_device(
    observations,
    pixel_geometry,
    block_counts,
    block_tiles,
    cutoff_lists,
    patch_geometry,
    stress,
    screens,
):
    devices = lax.axis_size("tile")
    here = lax.axis_index("tile")
    blocks, epochs, width = observations.shape
    local_tiles = screens.shape[0]
    layers = devices // LAYER
    local = stress.shape[1] // PBLK
    each = 2 * blocks // devices

    across = partner(screens, devices, PAIR)
    obs, obs_near, pix = pack(
        observations,
        pixel_geometry,
        block_counts,
        block_tiles,
        jnp.reshape(here, (1,)).astype(jnp.int32),
        devices,
        local_tiles,
    )
    pix = [pix[0]] + [partner(pix[x], devices, x * LAYER) for x in range(1, layers)]
    obs = [obs[0]] + [partner(obs[x], devices, x * LAYER) for x in range(1, layers)]
    obs_near = [obs_near[0]] + [partner(obs_near[x], devices, x * LAYER) for x in range(1, layers)]
    beside, corner = partner(screens, devices, 1), partner(across, devices, 1)

    mine = jnp.swapaxes(stress.reshape(epochs, local, PBLK), 0, 1)
    full = lax.all_gather(mine, "tile", axis=0, tiled=True)
    patch_blocks = full.shape[0]
    east, north, depth, compliance = patch_geometry
    patches = jnp.stack([east, north, depth, depth * depth, compliance * depth * depth])
    patches = jnp.swapaxes(patches.reshape(5, patch_blocks, PBLK), 0, 1)
    patches = jnp.broadcast_to(patches[:, :, None, :], (patch_blocks, 5, 8, PBLK))
    places = block_places(devices, here, patch_blocks, local)
    cutoffs = cutoff_lists.reshape(-1)
    slots = LAYER * each
    info = jnp.stack([p[slots, :2, :slots] for p in pix]).astype(jnp.int32).reshape(-1)

    grad, (far, diagonal) = fit(
        info, cutoffs, places, obs, pix, (across, corner), full, patches, None
    )
    there = (far + partner(diagonal, devices, 1)).astype(jnp.bfloat16)
    back = partner(there, devices, PAIR)
    (kept, given), (own, next_door) = fit(
        info, cutoffs, places, obs_near, pix, (screens, beside), full, patches, grad[0]
    )
    screen_gradient = own + partner(next_door, devices, 1) + back.astype(jnp.float32)
    grad = halve(kept, given, devices)
    return (jnp.swapaxes(grad, 0, 1).reshape(epochs, local * PBLK), screen_gradient)


def solution(mesh):
    return jax.shard_map(
        on_device,
        mesh=mesh,
        in_specs=(
            P(("groups", "tile"), None, None),
            P(("groups", "tile"), None, None),
            P(("groups", "tile")),
            P(("groups", "tile")),
            P(),
            P(),
            P(None, ("groups", "tile")),
            P(("groups", "tile"), None, None),
        ),
        out_specs=(P(None, ("groups", "tile")), P(("groups", "tile"), None, None)),
        check_vma=False,
    )
```

```python
import functools

import jax
import jax.numpy as jnp
from jax import lax
from jax.experimental import pallas as pl
from jax.experimental.pallas import tpu as pltpu
from jax.sharding import PartitionSpec as P

PBLK = 256
NEAR = 3
SG = 16
CHUNK = 128
LAYER = 4
PAIR = 2
NARROW = 3
ROUNDS = (6, 4, 2, 4)
MIB = 1 << 20


def round_sizes(slots):
    return [slots * r // sum(ROUNDS) for r in ROUNDS]


def pack_kernel(local_tiles, layers, slots, here, tiles, counts, obs, pix, *rest):
    sizes = round_sizes(slots)
    total = len(sizes)
    obs_out, pix_out = rest[: total * layers], rest[total * layers : (total + 2) * layers]
    fill, obs_all, pix_all, sems = rest[(total + 2) * layers :]
    my_layer, my_seat = lax.div(here[0], LAYER), lax.rem(here[0], LAYER)
    chunks = pix.shape[2] // CHUNK
    last = sum(sizes[:-1])
    stride = slots + 1

    def clear(i, _):
        fill[i] = 0
        return 0

    lax.fori_loop(0, layers, clear, 0)
    for x in range(layers):
        pix_all[x, last] = jnp.zeros((8, CHUNK), jnp.float32)
    lane = lax.broadcasted_iota(jnp.int32, (8, CHUNK), 1)
    row = lax.broadcasted_iota(jnp.int32, (8, CHUNK), 0)

    def put(b, _):
        tile = tiles[b]
        count = counts[b]
        owner = lax.div(tile, local_tiles)
        x = lax.div(owner, LAYER) ^ my_layer
        seat = lax.rem(owner, LAYER) ^ my_seat
        spot = lax.rem(seat, PAIR) * PAIR + lax.div(seat, PAIR)
        screen = spot * local_tiles + lax.rem(tile, local_tiles)
        for c in range(chunks):

            @pl.when(count > c * CHUNK)
            def _():
                slot = fill[x]
                fill[x] = slot + 1
                live = jnp.minimum(count - c * CHUNK, CHUNK)
                obs_all[x * slots + slot] = obs[b, :, c * CHUNK : (c + 1) * CHUNK]
                pix_all[x, slot + jnp.where(slot >= last, 1, 0)] = pix[
                    b, :, c * CHUNK : (c + 1) * CHUNK
                ]
                entry = jnp.where(row == 0, live, jnp.where(row == 1, tile, screen))
                info = pix_all[x, last]
                pix_all[x, last] = jnp.where(
                    (lane == slot) & (row < 3), entry.astype(jnp.float32), info
                )

        return 0

    lax.fori_loop(0, obs.shape[0], put, 0)
    copies = []
    for x in range(layers):
        copies.append((pix_all.at[x, pl.ds(0, last + 1)], pix_out[x]))
        copies.append((pix_all.at[x, pl.ds(last + 1, slots - last)], pix_out[layers + x]))
        at = 0
        for i, size in enumerate(sizes):
            copies.append((obs_all.at[pl.ds(x * slots + at, size)], obs_out[i * layers + x]))
            at += size
    copies = [pltpu.make_async_copy(a, b, sems.at[i]) for i, (a, b) in enumerate(copies)]
    for copy in copies:
        copy.start()
    for copy in copies:
        copy.wait()


def pack(observations, pixel_geometry, block_counts, block_tiles, here, devices, local_tiles):
    blocks, epochs, width = observations.shape
    layers = devices // LAYER
    slots = LAYER * (2 * blocks // devices) * (width // CHUNK)
    sizes = round_sizes(slots)
    last = sum(sizes[:-1])
    smem = pl.BlockSpec(memory_space=pltpu.SMEM)
    vmem = pl.BlockSpec(memory_space=pltpu.VMEM)
    hbm = pl.BlockSpec(memory_space=pl.ANY)

    def obs_part(size):
        return jax.ShapeDtypeStruct((size, epochs, CHUNK), observations.dtype)

    def pix_part(size):
        return jax.ShapeDtypeStruct((size, 8, CHUNK), jnp.float32)

    out = pl.pallas_call(
        functools.partial(pack_kernel, local_tiles, layers, slots),
        in_specs=[smem, smem, smem, vmem, vmem],
        out_specs=[hbm] * ((len(sizes) + 2) * layers) + [smem],
        out_shape=[obs_part(size) for size in sizes for _ in range(layers)]
        + [pix_part(last + 1)] * layers
        + [pix_part(slots - last)] * layers
        + [jax.ShapeDtypeStruct((layers,), jnp.int32)],
        scratch_shapes=[
            pltpu.VMEM((layers * slots, epochs, CHUNK), observations.dtype),
            pltpu.VMEM((layers, slots + 1, 8, CHUNK), jnp.float32),
            pltpu.SemaphoreType.DMA(((len(sizes) + 2) * layers,)),
        ],
        compiler_params=pltpu.CompilerParams(vmem_limit_bytes=16 * MIB),
        name="pack",
    )(here, block_tiles, block_counts, observations, pixel_geometry)
    rounds = len(sizes)
    obs = [out[i * layers : (i + 1) * layers] for i in range(rounds)]
    pix, pix_last = (out[(rounds + i) * layers : (rounds + i + 1) * layers] for i in range(2))
    return obs, pix, pix_last, out[-1]


def fit_kernel(first, final, layers, slots, groups, *refs):
    info, cutoffs, places, spots = refs[:4]
    rest = refs[4:]
    obs_in, pix_in = [], []
    for _ in groups:
        obs_in.append(rest[:layers])
        pix_in.append(rest[layers : 2 * layers])
        rest = rest[2 * layers :]
    screens, stress, patches = rest[:3]
    rest = rest[3:]
    rest = rest if first else rest[2:]
    grad, screen_grad = rest[:2]
    outs = rest[2:5] if final else ()
    rest = rest[2 + len(outs) :]
    obs, pix, green_a, hats_a, green_b, hats_b, items, sems = rest
    base = groups[0][0]
    span = sum(size for _, _, size in groups)
    local_tiles = screens.shape[0] // LAYER

    loads = []
    for x in range(layers):
        at = x * span
        for g, (_, low, size) in enumerate(groups):
            loads.append((obs_in[g][x], obs.at[pl.ds(at, size)]))
            loads.append((pix_in[g][x].at[pl.ds(low, size)], pix.at[pl.ds(at, size)]))
            at += size
    loads = [pltpu.make_async_copy(a, b, sems.at[i]) for i, (a, b) in enumerate(loads)]
    for copy in loads:
        copy.start()
    if first:
        screen_grad[...] = jnp.zeros_like(screen_grad)
        grad[...] = jnp.zeros_like(grad)

    def info_of(slot, kind):
        x = lax.div(slot, span)
        return info[(x * 3 + kind) * slots + base + lax.rem(slot, span)]

    def list_slot(slot, total):
        items[total] = slot
        return total + jnp.where(info_of(slot, 0) > 0, 1, 0)

    total = lax.fori_loop(0, layers * span, list_slot, 0)
    for copy in loads:
        copy.wait()

    def item_of(i):
        slot = items[jnp.minimum(i, total - 1)]
        tile = info_of(slot, 1)
        return slot, [cutoffs[tile * NEAR + k] for k in range(NEAR)]

    def make_strips(columns, near, lows, green):
        for low in lows:
            strips = [[] for _ in range(NEAR)]
            for at in (low, low + 8):
                east, north, le, ln, lu = (
                    jnp.broadcast_to(columns[at : at + 8, c : c + 1], (8, PBLK))
                    for c in (0, 1, 4, 5, 6)
                )
                for k in range(NEAR):
                    patch = patches.at[near[k]]
                    dx = east - patch[0]
                    dy = north - patch[1]
                    inverse = lax.rsqrt(dx * dx + dy * dy + patch[3])
                    along = le * dx + ln * dy + lu * patch[2]
                    strips[k].append(patch[4] * along * inverse * inverse * inverse)
            for k in range(NEAR):
                green[low : low + 16, k * PBLK : (k + 1) * PBLK] = jnp.concatenate(
                    strips[k], axis=0
                ).astype(jnp.bfloat16)

    def make_hats(rows, hats):
        node = lax.broadcasted_iota(jnp.int32, (SG, CHUNK), 0).astype(jnp.float32)
        across = jnp.maximum(0.0, 1.0 - jnp.abs(rows[2:3] - node))
        upward = jnp.maximum(0.0, 1.0 - jnp.abs(rows[3:4] - node))
        for a in range(SG):
            hats[a * SG : (a + 1) * SG] = (across[a : a + 1] * upward).astype(jnp.bfloat16)

    def make_all(i, green, hats):
        slot, near = item_of(i)
        rows = pix[slot]
        make_hats(rows, hats)
        make_strips(rows.T, near, range(0, CHUNK, 16), green)

    def turn(i, green, hats, green_next, hats_next):
        slot, near = item_of(i)
        slot_next, near_next = item_of(i + 1)
        rows = pix[slot_next]
        columns = rows.T
        screen = info_of(slot, 2)

        def fill(lows):
            make_strips(columns, near_next, lows, green_next)

        model = jnp.dot(screens[screen], hats[...], preferred_element_type=jnp.float32)
        for k in range(NEAR):
            model += lax.dot_general(
                stress[spots[near[k]]],
                green[:, k * PBLK : (k + 1) * PBLK],
                (((1,), (1,)), ((), ())),
                preferred_element_type=jnp.float32,
            )
        make_hats(rows, hats_next)
        fill(range(0, 64, 16))
        live = jnp.where(i < total, info_of(slot, 0), 0)
        lane = lax.broadcasted_iota(jnp.int32, (1, CHUNK), 1)
        scale = jnp.where(lane < live, pix[slot, 7:8, :], 0.0)
        weighted = ((model - obs[slot].astype(jnp.float32)) * scale).astype(jnp.bfloat16)

        def add(k):
            grad[places[near[k]]] += jnp.dot(
                weighted,
                green[:, k * PBLK : (k + 1) * PBLK],
                preferred_element_type=jnp.float32,
            )

        add(0)
        fill(range(64, 80, 16))
        add(1)
        fill(range(80, 96, 16))
        add(2)
        fill(range(96, 112, 16))
        screen_grad[screen] += lax.dot_general(
            weighted, hats[...], (((1,), (1,)), ((), ())), preferred_element_type=jnp.float32
        )
        fill(range(112, 128, 16))

    @pl.when(total > 0)
    def _():
        make_all(0, green_a, hats_a)

        def step(j, _):
            turn(2 * j, green_a, hats_a, green_b, hats_b)
            turn(2 * j + 1, green_b, hats_b, green_a, hats_a)
            return 0

        lax.fori_loop(0, lax.div(total + 1, 2), step, 0)

    if final:
        half = grad.shape[0] // 2
        outs[0][...] = grad[half:].astype(outs[0].dtype)
        for i, out in enumerate(outs[1:]):
            low = (PAIR + i) * local_tiles
            out[...] = screen_grad[low : low + local_tiles].astype(out.dtype)


def fit(info, cutoffs, places, spots, groups, screens, stress, patches, state, final):
    first = state is None
    layers = len(groups[0][1])
    blocks, epochs = stress.shape[0], stress.shape[1]
    slots = info.shape[0] // (3 * layers)
    local_tiles = screens.shape[0] // LAYER
    smem = pl.BlockSpec(memory_space=pltpu.SMEM)
    vmem = pl.BlockSpec(memory_space=pltpu.VMEM)
    hbm = pl.BlockSpec(memory_space=pl.ANY)
    extra = () if first else state
    spans = tuple((base, low, obs[0].shape[0]) for base, obs, _, low in groups)
    arrays = [a for _, obs, pix, _ in groups for a in (*obs, *pix)]
    span = sum(size for _, _, size in spans)
    out_shape = [
        jax.ShapeDtypeStruct((blocks, epochs, PBLK), jnp.float32),
        jax.ShapeDtypeStruct(screens.shape, jnp.float32),
    ]
    if final:
        out_shape.append(jax.ShapeDtypeStruct((blocks // 2, epochs, PBLK), jnp.bfloat16))
        shape = (local_tiles,) + screens.shape[1:]
        out_shape += [jax.ShapeDtypeStruct(shape, jnp.bfloat16)] * 2
    before = 4 + len(arrays) + 3
    return pl.pallas_call(
        functools.partial(fit_kernel, first, final, layers, slots, spans),
        in_specs=[smem] * 4 + [hbm] * len(arrays) + [vmem] * (3 + len(extra)),
        out_specs=[vmem] * len(out_shape),
        out_shape=out_shape,
        scratch_shapes=[
            pltpu.VMEM((layers * span, epochs, CHUNK), arrays[0].dtype),
            pltpu.VMEM((layers * span, 8, CHUNK), jnp.float32),
        ]
        + [
            pltpu.VMEM((CHUNK, NEAR * PBLK), jnp.bfloat16),
            pltpu.VMEM((SG * SG, CHUNK), jnp.bfloat16),
        ]
        * 2
        + [
            pltpu.SMEM((layers * span + 1,), jnp.int32),
            pltpu.SemaphoreType.DMA((2 * layers * len(groups),)),
        ],
        input_output_aliases={} if first else {before: 0, before + 1: 1},
        compiler_params=pltpu.CompilerParams(vmem_limit_bytes=12 * MIB),
        cost_estimate=pl.CostEstimate(
            flops=layers * span * 4 * epochs * CHUNK * (NEAR + 1) * PBLK,
            bytes_accessed=20 * MIB,
            transcendentals=layers * span * CHUNK * NEAR * PBLK,
        ),
        name="fit",
    )(info, cutoffs, places, spots, *arrays, screens, stress, patches, *extra)


def partner(values, devices, distance):
    return lax.ppermute(values, "tile", [(i, i ^ distance) for i in range(devices)])


def orders(devices):
    stages = devices.bit_length() - 1
    high = list(range(stages - 1, 1, -1))
    return [1] + high, high + [1]


def block_places(devices, here, blocks, local):
    block = jnp.arange(blocks)
    other = (block // local) ^ here
    seat = block % local
    half = local // 2
    turned = []
    for order in orders(devices):
        spot = 0
        for bit in order:
            spot = spot * 2 + ((other >> bit) & 1)
        turned.append(spot)
    chips = devices // 2
    upper = seat // half
    spot = jnp.where(upper == 0, turned[0], turned[1])
    place = (((other & 1) * 2 + upper) * chips + spot) * half + seat % half
    stages = devices.bit_length() - 1
    held = sum(((other >> (stages - 1 - s)) & 1) << s for s in range(stages))
    return place.astype(jnp.int32), (held * local + seat).astype(jnp.int32)


def halve(kept, given, devices):
    total = kept + partner(given, devices, 1).astype(jnp.float32)
    middle = total.shape[0] // 2
    parts = [total[:middle], total[middle:]]
    both = orders(devices)
    stages = len(both[0])
    for stage in range(stages):
        for side in range(2):
            size = parts[side].shape[0] // 2
            given = parts[side][size:]
            if stages - stage <= NARROW:
                given = given.astype(jnp.bfloat16)
            got = partner(given, devices, 1 << both[side][stage])
            parts[side] = parts[side][:size] + got.astype(jnp.float32)
    return jnp.concatenate(parts, axis=0)


def on_device(
    observations,
    pixel_geometry,
    block_counts,
    block_tiles,
    cutoff_lists,
    patch_geometry,
    stress,
    screens,
):
    devices = lax.axis_size("tile")
    here = lax.axis_index("tile")
    blocks, epochs, width = observations.shape
    local_tiles = screens.shape[0]
    layers = devices // LAYER
    local = stress.shape[1] // PBLK

    full = jnp.swapaxes(stress.reshape(epochs, local, PBLK), 0, 1)
    distance = devices // 2
    while distance:
        full = jnp.concatenate([full, partner(full, devices, distance)], axis=0)
        distance //= 2
    near_screens = jnp.concatenate([screens, partner(screens, devices, PAIR)], axis=0)
    all_screens = jnp.concatenate([near_screens, partner(near_screens, devices, 1)], axis=0)

    obs, pix, pix_last, fill = pack(
        observations,
        pixel_geometry,
        block_counts,
        block_tiles,
        jnp.reshape(here, (1,)).astype(jnp.int32),
        devices,
        local_tiles,
    )
    rounds = len(obs)
    sizes = [o[0].shape[0] for o in obs]
    early = sum(sizes[:-1])
    slots = early + sizes[-1]
    most = lax.pmax(jnp.max(fill[1:]), ("groups", "tile"))

    def exchange(parts):
        return [parts[0]] + [partner(parts[x], devices, x * LAYER) for x in range(1, layers)]

    pix = exchange(pix)
    got = [exchange(o) for o in obs[:-1]]
    late_obs, late_pix = lax.cond(
        most > early,
        lambda o, p: (exchange(o), exchange(p)),
        lambda o, p: (list(o), list(p)),
        list(obs[-1]),
        list(pix_last),
    )

    east, north, depth, compliance = patch_geometry
    patches = jnp.stack([east, north, depth, depth * depth, compliance * depth * depth])
    patch_blocks = full.shape[0]
    patches = jnp.swapaxes(patches.reshape(5, patch_blocks, PBLK), 0, 1)
    patches = jnp.broadcast_to(patches[:, :, None, :], (patch_blocks, 5, 8, PBLK))
    places, spots = block_places(devices, here, patch_blocks, local)
    cutoffs = cutoff_lists.reshape(-1)
    info = jnp.stack([p[early, :3, :slots] for p in pix]).astype(jnp.int32).reshape(-1)

    state, base = None, 0
    for i in range(rounds - 1):
        groups = [(base, got[i], pix, base)]
        final = i == rounds - 2
        if final:
            groups.append((early, late_obs, late_pix, 0))
        state = fit(
            info, cutoffs, places, spots, groups, all_screens, full, patches, state, final
        )
        base += sizes[i]
    grad, screen_grad, given, next_door, diagonal = state
    own, far = screen_grad[:local_tiles], screen_grad[local_tiles : PAIR * local_tiles]
    there = (far + partner(diagonal, devices, 1).astype(jnp.float32)).astype(jnp.bfloat16)
    back = partner(there, devices, PAIR)
    grad = halve(grad[: grad.shape[0] // 2], given, devices)
    screen_gradient = (
        own + partner(next_door, devices, 1).astype(jnp.float32) + back.astype(jnp.float32)
    )
    return (jnp.swapaxes(grad, 0, 1).reshape(epochs, local * PBLK), screen_gradient)


def solution(mesh):
    return jax.shard_map(
        on_device,
        mesh=mesh,
        in_specs=(
            P(("groups", "tile"), None, None),
            P(("groups", "tile"), None, None),
            P(("groups", "tile")),
            P(("groups", "tile")),
            P(),
            P(),
            P(None, ("groups", "tile")),
            P(("groups", "tile"), None, None),
        ),
        out_specs=(P(None, ("groups", "tile")), P(("groups", "tile"), None, None)),
        check_vma=False,
    )
```

```python
import functools

import jax
import jax.numpy as jnp
from jax import lax
from jax.experimental import pallas as pl
from jax.experimental.pallas import tpu as pltpu
from jax.sharding import PartitionSpec as P

PBLK = 256
NEAR = 3
SG = 16
CHUNK = 128
LAYER = 4
PAIR = 2
NARROW = 3
ROUNDS = (6, 4, 2, 4)
MIB = 1 << 20
LARGE = 3e38
COLUMNS = (0, 1, 4, 5, 6)
NOTE = 16


def round_sizes(slots):
    return [slots * r // sum(ROUNDS) for r in ROUNDS]


def pack_kernel(local_tiles, layers, slots, here, tiles, counts, obs_in, pix_in, *rest):
    sizes = round_sizes(slots)
    total = len(sizes)
    obs_out, pix_out = rest[: total * layers], rest[total * layers : (total + 2) * layers]
    obs, pix, obs_all, pix_all, fill, sems = rest[(total + 2) * layers :]
    loads = [
        pltpu.make_async_copy(obs_in, obs, sems.at[0]),
        pltpu.make_async_copy(pix_in, pix, sems.at[1]),
    ]
    for copy in loads:
        copy.start()
    my_layer, my_seat = lax.div(here[0], LAYER), lax.rem(here[0], LAYER)
    chunks = pix.shape[2] // CHUNK
    last = sum(sizes[:-1])
    stride = slots + 1
    for x in range(layers):
        fill[x] = 0
    lane = lax.broadcasted_iota(jnp.int32, (8, CHUNK), 1)
    row = lax.broadcasted_iota(jnp.int32, (8, CHUNK), 0)
    for copy in loads:
        copy.wait()

    def put(b, infos):
        tile = tiles[b]
        count = counts[b]
        owner = lax.div(tile, local_tiles)
        x = lax.div(owner, LAYER) ^ my_layer
        seat = lax.rem(owner, LAYER) ^ my_seat
        spot = lax.rem(seat, PAIR) * PAIR + lax.div(seat, PAIR)
        screen = spot * local_tiles + lax.rem(tile, local_tiles)
        slot = fill[x]
        fill[x] = slot + lax.div(count + CHUNK - 1, CHUNK)
        for c in range(chunks):
            at = slot + c
            live = jnp.clip(count - c * CHUNK, 0, CHUNK)
            obs_all[x * stride + at] = obs[b, :, c * CHUNK : (c + 1) * CHUNK]
            pix_all[x * (stride + 1) + at + jnp.where(at >= last, 1, 0)] = pix[
                b, :, c * CHUNK : (c + 1) * CHUNK
            ]
            entry = jnp.where(row == 0, live, jnp.where(row == 1, tile, screen))
            here_only = (lane == at) & (row < 3)
            infos = tuple(
                jnp.where(here_only & (x == i), entry, info) for i, info in enumerate(infos)
            )
        return infos

    infos = lax.fori_loop(
        0, obs.shape[0], put, tuple(jnp.zeros((8, CHUNK), jnp.int32) for _ in range(layers))
    )
    copies = []
    for x in range(layers):
        low = x * (stride + 1)
        pix_all[low + last] = infos[x].astype(jnp.float32)
        copies.append((pix_all.at[pl.ds(low, last + 1)], pix_out[x]))
        copies.append((pix_all.at[pl.ds(low + last + 1, slots - last)], pix_out[layers + x]))
        at = x * stride
        for i, size in enumerate(sizes):
            copies.append((obs_all.at[pl.ds(at, size)], obs_out[i * layers + x]))
            at += size
    copies = [pltpu.make_async_copy(a, b, sems.at[i]) for i, (a, b) in enumerate(copies)]
    for copy in copies:
        copy.start()
    for copy in copies:
        copy.wait()


def pack(observations, pixel_geometry, block_counts, block_tiles, here, devices, local_tiles):
    blocks, epochs, width = observations.shape
    layers = devices // LAYER
    slots = LAYER * (2 * blocks // devices) * (width // CHUNK)
    sizes = round_sizes(slots)
    last = sum(sizes[:-1])
    smem = pl.BlockSpec(memory_space=pltpu.SMEM)
    hbm = pl.BlockSpec(memory_space=pl.ANY)

    def obs_part(size):
        return jax.ShapeDtypeStruct((size, epochs, CHUNK), observations.dtype)

    def pix_part(size):
        return jax.ShapeDtypeStruct((size, 8, CHUNK), jnp.float32)

    out = pl.pallas_call(
        functools.partial(pack_kernel, local_tiles, layers, slots),
        in_specs=[smem, smem, smem, hbm, hbm],
        out_specs=[hbm] * ((len(sizes) + 2) * layers),
        out_shape=[obs_part(size) for size in sizes for _ in range(layers)]
        + [pix_part(last + 1)] * layers
        + [pix_part(slots - last)] * layers,
        scratch_shapes=[
            pltpu.VMEM(observations.shape, observations.dtype),
            pltpu.VMEM(pixel_geometry.shape, jnp.float32),
            pltpu.VMEM((layers * (slots + 1), epochs, CHUNK), observations.dtype),
            pltpu.VMEM((layers * (slots + 2), 8, CHUNK), jnp.float32),
            pltpu.SMEM((layers,), jnp.int32),
            pltpu.SemaphoreType.DMA(((len(sizes) + 2) * layers,)),
        ],
        compiler_params=pltpu.CompilerParams(vmem_limit_bytes=10 * MIB),
        name="pack",
    )(here, block_tiles, block_counts, observations, pixel_geometry)
    rounds = len(sizes)
    obs = [out[i * layers : (i + 1) * layers] for i in range(rounds)]
    pix, pix_last = (out[(rounds + i) * layers : (rounds + i + 1) * layers] for i in range(2))
    return obs, pix, pix_last


def fit_kernel(first, final, layers, slots, groups, *refs):
    info, cutoffs, places, spots = refs[:4]
    rest = refs[4:]
    obs_in, pix_in = [], []
    for _ in groups:
        obs_in.append(rest[:layers])
        pix_in.append(rest[layers : 2 * layers])
        rest = rest[2 * layers :]
    patches = rest[0]
    if first:
        screen_parts, stress_parts = rest[1 : 1 + LAYER], rest[1 + LAYER : 1 + 2 * LAYER]
        rest = rest[1 + 2 * LAYER :]
        grad, screen_grad, screens, stress = rest[:4]
        rest = rest[4:]
    else:
        screens, stress = rest[1:3]
        grad, screen_grad = rest[5:7]
        rest = rest[7:]
    outs = rest[:3] if final else ()
    rest = rest[len(outs) :]
    obs, pix, green_a, hats_a, green_b, hats_b, wide, items, sems = rest
    epochs = obs.shape[1]
    base = groups[0][0]
    span = sum(size for _, _, size in groups)
    local_tiles = screens.shape[0] // LAYER

    loads = []
    for x in range(layers):
        at = x * span
        for g, (_, low, size) in enumerate(groups):
            loads.append((obs_in[g][x], obs.at[pl.ds(at, size)]))
            loads.append((pix_in[g][x].at[pl.ds(low, size)], pix.at[pl.ds(at, size)]))
            at += size
    if first:
        for parts, whole in ((screen_parts, screens), (stress_parts, stress)):
            size = whole.shape[0] // LAYER
            for i, part in enumerate(parts):
                loads.append((part, whole.at[pl.ds(i * size, size)]))
    loads = [pltpu.make_async_copy(a, b, sems.at[i]) for i, (a, b) in enumerate(loads)]
    for copy in loads:
        copy.start()
    if first:
        grad[...] = jnp.zeros_like(grad)
        screen_grad[...] = jnp.zeros_like(screen_grad)

    def info_of(slot, kind):
        x = lax.div(slot, span)
        return info[(x * 3 + kind) * slots + base + lax.rem(slot, span)]

    def list_slot(slot, total):
        items[total] = slot
        return total + jnp.where(info_of(slot, 0) > 0, 1, 0)

    total = lax.fori_loop(0, layers * span, list_slot, 0)
    for copy in loads:
        copy.wait()

    def item_of(i):
        slot = items[jnp.minimum(i, total - 1)]
        tile = info_of(slot, 1)
        return slot, [cutoffs[tile * NEAR + k] for k in range(NEAR)]

    def spread(columns):
        for i, c in enumerate(COLUMNS):
            wide[i] = jnp.broadcast_to(columns[:, c : c + 1], (CHUNK, CHUNK))

    def make_strips(near, k, lows, green):
        patch = [
            jnp.broadcast_to(patches[near[k], r : r + 1], (8, PBLK)) for r in range(5)
        ]
        for low in lows:
            radii, alongs = [], []
            for at in (low, low + 8):
                east, north, le, ln, lu = (
                    jnp.concatenate([wide[i, at : at + 8]] * (PBLK // CHUNK), axis=1)
                    for i in range(len(COLUMNS))
                )
                dx = east - patch[0]
                dy = north - patch[1]
                radii.append(jnp.minimum(dx * dx + dy * dy + patch[3], LARGE))
                alongs.append(patch[4] * (le * dx + ln * dy + lu * patch[2]))
            radius, along = jnp.concatenate(radii, axis=0), jnp.concatenate(alongs, axis=0)
            rough = lax.rsqrt(radius.astype(jnp.bfloat16)).astype(jnp.float32)
            square = rough * rough
            mend = 2.5 - 1.5 * (radius * square)
            green[low : low + 16, k * PBLK : (k + 1) * PBLK] = (
                along * rough * square * mend
            ).astype(jnp.bfloat16)

    def make_hats(rows, hats):
        node = lax.broadcasted_iota(jnp.int32, (SG, CHUNK), 0).astype(jnp.float32)
        across = jnp.maximum(0.0, 1.0 - jnp.abs(rows[2:3] - node))
        upward = jnp.maximum(0.0, 1.0 - jnp.abs(rows[3:4] - node))
        for a in range(SG):
            hats[a * SG : (a + 1) * SG] = (across[a : a + 1] * upward).astype(jnp.bfloat16)

    def make_all(i, green, hats):
        slot, near = item_of(i)
        rows = pix[slot]
        make_hats(rows, hats)
        spread(rows.T)
        for k in range(NEAR):
            make_strips(near, k, range(0, CHUNK, 16), green)

    def turn(i, green, hats, green_next, hats_next):
        slot, near = item_of(i)
        slot_next, near_next = item_of(i + 1)
        rows = pix[slot_next]
        screen = info_of(slot, 2)

        def fill(k, low, high):
            make_strips(near_next, k, range(low, high, 16), green_next)

        model = jnp.dot(screens[screen], hats[...], preferred_element_type=jnp.float32)
        for k in range(NEAR):
            model += lax.dot_general(
                stress[pl.ds(pl.multiple_of(spots[near[k]], 16), epochs), :],
                green[:, k * PBLK : (k + 1) * PBLK],
                (((1,), (1,)), ((), ())),
                preferred_element_type=jnp.float32,
            )
        make_hats(rows, hats_next)
        spread(rows.T)
        fill(0, 0, CHUNK)
        live = jnp.where(i < total, info_of(slot, 0), 0)
        lane = lax.broadcasted_iota(jnp.int32, (1, CHUNK), 1)
        scale = jnp.where(lane < live, pix[slot, 7:8, :], 0.0)
        weighted = ((model - obs[slot].astype(jnp.float32)) * scale).astype(jnp.bfloat16)

        def add(k):
            grad[places[near[k]]] += jnp.dot(
                weighted,
                green[:, k * PBLK : (k + 1) * PBLK],
                preferred_element_type=jnp.float32,
            )

        add(0)
        fill(1, 0, CHUNK // 2)
        add(1)
        fill(1, CHUNK // 2, CHUNK)
        add(2)
        fill(2, 0, CHUNK // 2)
        screen_grad[screen] += lax.dot_general(
            weighted, hats[...], (((1,), (1,)), ((), ())), preferred_element_type=jnp.float32
        )
        fill(2, CHUNK // 2, CHUNK)

    @pl.when(total > 0)
    def _():
        make_all(0, green_a, hats_a)

        def step(j, _):
            turn(2 * j, green_a, hats_a, green_b, hats_b)
            turn(2 * j + 1, green_b, hats_b, green_a, hats_a)
            return 0

        lax.fori_loop(0, lax.div(total + 1, 2), step, 0)

    if final:
        half = grad.shape[0] // 2
        outs[0][...] = grad[half:].astype(outs[0].dtype)
        for i, out in enumerate(outs[1:]):
            low = (PAIR + i) * local_tiles
            out[...] = screen_grad[low : low + local_tiles].astype(out.dtype)


def fit(info, cutoffs, places, spots, groups, patches, screens, stress, state, first, final):
    layers = len(groups[0][1])
    slots = info.shape[0] // (3 * layers)
    smem = pl.BlockSpec(memory_space=pltpu.SMEM)
    vmem = pl.BlockSpec(memory_space=pltpu.VMEM)
    hbm = pl.BlockSpec(memory_space=pl.ANY)
    spans = tuple((base, low, obs[0].shape[0]) for base, obs, _, low in groups)
    arrays = [a for _, obs, pix, _ in groups for a in (*obs, *pix)]
    span = sum(size for _, _, size in spans)
    blocks, epochs = state[0].shape[0], state[0].shape[1]
    out_shape = [jax.ShapeDtypeStruct(a.shape, a.dtype) for a in state]
    if first:
        state = ()
        for parts in (screens, stress):
            shape = (LAYER * parts[0].shape[0],) + parts[0].shape[1:]
            out_shape.append(jax.ShapeDtypeStruct(shape, parts[0].dtype))
    else:
        screens, stress = [screens], [stress]
    if final:
        out_shape.append(jax.ShapeDtypeStruct((blocks // 2, epochs, PBLK), jnp.bfloat16))
        shape = (state[1].shape[0] // LAYER,) + state[1].shape[1:]
        out_shape += [jax.ShapeDtypeStruct(shape, jnp.bfloat16)] * 2
    before = 4 + len(arrays) + 1 + len(screens) + len(stress)
    return pl.pallas_call(
        functools.partial(fit_kernel, first, final, layers, slots, spans),
        in_specs=[smem] * 4
        + [hbm] * len(arrays)
        + [vmem]
        + [hbm if first else vmem] * (len(screens) + len(stress))
        + [vmem] * len(state),
        out_specs=[vmem] * len(out_shape),
        out_shape=out_shape,
        scratch_shapes=[
            pltpu.VMEM((layers * span, epochs, CHUNK), arrays[0].dtype),
            pltpu.VMEM((layers * span, 8, CHUNK), jnp.float32),
        ]
        + [
            pltpu.VMEM((CHUNK, NEAR * PBLK), jnp.bfloat16),
            pltpu.VMEM((SG * SG, CHUNK), jnp.bfloat16),
        ]
        * 2
        + [
            pltpu.VMEM((len(COLUMNS), CHUNK, CHUNK), jnp.float32),
            pltpu.SMEM((layers * span + 1,), jnp.int32),
            pltpu.SemaphoreType.DMA((2 * layers * len(groups) + 2 * LAYER,)),
        ],
        input_output_aliases={} if first else {before: 0, before + 1: 1},
        compiler_params=pltpu.CompilerParams(vmem_limit_bytes=8 * MIB),
        cost_estimate=pl.CostEstimate(
            flops=layers * span * 4 * epochs * CHUNK * (NEAR + 1) * PBLK,
            bytes_accessed=20 * MIB,
            transcendentals=layers * span * CHUNK * NEAR * PBLK,
        ),
        name="fit",
    )(info, cutoffs, places, spots, *arrays, patches, *screens, *stress, *state)


def partner(values, devices, distance):
    return lax.ppermute(values, "tile", [(i, i ^ distance) for i in range(devices)])


def orders(devices):
    stages = devices.bit_length() - 1
    high = list(range(stages - 1, 1, -1))
    return [1] + high, high + [1]


def block_places(devices, here, blocks, local, epochs):
    block = jnp.arange(blocks)
    other = (block // local) ^ here
    seat = block % local
    half = local // 2
    turned = []
    for order in orders(devices):
        spot = 0
        for bit in order:
            spot = spot * 2 + ((other >> bit) & 1)
        turned.append(spot)
    chips = devices // 2
    upper = seat // half
    spot = jnp.where(upper == 0, turned[0], turned[1])
    place = (((other & 1) * 2 + upper) * chips + spot) * half + seat % half
    stages = devices.bit_length() - 1
    held = sum(((other >> (stages - 1 - s)) & 1) << s for s in range(stages))
    return place.astype(jnp.int32), (held * (local * epochs + NOTE) + seat * epochs).astype(jnp.int32)


def halve(kept, given, there, devices):
    total = kept + partner(given, devices, 1).astype(jnp.float32)
    middle = total.shape[0] // 2
    parts = [total[:middle], total[middle:]]
    both = orders(devices)
    stages = len(both[0])
    for stage in range(stages):
        for side in range(2):
            size = parts[side].shape[0] // 2
            given = parts[side][size:]
            if stages - stage <= NARROW:
                given = given.astype(jnp.bfloat16)
            got = partner(given, devices, 1 << both[side][stage])
            if stage == 0 and side == 0:
                got, there = lax.optimization_barrier((got, there))
                back = partner(there, devices, PAIR)
            parts[side] = parts[side][:size] + got.astype(jnp.float32)
    return jnp.concatenate(parts, axis=0), back


def on_device(
    observations,
    pixel_geometry,
    block_counts,
    block_tiles,
    cutoff_lists,
    patch_geometry,
    stress,
    screens,
):
    devices = lax.axis_size("tile")
    here = lax.axis_index("tile")
    blocks, epochs, width = observations.shape
    local_tiles = screens.shape[0]
    layers = devices // LAYER
    local = stress.shape[1] // PBLK

    slots = LAYER * (2 * blocks // devices) * (width // CHUNK)
    sizes = round_sizes(slots)
    early = sum(sizes[:-1])

    layer_of = block_tiles // (local_tiles * LAYER)
    chunks = (block_counts + CHUNK - 1) // CHUNK
    sent = jnp.where(
        layer_of[None, :] == jnp.arange(layers)[:, None], chunks[None, :], 0
    ).sum(axis=1)
    most = jnp.max(jnp.where(jnp.arange(layers) == here // LAYER, 0, sent))
    note = jnp.full((NOTE, PBLK), most.astype(jnp.bfloat16))
    mine = jnp.swapaxes(stress.reshape(epochs, local, PBLK), 0, 1).reshape(-1, PBLK)
    held = jnp.concatenate([mine, note], axis=0)
    obs, pix, pix_last = pack(
        observations,
        pixel_geometry,
        block_counts,
        block_tiles,
        jnp.reshape(here, (1,)).astype(jnp.int32),
        devices,
        local_tiles,
    )

    distance = devices // 2
    while distance >= LAYER:
        other = partner(held, devices, distance)
        if distance == devices // 2:
            other, pix = lax.optimization_barrier((other, pix))
        held = jnp.concatenate([held, other], axis=0)
        distance //= 2
    across_screens = partner(screens, devices, PAIR)
    beside_screens = partner(screens, devices, 1)
    across = partner(held, devices, PAIR)
    all_stress = [held, across, partner(held, devices, 1), partner(across, devices, 1)]
    all_screens = [
        screens,
        across_screens,
        beside_screens,
        partner(across_screens, devices, 1),
    ]

    def exchange(parts):
        return [parts[0]] + [partner(parts[x], devices, x * LAYER) for x in range(1, layers)]

    pix = exchange(pix)
    got = [exchange(o) for o in obs[:-1]]
    rows = local * epochs
    notes = jnp.stack([part[rows :: rows + NOTE, 0] for part in all_stress])
    most = jnp.max(notes.astype(jnp.float32)).reshape(1)
    teams = lax.axis_size("groups")
    team_distance = 1
    while team_distance < teams:
        pairs = [(i, i ^ team_distance) for i in range(teams)]
        most = jnp.maximum(most, lax.ppermute(most, "groups", pairs))
        team_distance *= 2
    most, got[-1] = lax.optimization_barrier((most, got[-1]))
    late_obs, late_pix = lax.cond(
        most[0] > early,
        lambda o, p: (exchange(o), exchange(p)),
        lambda o, p: (list(o), list(p)),
        list(obs[-1]),
        list(pix_last),
    )

    east, north, depth, compliance = patch_geometry
    patches = jnp.stack([east, north, depth, depth * depth, compliance * depth * depth])
    patch_blocks = devices * local
    patches = jnp.swapaxes(patches.reshape(5, patch_blocks, PBLK), 0, 1)
    places, spots = block_places(devices, here, patch_blocks, local, epochs)
    cutoffs = cutoff_lists.reshape(-1)
    info = jnp.stack([p[early, :3, :slots] for p in pix]).astype(jnp.int32).reshape(-1)

    state = (
        jax.ShapeDtypeStruct((patch_blocks, epochs, PBLK), jnp.float32),
        jax.ShapeDtypeStruct((LAYER * local_tiles,) + screens.shape[1:], jnp.float32),
    )
    base = 0
    for i in range(len(sizes) - 1):
        groups = [(base, got[i], pix, base)]
        first, final = i == 0, i == len(sizes) - 2
        if final:
            groups.append((early, late_obs, late_pix, 0))
        state = fit(
            info,
            cutoffs,
            places,
            spots,
            groups,
            patches,
            all_screens,
            all_stress,
            state[:2],
            first,
            final,
        )
        if first:
            all_screens, all_stress = state[2:]
        base += sizes[i]
    grad, screen_grad, given, next_door, diagonal = state
    own, far = screen_grad[:local_tiles], screen_grad[local_tiles : PAIR * local_tiles]
    there = (far + partner(diagonal, devices, 1).astype(jnp.float32)).astype(jnp.bfloat16)
    grad, back = halve(grad[: grad.shape[0] // 2], given, there, devices)
    screen_gradient = (
        own + partner(next_door, devices, 1).astype(jnp.float32) + back.astype(jnp.float32)
    )
    return (jnp.swapaxes(grad, 0, 1).reshape(epochs, local * PBLK), screen_gradient)


def solution(mesh):
    return jax.shard_map(
        on_device,
        mesh=mesh,
        in_specs=(
            P(("groups", "tile"), None, None),
            P(("groups", "tile"), None, None),
            P(("groups", "tile")),
            P(("groups", "tile")),
            P(),
            P(),
            P(None, ("groups", "tile")),
            P(("groups", "tile"), None, None),
        ),
        out_specs=(P(None, ("groups", "tile")), P(("groups", "tile"), None, None)),
        check_vma=False,
    )
```

```python
import functools

import jax
import jax.numpy as jnp
from jax import lax
from jax.experimental import pallas as pl
from jax.experimental.pallas import tpu as pltpu
from jax.sharding import PartitionSpec as P

PBLK = 256
NEAR = 3
SG = 16
CHUNK = 128
LAYER = 4
PAIR = 2
NARROW = 3
ROUNDS = (6, 6, 4)
MIB = 1 << 20
TERMS = 32
CROSS = ((0, 0), (0, 1), (1, 0), (0, 2), (1, 1), (2, 0))


def round_sizes(slots):
    return [slots * r // sum(ROUNDS) for r in ROUNDS]


def pack_kernel(local_tiles, layers, slots, here, tiles, counts, obs_in, pix_in, *rest):
    sizes = round_sizes(slots)
    total = len(sizes)
    obs_out, pix_out = rest[: total * layers], rest[total * layers : (total + 1) * layers]
    obs, pix, obs_all, pix_all, fill, sems = rest[(total + 1) * layers :]
    loads = [
        pltpu.make_async_copy(obs_in, obs, sems.at[0]),
        pltpu.make_async_copy(pix_in, pix, sems.at[1]),
    ]
    for copy in loads:
        copy.start()
    my_layer, my_seat = lax.div(here[0], LAYER), lax.rem(here[0], LAYER)
    chunks = pix.shape[2] // CHUNK
    stride = slots + 1
    for x in range(layers):
        fill[x] = 0
    lane = lax.broadcasted_iota(jnp.int32, (8, CHUNK), 1)
    row = lax.broadcasted_iota(jnp.int32, (8, CHUNK), 0)
    for copy in loads:
        copy.wait()

    def put(b, infos):
        tile = tiles[b]
        count = counts[b]
        owner = lax.div(tile, local_tiles)
        x = lax.div(owner, LAYER) ^ my_layer
        seat = lax.rem(owner, LAYER) ^ my_seat
        spot = lax.rem(seat, PAIR) * PAIR + lax.div(seat, PAIR)
        screen = spot * local_tiles + lax.rem(tile, local_tiles)
        slot = fill[x]
        fill[x] = slot + lax.div(count + CHUNK - 1, CHUNK)
        for c in range(chunks):
            at = slot + c
            live = jnp.clip(count - c * CHUNK, 0, CHUNK)
            obs_all[x * stride + at] = obs[b, :, c * CHUNK : (c + 1) * CHUNK]
            pix_all[x * stride + at] = pix[b, :, c * CHUNK : (c + 1) * CHUNK]
            entry = jnp.where(row == 0, live, jnp.where(row == 1, tile, screen))
            here_only = (lane == at) & (row < 3)
            infos = tuple(
                jnp.where(here_only & (x == i), entry, info) for i, info in enumerate(infos)
            )
        return infos

    infos = lax.fori_loop(
        0, obs.shape[0], put, tuple(jnp.zeros((8, CHUNK), jnp.int32) for _ in range(layers))
    )
    copies = []
    for x in range(layers):
        at = x * stride
        pix_all[at + slots] = infos[x].astype(jnp.float32)
        copies.append((pix_all.at[pl.ds(at, stride)], pix_out[x]))
        for i, size in enumerate(sizes):
            copies.append((obs_all.at[pl.ds(at, size)], obs_out[i * layers + x]))
            at += size
    copies = [pltpu.make_async_copy(a, b, sems.at[i]) for i, (a, b) in enumerate(copies)]
    for copy in copies:
        copy.start()
    for copy in copies:
        copy.wait()


def pack(observations, pixel_geometry, block_counts, block_tiles, here, devices, local_tiles):
    blocks, epochs, width = observations.shape
    layers = devices // LAYER
    slots = LAYER * (2 * blocks // devices) * (width // CHUNK)
    sizes = round_sizes(slots)
    smem = pl.BlockSpec(memory_space=pltpu.SMEM)
    hbm = pl.BlockSpec(memory_space=pl.ANY)
    pix_part = jax.ShapeDtypeStruct((slots + 1, 8, CHUNK), jnp.float32)
    out = pl.pallas_call(
        functools.partial(pack_kernel, local_tiles, layers, slots),
        in_specs=[smem, smem, smem, hbm, hbm],
        out_specs=[hbm] * ((len(sizes) + 1) * layers),
        out_shape=[
            jax.ShapeDtypeStruct((size, epochs, CHUNK), observations.dtype)
            for size in sizes
            for _ in range(layers)
        ]
        + [pix_part] * layers,
        scratch_shapes=[
            pltpu.VMEM(observations.shape, observations.dtype),
            pltpu.VMEM(pixel_geometry.shape, jnp.float32),
            pltpu.VMEM((layers * (slots + 1), epochs, CHUNK), observations.dtype),
            pltpu.VMEM((layers * (slots + 1), 8, CHUNK), jnp.float32),
            pltpu.SMEM((layers,), jnp.int32),
            pltpu.SemaphoreType.DMA(((len(sizes) + 1) * layers,)),
        ],
        compiler_params=pltpu.CompilerParams(vmem_limit_bytes=10 * MIB),
        name="pack",
    )(here, block_tiles, block_counts, observations, pixel_geometry)
    rounds = len(sizes)
    return [out[i * layers : (i + 1) * layers] for i in range(rounds)], out[rounds * layers :]


def split(values):
    parts = []
    for _ in range(3):
        part = lax.reduce_precision(values, 8, 7)
        parts.append(part)
        values = values - part
    return parts


def kernel_split(values):
    parts = []
    for _ in range(3):
        part = values.astype(jnp.bfloat16).astype(jnp.float32)
        parts.append(part)
        values = values - part
    return parts


def fit_kernel(first, final, layers, slots, groups, *refs):
    info, cutoffs, places, spots, origin = refs[:5]
    rest = refs[5:]
    obs_in, pix_in = [], []
    for _ in groups:
        obs_in.append(rest[:layers])
        pix_in.append(rest[layers : 2 * layers])
        rest = rest[2 * layers :]
    patches, forms = rest[:2]
    rest = rest[1:]
    if first:
        screen_parts, stress_parts = rest[1 : 1 + LAYER], rest[1 + LAYER : 1 + 2 * LAYER]
        rest = rest[1 + 2 * LAYER :]
        grad, screen_grad, screens, stress = rest[:4]
        rest = rest[4:]
    else:
        screens, stress = rest[1:3]
        grad, screen_grad = rest[5:7]
        rest = rest[7:]
    outs = rest[:3] if final else ()
    rest = rest[len(outs) :]
    obs, pix, green_a, hats_a, green_b, hats_b, wide, sights, items, sems = rest
    epochs = obs.shape[1]
    base = groups[0][0]
    span = sum(size for _, _, size in groups)
    local_tiles = screens.shape[0] // LAYER

    loads = []
    for x in range(layers):
        at = x * span
        for g, (_, low, size) in enumerate(groups):
            loads.append((obs_in[g][x], obs.at[pl.ds(at, size)]))
            loads.append((pix_in[g][x].at[pl.ds(low, size)], pix.at[pl.ds(at, size)]))
            at += size
    if first:
        for parts, whole in ((screen_parts, screens), (stress_parts, stress)):
            size = whole.shape[0] // LAYER
            for i, part in enumerate(parts):
                loads.append((part, whole.at[pl.ds(i * size, size)]))
    loads = [pltpu.make_async_copy(a, b, sems.at[i]) for i, (a, b) in enumerate(loads)]
    for copy in loads:
        copy.start()
    if first:
        grad[...] = jnp.zeros_like(grad)
        screen_grad[...] = jnp.zeros_like(screen_grad)

    def info_of(slot, kind):
        x = lax.div(slot, span)
        return info[(x * 3 + kind) * slots + base + lax.rem(slot, span)]

    def list_slot(slot, total):
        items[total] = slot
        return total + jnp.where(info_of(slot, 0) > 0, 1, 0)

    total = lax.fori_loop(0, layers * span, list_slot, 0)
    for copy in loads:
        copy.wait()

    def item_of(i):
        slot = items[jnp.minimum(i, total - 1)]
        tile = info_of(slot, 1)
        return slot, [cutoffs[tile * NEAR + k] for k in range(NEAR)]

    def spread(rows, sights):
        columns = rows.T
        for i in range(2):
            wide[i] = jnp.broadcast_to(columns[:, i : i + 1], (CHUNK, CHUNK))
        le, ln = rows[4:5], rows[5:6]
        along = le * (rows[0:1] - origin[0]) + ln * (rows[1:2] - origin[1])
        row = lax.broadcasted_iota(jnp.int32, (8, CHUNK), 0)
        factors = jnp.where(
            row == 0, along, jnp.where(row == 1, le, jnp.where(row == 2, ln, rows[6:7]))
        )
        parts = kernel_split(factors)
        low = row < 4
        tiles = []
        for first_part, second_part in zip(CROSS[::2], CROSS[1::2]):
            upper = jnp.concatenate([parts[second_part[0]][:4]] * 2, axis=0)
            tiles.append(jnp.where(low, parts[first_part[0]], upper))
        tiles.append(jnp.zeros((8, CHUNK), jnp.float32))
        sights[...] = jnp.concatenate(tiles, axis=0).T.astype(jnp.bfloat16)

    def make_strips(near, k, lows, sights, green):
        patch = [
            jnp.broadcast_to(patches[near[k], r : r + 1], (8, PBLK)) for r in range(3)
        ]
        begin, end = lows[0], lows[-1] + 16
        alongs = jnp.dot(sights[begin:end], forms[near[k]], preferred_element_type=jnp.float32)
        for low in lows:
            along = alongs[low - begin : low - begin + 16]
            inverses = []
            for at in (low, low + 8):
                east, north = (
                    jnp.concatenate([wide[i, at : at + 8]] * (PBLK // CHUNK), axis=1)
                    for i in range(2)
                )
                dx = east - patch[0]
                dy = north - patch[1]
                inverses.append(lax.rsqrt(dx * dx + dy * dy + patch[2]))
            inverse = jnp.concatenate(inverses, axis=0)
            green[low : low + 16, k * PBLK : (k + 1) * PBLK] = (
                along * inverse * inverse * inverse
            ).astype(jnp.bfloat16)

    def make_hats(rows, hats):
        node = lax.broadcasted_iota(jnp.int32, (SG, CHUNK), 0).astype(jnp.float32)
        across = jnp.maximum(0.0, 1.0 - jnp.abs(rows[2:3] - node))
        upward = jnp.maximum(0.0, 1.0 - jnp.abs(rows[3:4] - node))
        for a in range(SG):
            hats[a * SG : (a + 1) * SG] = (across[a : a + 1] * upward).astype(jnp.bfloat16)

    def make_all(i, green, hats):
        slot, near = item_of(i)
        rows = pix[slot]
        make_hats(rows, hats)
        spread(rows, sights)
        for k in range(NEAR):
            for low in (0, CHUNK // 2):
                make_strips(near, k, range(low, low + CHUNK // 2, 16), sights, green)

    def turn(i, green, hats, green_next, hats_next):
        slot, near = item_of(i)
        slot_next, near_next = item_of(i + 1)
        rows = pix[slot_next]
        screen = info_of(slot, 2)

        def fill(k, low, high):
            make_strips(near_next, k, range(low, high, 16), sights, green_next)

        model = jnp.dot(screens[screen], hats[...], preferred_element_type=jnp.float32)
        for k in range(NEAR):
            model += lax.dot_general(
                stress[pl.ds(pl.multiple_of(spots[near[k]], 16), epochs), :],
                green[:, k * PBLK : (k + 1) * PBLK],
                (((1,), (1,)), ((), ())),
                preferred_element_type=jnp.float32,
            )
        make_hats(rows, hats_next)
        spread(rows, sights)
        fill(0, 0, CHUNK // 2)
        fill(0, CHUNK // 2, CHUNK)
        live = jnp.where(i < total, info_of(slot, 0), 0)
        lane = lax.broadcasted_iota(jnp.int32, (1, CHUNK), 1)
        scale = jnp.where(lane < live, pix[slot, 7:8, :], 0.0)
        weighted = ((model - obs[slot].astype(jnp.float32)) * scale).astype(jnp.bfloat16)

        def add(k):
            grad[places[near[k]]] += jnp.dot(
                weighted,
                green[:, k * PBLK : (k + 1) * PBLK],
                preferred_element_type=jnp.float32,
            )

        add(0)
        fill(1, 0, CHUNK // 2)
        add(1)
        fill(1, CHUNK // 2, CHUNK)
        add(2)
        fill(2, 0, CHUNK // 2)
        screen_grad[screen] += lax.dot_general(
            weighted, hats[...], (((1,), (1,)), ((), ())), preferred_element_type=jnp.float32
        )
        fill(2, CHUNK // 2, CHUNK)

    @pl.when(total > 0)
    def _():
        make_all(0, green_a, hats_a)

        def step(j, _):
            turn(2 * j, green_a, hats_a, green_b, hats_b)
            turn(2 * j + 1, green_b, hats_b, green_a, hats_a)
            return 0

        lax.fori_loop(0, lax.div(total + 1, 2), step, 0)

    if final:
        half = grad.shape[0] // 2
        outs[0][...] = grad[half:].astype(outs[0].dtype)
        for i, out in enumerate(outs[1:]):
            low = (PAIR + i) * local_tiles
            out[...] = screen_grad[low : low + local_tiles].astype(out.dtype)


def fit(tables, groups, patches, forms, screens, stress, state, first, final):
    layers = len(groups[0][1])
    slots = tables[0].shape[0] // (3 * layers)
    smem = pl.BlockSpec(memory_space=pltpu.SMEM)
    vmem = pl.BlockSpec(memory_space=pltpu.VMEM)
    hbm = pl.BlockSpec(memory_space=pl.ANY)
    spans = tuple((base, low, obs[0].shape[0]) for base, obs, _, low in groups)
    arrays = [a for _, obs, pix, _ in groups for a in (*obs, *pix)]
    span = sum(size for _, _, size in spans)
    blocks, epochs = state[0].shape[0], state[0].shape[1]
    out_shape = [jax.ShapeDtypeStruct(a.shape, a.dtype) for a in state]
    if first:
        state = ()
        for parts in (screens, stress):
            shape = (LAYER * parts[0].shape[0],) + parts[0].shape[1:]
            out_shape.append(jax.ShapeDtypeStruct(shape, parts[0].dtype))
    else:
        screens, stress = [screens], [stress]
    if final:
        out_shape.append(jax.ShapeDtypeStruct((blocks // 2, epochs, PBLK), jnp.bfloat16))
        shape = (state[1].shape[0] // LAYER,) + state[1].shape[1:]
        out_shape += [jax.ShapeDtypeStruct(shape, jnp.bfloat16)] * 2
    before = len(tables) + len(arrays) + 2 + len(screens) + len(stress)
    return pl.pallas_call(
        functools.partial(fit_kernel, first, final, layers, slots, spans),
        in_specs=[smem] * len(tables)
        + [hbm] * len(arrays)
        + [vmem] * 2
        + [hbm if first else vmem] * (len(screens) + len(stress))
        + [vmem] * len(state),
        out_specs=[vmem] * len(out_shape),
        out_shape=out_shape,
        scratch_shapes=[
            pltpu.VMEM((layers * span, epochs, CHUNK), arrays[0].dtype),
            pltpu.VMEM((layers * span, 8, CHUNK), jnp.float32),
        ]
        + [
            pltpu.VMEM((CHUNK, NEAR * PBLK), jnp.bfloat16),
            pltpu.VMEM((SG * SG, CHUNK), jnp.bfloat16),
        ]
        * 2
        + [
            pltpu.VMEM((2, CHUNK, CHUNK), jnp.float32),
            pltpu.VMEM((CHUNK, TERMS), jnp.bfloat16),
            pltpu.SMEM((layers * span + 1,), jnp.int32),
            pltpu.SemaphoreType.DMA((2 * layers * len(groups) + 2 * LAYER,)),
        ],
        input_output_aliases={} if first else {before: 0, before + 1: 1},
        compiler_params=pltpu.CompilerParams(vmem_limit_bytes=8 * MIB),
        cost_estimate=pl.CostEstimate(
            flops=layers * span * 4 * epochs * CHUNK * (NEAR + 1) * PBLK,
            bytes_accessed=20 * MIB,
            transcendentals=layers * span * CHUNK * NEAR * PBLK,
        ),
        name="fit",
    )(*tables, *arrays, patches, forms, *screens, *stress, *state)


def partner(values, devices, distance):
    return lax.ppermute(values, "tile", [(i, i ^ distance) for i in range(devices)])


def orders(devices):
    stages = devices.bit_length() - 1
    high = list(range(stages - 1, 1, -1))
    return [1] + high, high + [1]


def block_places(devices, here, blocks, local, epochs):
    block = jnp.arange(blocks)
    other = (block // local) ^ here
    seat = block % local
    half = local // 2
    turned = []
    for order in orders(devices):
        spot = 0
        for bit in order:
            spot = spot * 2 + ((other >> bit) & 1)
        turned.append(spot)
    chips = devices // 2
    upper = seat // half
    spot = jnp.where(upper == 0, turned[0], turned[1])
    place = (((other & 1) * 2 + upper) * chips + spot) * half + seat % half
    stages = devices.bit_length() - 1
    held = sum(((other >> (stages - 1 - s)) & 1) << s for s in range(stages))
    return place.astype(jnp.int32), ((held * local + seat) * epochs).astype(jnp.int32)


def halve(kept, given, there, devices):
    total = kept + partner(given, devices, 1).astype(jnp.float32)
    middle = total.shape[0] // 2
    parts = [total[:middle], total[middle:]]
    both = orders(devices)
    stages = len(both[0])
    back = None
    for stage in range(stages):
        got = []
        for side in range(2):
            given = parts[side][parts[side].shape[0] // 2 :]
            if stages - stage <= NARROW:
                given = given.astype(jnp.bfloat16)
            got.append(partner(given, devices, 1 << both[side][stage]))
        for side in range(2):
            if side:
                parts[0], got[1] = lax.optimization_barrier((parts[0], got[1]))
            size = parts[side].shape[0] // 2
            parts[side] = parts[side][:size] + got[side].astype(jnp.float32)
            if back is None:
                parts[0], there = lax.optimization_barrier((parts[0], there))
                back = partner(there, devices, PAIR)
    return jnp.concatenate(parts, axis=0), back


def on_device(
    observations,
    pixel_geometry,
    block_counts,
    block_tiles,
    cutoff_lists,
    patch_geometry,
    stress,
    screens,
):
    devices = lax.axis_size("tile")
    here = lax.axis_index("tile")
    blocks, epochs, width = observations.shape
    local_tiles = screens.shape[0]
    layers = devices // LAYER
    local = stress.shape[1] // PBLK

    slots = LAYER * (2 * blocks // devices) * (width // CHUNK)
    sizes = round_sizes(slots)

    held = jnp.swapaxes(stress.reshape(epochs, local, PBLK), 0, 1).reshape(-1, PBLK)
    other = partner(held, devices, devices // 2)
    across_screens = partner(screens, devices, PAIR)
    obs, pix = pack(
        observations,
        pixel_geometry,
        block_counts,
        block_tiles,
        jnp.reshape(here, (1,)).astype(jnp.int32),
        devices,
        local_tiles,
    )

    def exchange(parts):
        return [parts[0]] + [partner(parts[x], devices, x * LAYER) for x in range(1, layers)]

    other, pix = lax.optimization_barrier((other, pix))
    pix = exchange(pix)
    distance = devices // 2
    while distance >= LAYER:
        if distance < devices // 2:
            other = partner(held, devices, distance)
        held = jnp.concatenate([held, other], axis=0)
        distance //= 2
    held, pix, across_screens = lax.optimization_barrier((held, pix, across_screens))
    got = [exchange(o) for o in obs]
    across = partner(held, devices, PAIR)
    across, got[0][1] = lax.optimization_barrier((across, got[0][1]))
    all_stress = [held, across, partner(held, devices, 1), partner(across, devices, 1)]
    all_screens = [
        screens,
        across_screens,
        partner(screens, devices, 1),
        partner(across_screens, devices, 1),
    ]

    patch_blocks = devices * local
    east, north, depth, compliance = patch_geometry
    origin = patch_geometry[:2, 0]
    strength = compliance * depth * depth
    faces = split(
        jnp.stack(
            [
                strength,
                -strength * (east - origin[0]),
                -strength * (north - origin[1]),
                strength * depth,
            ]
        )
    )
    forms = jnp.concatenate(
        [faces[second] for _, second in CROSS] + [jnp.zeros((8,) + east.shape, jnp.float32)]
    ).astype(jnp.bfloat16)
    forms = jnp.swapaxes(forms.reshape(TERMS, patch_blocks, PBLK), 0, 1)
    patches = jnp.stack([east, north, depth * depth])
    patches = jnp.swapaxes(patches.reshape(3, patch_blocks, PBLK), 0, 1)
    places, spots = block_places(devices, here, patch_blocks, local, epochs)
    info = jnp.stack([p[slots, :3, :slots] for p in pix]).astype(jnp.int32).reshape(-1)
    tables = (info, cutoff_lists.reshape(-1), places, spots, origin)

    state = (
        jax.ShapeDtypeStruct((patch_blocks, epochs, PBLK), jnp.float32),
        jax.ShapeDtypeStruct((LAYER * local_tiles,) + screens.shape[1:], jnp.float32),
    )
    base = 0
    for i, size in enumerate(sizes):
        first, final = i == 0, i == len(sizes) - 1
        groups = [(base, got[i], pix, base)]
        state = fit(
            tables,
            groups,
            patches,
            forms,
            all_screens,
            all_stress,
            state[:2],
            first,
            final,
        )
        if first:
            all_screens, all_stress = state[2:]
        base += size
    grad, screen_grad, given, next_door, diagonal = state
    own, far = screen_grad[:local_tiles], screen_grad[local_tiles : PAIR * local_tiles]
    there = (far + partner(diagonal, devices, 1).astype(jnp.float32)).astype(jnp.bfloat16)
    grad, back = halve(grad[: grad.shape[0] // 2], given, there, devices)
    screen_gradient = (
        own + partner(next_door, devices, 1).astype(jnp.float32) + back.astype(jnp.float32)
    )
    return (jnp.swapaxes(grad, 0, 1).reshape(epochs, local * PBLK), screen_gradient)


def solution(mesh):
    return jax.shard_map(
        on_device,
        mesh=mesh,
        in_specs=(
            P(("groups", "tile"), None, None),
            P(("groups", "tile"), None, None),
            P(("groups", "tile")),
            P(("groups", "tile")),
            P(),
            P(),
            P(None, ("groups", "tile")),
            P(("groups", "tile"), None, None),
        ),
        out_specs=(P(None, ("groups", "tile")), P(("groups", "tile"), None, None)),
        check_vma=False,
    )
```

```python
import functools

import jax
import jax.numpy as jnp
from jax import lax
from jax.experimental import pallas as pl
from jax.experimental.pallas import tpu as pltpu
from jax.sharding import PartitionSpec as P

PBLK = 256
NEAR = 3
SG = 16
CHUNK = 128
LAYER = 4
PAIR = 2
NARROW = 3
ROUNDS = (6, 6, 4)
MIB = 1 << 20
TERMS = 32
CROSS = ((0, 0), (0, 1), (1, 0), (0, 2), (1, 1), (2, 0))


def round_sizes(slots):
    return [slots * r // sum(ROUNDS) for r in ROUNDS]


def pack_kernel(local_tiles, layers, slots, here, tiles, counts, obs_in, pix_in, *rest):
    sizes = round_sizes(slots)
    total = len(sizes)
    obs_out, pix_out = rest[: total * layers], rest[total * layers : (total + 1) * layers]
    obs, pix, obs_all, pix_all, fill, sems = rest[(total + 1) * layers :]
    loads = [
        pltpu.make_async_copy(obs_in, obs, sems.at[0]),
        pltpu.make_async_copy(pix_in, pix, sems.at[1]),
    ]
    for copy in loads:
        copy.start()
    my_layer, my_seat = lax.div(here[0], LAYER), lax.rem(here[0], LAYER)
    chunks = pix.shape[2] // CHUNK
    stride = slots + 1
    for x in range(layers):
        fill[x] = 0
    lane = lax.broadcasted_iota(jnp.int32, (8, CHUNK), 1)
    row = lax.broadcasted_iota(jnp.int32, (8, CHUNK), 0)
    for copy in loads:
        copy.wait()

    def put(b, infos):
        tile = tiles[b]
        count = counts[b]
        owner = lax.div(tile, local_tiles)
        x = lax.div(owner, LAYER) ^ my_layer
        seat = lax.rem(owner, LAYER) ^ my_seat
        spot = lax.rem(seat, PAIR) * PAIR + lax.div(seat, PAIR)
        screen = spot * local_tiles + lax.rem(tile, local_tiles)
        slot = fill[x]
        fill[x] = slot + lax.div(count + CHUNK - 1, CHUNK)
        for c in range(chunks):
            at = slot + c
            live = jnp.clip(count - c * CHUNK, 0, CHUNK)
            obs_all[x * stride + at] = obs[b, :, c * CHUNK : (c + 1) * CHUNK]
            pix_all[x * stride + at] = pix[b, :, c * CHUNK : (c + 1) * CHUNK]
            entry = jnp.where(row == 0, live, jnp.where(row == 1, tile, screen))
            here_only = (lane == at) & (row < 3)
            infos = tuple(
                jnp.where(here_only & (x == i), entry, info) for i, info in enumerate(infos)
            )
        return infos

    infos = lax.fori_loop(
        0, obs.shape[0], put, tuple(jnp.zeros((8, CHUNK), jnp.int32) for _ in range(layers))
    )
    copies = []
    for x in range(layers):
        at = x * stride
        pix_all[at + slots] = infos[x].astype(jnp.float32)
        copies.append((pix_all.at[pl.ds(at, stride)], pix_out[x]))
        for i, size in enumerate(sizes):
            copies.append((obs_all.at[pl.ds(at, size)], obs_out[i * layers + x]))
            at += size
    copies = [pltpu.make_async_copy(a, b, sems.at[i]) for i, (a, b) in enumerate(copies)]
    for copy in copies:
        copy.start()
    for copy in copies:
        copy.wait()


def pack(observations, pixel_geometry, block_counts, block_tiles, here, devices, local_tiles):
    blocks, epochs, width = observations.shape
    layers = devices // LAYER
    slots = LAYER * (2 * blocks // devices) * (width // CHUNK)
    sizes = round_sizes(slots)
    smem = pl.BlockSpec(memory_space=pltpu.SMEM)
    hbm = pl.BlockSpec(memory_space=pl.ANY)
    pix_part = jax.ShapeDtypeStruct((slots + 1, 8, CHUNK), jnp.float32)
    out = pl.pallas_call(
        functools.partial(pack_kernel, local_tiles, layers, slots),
        in_specs=[smem, smem, smem, hbm, hbm],
        out_specs=[hbm] * ((len(sizes) + 1) * layers),
        out_shape=[
            jax.ShapeDtypeStruct((size, epochs, CHUNK), observations.dtype)
            for size in sizes
            for _ in range(layers)
        ]
        + [pix_part] * layers,
        scratch_shapes=[
            pltpu.VMEM(observations.shape, observations.dtype),
            pltpu.VMEM(pixel_geometry.shape, jnp.float32),
            pltpu.VMEM((layers * (slots + 1), epochs, CHUNK), observations.dtype),
            pltpu.VMEM((layers * (slots + 1), 8, CHUNK), jnp.float32),
            pltpu.SMEM((layers,), jnp.int32),
            pltpu.SemaphoreType.DMA(((len(sizes) + 1) * layers,)),
        ],
        compiler_params=pltpu.CompilerParams(vmem_limit_bytes=10 * MIB),
        name="pack",
    )(here, block_tiles, block_counts, observations, pixel_geometry)
    rounds = len(sizes)
    return [out[i * layers : (i + 1) * layers] for i in range(rounds)], out[rounds * layers :]


def split(values):
    parts = []
    for _ in range(3):
        part = lax.reduce_precision(values, 8, 7)
        parts.append(part)
        values = values - part
    return parts


def kernel_split(values):
    parts = []
    for _ in range(3):
        part = values.astype(jnp.bfloat16).astype(jnp.float32)
        parts.append(part)
        values = values - part
    return parts


def fit_kernel(first, final, layers, slots, groups, *refs):
    info, cutoffs, places, spots, origin = refs[:5]
    rest = refs[5:]
    obs_in, pix_in = [], []
    for _ in groups:
        obs_in.append(rest[:layers])
        pix_in.append(rest[layers : 2 * layers])
        rest = rest[2 * layers :]
    patches, forms = rest[:2]
    rest = rest[1:]
    if first:
        screen_parts, stress_parts = rest[1 : 1 + LAYER], rest[1 + LAYER : 1 + 2 * LAYER]
        rest = rest[1 + 2 * LAYER :]
        grad, screen_grad, screens, stress = rest[:4]
        rest = rest[4:]
    else:
        screens, stress = rest[1:3]
        grad, screen_grad = rest[5:7]
        rest = rest[7:]
    outs = rest[:3] if final else ()
    rest = rest[len(outs) :]
    obs, pix, green_a, hats_a, green_b, hats_b, wide, sights, items, sems = rest
    epochs = obs.shape[1]
    base = groups[0][0]
    span = sum(size for _, _, size in groups)
    local_tiles = screens.shape[0] // LAYER

    loads = []
    for x in range(layers):
        at = x * span
        for g, (_, low, size) in enumerate(groups):
            loads.append((obs_in[g][x], obs.at[pl.ds(at, size)]))
            loads.append((pix_in[g][x].at[pl.ds(low, size)], pix.at[pl.ds(at, size)]))
            at += size
    if first:
        for parts, whole in ((screen_parts, screens), (stress_parts, stress)):
            size = whole.shape[0] // LAYER
            for i, part in enumerate(parts):
                loads.append((part, whole.at[pl.ds(i * size, size)]))
    loads = [pltpu.make_async_copy(a, b, sems.at[i]) for i, (a, b) in enumerate(loads)]
    for copy in loads:
        copy.start()
    if first:
        grad[...] = jnp.zeros_like(grad)
        screen_grad[...] = jnp.zeros_like(screen_grad)

    def info_of(slot, kind):
        x = lax.div(slot, span)
        return info[(x * 3 + kind) * slots + base + lax.rem(slot, span)]

    def list_slot(slot, total):
        items[total] = slot
        return total + jnp.where(info_of(slot, 0) > 0, 1, 0)

    total = lax.fori_loop(0, layers * span, list_slot, 0)
    for copy in loads:
        copy.wait()

    def item_of(i):
        slot = items[jnp.minimum(i, total - 1)]
        tile = info_of(slot, 1)
        return slot, [cutoffs[tile * NEAR + k] for k in range(NEAR)]

    def spread(rows, sights):
        columns = rows.T
        for i in range(2):
            wide[i] = jnp.broadcast_to(columns[:, i : i + 1], (CHUNK, CHUNK))
        le, ln = rows[4:5], rows[5:6]
        along = le * (rows[0:1] - origin[0]) + ln * (rows[1:2] - origin[1])
        row = lax.broadcasted_iota(jnp.int32, (8, CHUNK), 0)
        factors = jnp.where(
            row == 0, along, jnp.where(row == 1, le, jnp.where(row == 2, ln, rows[6:7]))
        )
        parts = kernel_split(factors)
        low = row < 4
        tiles = []
        for first_part, second_part in zip(CROSS[::2], CROSS[1::2]):
            upper = jnp.concatenate([parts[second_part[0]][:4]] * 2, axis=0)
            tiles.append(jnp.where(low, parts[first_part[0]], upper))
        tiles.append(jnp.zeros((8, CHUNK), jnp.float32))
        sights[...] = jnp.concatenate(tiles, axis=0).T.astype(jnp.bfloat16)

    def make_strips(near, k, lows, sights, green):
        patch = [
            jnp.broadcast_to(patches[near[k], r : r + 1], (8, PBLK)) for r in range(3)
        ]
        begin, end = lows[0], lows[-1] + 16
        alongs = jnp.dot(sights[begin:end], forms[near[k]], preferred_element_type=jnp.float32)
        for low in lows:
            along = alongs[low - begin : low - begin + 16]
            inverses = []
            for at in (low, low + 8):
                east, north = (
                    jnp.concatenate([wide[i, at : at + 8]] * (PBLK // CHUNK), axis=1)
                    for i in range(2)
                )
                dx = east - patch[0]
                dy = north - patch[1]
                inverses.append(lax.rsqrt(dx * dx + dy * dy + patch[2]))
            inverse = jnp.concatenate(inverses, axis=0)
            green[low : low + 16, k * PBLK : (k + 1) * PBLK] = (
                along * inverse * inverse * inverse
            ).astype(jnp.bfloat16)

    def make_hats(rows, hats):
        node = lax.broadcasted_iota(jnp.int32, (SG, CHUNK), 0).astype(jnp.float32)
        across = jnp.maximum(0.0, 1.0 - jnp.abs(rows[2:3] - node))
        upward = jnp.maximum(0.0, 1.0 - jnp.abs(rows[3:4] - node))
        for a in range(SG):
            hats[a * SG : (a + 1) * SG] = (across[a : a + 1] * upward).astype(jnp.bfloat16)

    def make_all(i, green, hats):
        slot, near = item_of(i)
        rows = pix[slot]
        make_hats(rows, hats)
        spread(rows, sights)
        for k in range(NEAR):
            for low in (0, CHUNK // 2):
                make_strips(near, k, range(low, low + CHUNK // 2, 16), sights, green)

    def turn(i, green, hats, green_next, hats_next):
        slot, near = item_of(i)
        slot_next, near_next = item_of(i + 1)
        rows = pix[slot_next]
        screen = info_of(slot, 2)

        def fill(k, low, high):
            make_strips(near_next, k, range(low, high, 16), sights, green_next)

        model = jnp.dot(screens[screen], hats[...], preferred_element_type=jnp.float32)
        side = lax.broadcasted_iota(jnp.int32, (1, 2 * epochs), 1) >= epochs
        turned = jnp.zeros((CHUNK, 2 * epochs), jnp.float32)
        for k in range(NEAR):
            both = jnp.dot(
                green[:, k * PBLK : (k + 1) * PBLK],
                stress[pl.ds(pl.multiple_of(spots[near[k]], PBLK), PBLK), :],
                preferred_element_type=jnp.float32,
            )
            odd = lax.rem(near[k], 2) == 1
            turned += jnp.where(side == odd, both, 0.0)
        make_hats(rows, hats_next)
        spread(rows, sights)
        fill(0, 0, CHUNK // 2)
        turned = turned.T
        model += turned[:epochs] + turned[epochs:]
        fill(0, CHUNK // 2, CHUNK)
        live = jnp.where(i < total, info_of(slot, 0), 0)
        lane = lax.broadcasted_iota(jnp.int32, (1, CHUNK), 1)
        scale = jnp.where(lane < live, pix[slot, 7:8, :], 0.0)
        weighted = ((model - obs[slot].astype(jnp.float32)) * scale).astype(jnp.bfloat16)

        def add(k):
            grad[places[near[k]]] += jnp.dot(
                weighted,
                green[:, k * PBLK : (k + 1) * PBLK],
                preferred_element_type=jnp.float32,
            )

        add(0)
        fill(1, 0, CHUNK // 2)
        add(1)
        fill(1, CHUNK // 2, CHUNK)
        add(2)
        fill(2, 0, CHUNK // 2)
        screen_grad[screen] += lax.dot_general(
            weighted, hats[...], (((1,), (1,)), ((), ())), preferred_element_type=jnp.float32
        )
        fill(2, CHUNK // 2, CHUNK)

    @pl.when(total > 0)
    def _():
        make_all(0, green_a, hats_a)

        def step(j, _):
            turn(2 * j, green_a, hats_a, green_b, hats_b)
            turn(2 * j + 1, green_b, hats_b, green_a, hats_a)
            return 0

        lax.fori_loop(0, lax.div(total + 1, 2), step, 0)

    if final:
        half = grad.shape[0] // 2
        outs[0][...] = grad[half:].astype(outs[0].dtype)
        for i, out in enumerate(outs[1:]):
            low = (PAIR + i) * local_tiles
            out[...] = screen_grad[low : low + local_tiles].astype(out.dtype)


def fit(tables, groups, patches, forms, screens, stress, state, first, final):
    layers = len(groups[0][1])
    slots = tables[0].shape[0] // (3 * layers)
    smem = pl.BlockSpec(memory_space=pltpu.SMEM)
    vmem = pl.BlockSpec(memory_space=pltpu.VMEM)
    hbm = pl.BlockSpec(memory_space=pl.ANY)
    spans = tuple((base, low, obs[0].shape[0]) for base, obs, _, low in groups)
    arrays = [a for _, obs, pix, _ in groups for a in (*obs, *pix)]
    span = sum(size for _, _, size in spans)
    blocks, epochs = state[0].shape[0], state[0].shape[1]
    out_shape = [jax.ShapeDtypeStruct(a.shape, a.dtype) for a in state]
    if first:
        state = ()
        for parts in (screens, stress):
            shape = (LAYER * parts[0].shape[0],) + parts[0].shape[1:]
            out_shape.append(jax.ShapeDtypeStruct(shape, parts[0].dtype))
    else:
        screens, stress = [screens], [stress]
    if final:
        out_shape.append(jax.ShapeDtypeStruct((blocks // 2, epochs, PBLK), jnp.bfloat16))
        shape = (state[1].shape[0] // LAYER,) + state[1].shape[1:]
        out_shape += [jax.ShapeDtypeStruct(shape, jnp.bfloat16)] * 2
    before = len(tables) + len(arrays) + 2 + len(screens) + len(stress)
    return pl.pallas_call(
        functools.partial(fit_kernel, first, final, layers, slots, spans),
        in_specs=[smem] * len(tables)
        + [hbm] * len(arrays)
        + [vmem] * 2
        + [hbm if first else vmem] * (len(screens) + len(stress))
        + [vmem] * len(state),
        out_specs=[vmem] * len(out_shape),
        out_shape=out_shape,
        scratch_shapes=[
            pltpu.VMEM((layers * span, epochs, CHUNK), arrays[0].dtype),
            pltpu.VMEM((layers * span, 8, CHUNK), jnp.float32),
        ]
        + [
            pltpu.VMEM((CHUNK, NEAR * PBLK), jnp.bfloat16),
            pltpu.VMEM((SG * SG, CHUNK), jnp.bfloat16),
        ]
        * 2
        + [
            pltpu.VMEM((2, CHUNK, CHUNK), jnp.float32),
            pltpu.VMEM((CHUNK, TERMS), jnp.bfloat16),
            pltpu.SMEM((layers * span + 1,), jnp.int32),
            pltpu.SemaphoreType.DMA((2 * layers * len(groups) + 2 * LAYER,)),
        ],
        input_output_aliases={} if first else {before: 0, before + 1: 1},
        compiler_params=pltpu.CompilerParams(vmem_limit_bytes=8 * MIB),
        cost_estimate=pl.CostEstimate(
            flops=layers * span * 4 * epochs * CHUNK * (NEAR + 1) * PBLK,
            bytes_accessed=20 * MIB,
            transcendentals=layers * span * CHUNK * NEAR * PBLK,
        ),
        name="fit",
    )(*tables, *arrays, patches, forms, *screens, *stress, *state)


def partner(values, devices, distance):
    return lax.ppermute(values, "tile", [(i, i ^ distance) for i in range(devices)])


def orders(devices):
    stages = devices.bit_length() - 1
    high = list(range(stages - 1, 1, -1))
    return [1] + high, high + [1]


def block_places(devices, here, blocks, local, epochs):
    block = jnp.arange(blocks)
    other = (block // local) ^ here
    seat = block % local
    half = local // 2
    turned = []
    for order in orders(devices):
        spot = 0
        for bit in order:
            spot = spot * 2 + ((other >> bit) & 1)
        turned.append(spot)
    chips = devices // 2
    upper = seat // half
    spot = jnp.where(upper == 0, turned[0], turned[1])
    place = (((other & 1) * 2 + upper) * chips + spot) * half + seat % half
    stages = devices.bit_length() - 1
    held = sum(((other >> (stages - 1 - s)) & 1) << s for s in range(stages))
    return place.astype(jnp.int32), ((held * local + seat) // 2 * PBLK).astype(jnp.int32)


def halve(kept, given, there, devices):
    total = kept + partner(given, devices, 1).astype(jnp.float32)
    middle = total.shape[0] // 2
    parts = [total[:middle], total[middle:]]
    both = orders(devices)
    stages = len(both[0])
    back = partner(there, devices, PAIR)
    for stage in range(stages):
        got = []
        for side in range(2):
            given = parts[side][parts[side].shape[0] // 2 :]
            if stages - stage <= NARROW:
                given = given.astype(jnp.bfloat16)
            got.append(partner(given, devices, 1 << both[side][stage]))
        for side in range(2):
            if side:
                parts[0], got[1] = lax.optimization_barrier((parts[0], got[1]))
            size = parts[side].shape[0] // 2
            parts[side] = parts[side][:size] + got[side].astype(jnp.float32)
    return jnp.concatenate(parts, axis=0), back


def on_device(
    observations,
    pixel_geometry,
    block_counts,
    block_tiles,
    cutoff_lists,
    patch_geometry,
    stress,
    screens,
):
    devices = lax.axis_size("tile")
    here = lax.axis_index("tile")
    blocks, epochs, width = observations.shape
    local_tiles = screens.shape[0]
    layers = devices // LAYER
    local = stress.shape[1] // PBLK

    slots = LAYER * (2 * blocks // devices) * (width // CHUNK)
    sizes = round_sizes(slots)

    held = jnp.transpose(stress.reshape(epochs, local // 2, 2, PBLK), (1, 3, 2, 0))
    held = held.reshape(local // 2 * PBLK, 2 * epochs)
    other = partner(held, devices, devices // 2)
    across_screens = partner(screens, devices, PAIR)
    obs, pix = pack(
        observations,
        pixel_geometry,
        block_counts,
        block_tiles,
        jnp.reshape(here, (1,)).astype(jnp.int32),
        devices,
        local_tiles,
    )

    def exchange(parts):
        return [parts[0]] + [partner(parts[x], devices, x * LAYER) for x in range(1, layers)]

    other, pix = lax.optimization_barrier((other, pix))
    pix = exchange(pix)
    distance = devices // 2
    while distance >= LAYER:
        if distance < devices // 2:
            other = partner(held, devices, distance)
        held = jnp.concatenate([held, other], axis=0)
        distance //= 2
    held, pix, across_screens = lax.optimization_barrier((held, pix, across_screens))
    got = [exchange(o) for o in obs]
    across = partner(held, devices, PAIR)
    across, got[0][1] = lax.optimization_barrier((across, got[0][1]))
    all_stress = [held, across, partner(held, devices, 1), partner(across, devices, 1)]
    all_screens = [
        screens,
        across_screens,
        partner(screens, devices, 1),
        partner(across_screens, devices, 1),
    ]

    patch_blocks = devices * local
    east, north, depth, compliance = patch_geometry
    origin = patch_geometry[:2, 0]
    strength = compliance * depth * depth
    faces = split(
        jnp.stack(
            [
                strength,
                -strength * (east - origin[0]),
                -strength * (north - origin[1]),
                strength * depth,
            ]
        )
    )
    forms = jnp.concatenate(
        [faces[second] for _, second in CROSS] + [jnp.zeros((8,) + east.shape, jnp.float32)]
    ).astype(jnp.bfloat16)
    forms = jnp.swapaxes(forms.reshape(TERMS, patch_blocks, PBLK), 0, 1)
    patches = jnp.stack([east, north, depth * depth])
    patches = jnp.swapaxes(patches.reshape(3, patch_blocks, PBLK), 0, 1)
    places, spots = block_places(devices, here, patch_blocks, local, epochs)
    info = jnp.stack([p[slots, :3, :slots] for p in pix]).astype(jnp.int32).reshape(-1)
    tables = (info, cutoff_lists.reshape(-1), places, spots, origin)

    state = (
        jax.ShapeDtypeStruct((patch_blocks, epochs, PBLK), jnp.float32),
        jax.ShapeDtypeStruct((LAYER * local_tiles,) + screens.shape[1:], jnp.float32),
    )
    base = 0
    for i, size in enumerate(sizes):
        first, final = i == 0, i == len(sizes) - 1
        groups = [(base, got[i], pix, base)]
        state = fit(
            tables,
            groups,
            patches,
            forms,
            all_screens,
            all_stress,
            state[:2],
            first,
            final,
        )
        if first:
            all_screens, all_stress = state[2:]
        base += size
    grad, screen_grad, given, next_door, diagonal = state
    own, far = screen_grad[:local_tiles], screen_grad[local_tiles : PAIR * local_tiles]
    there = (far + partner(diagonal, devices, 1).astype(jnp.float32)).astype(jnp.bfloat16)
    grad, back = halve(grad[: grad.shape[0] // 2], given, there, devices)
    screen_gradient = (
        own + partner(next_door, devices, 1).astype(jnp.float32) + back.astype(jnp.float32)
    )
    return (jnp.swapaxes(grad, 0, 1).reshape(epochs, local * PBLK), screen_gradient)


def solution(mesh):
    return jax.shard_map(
        on_device,
        mesh=mesh,
        in_specs=(
            P(("groups", "tile"), None, None),
            P(("groups", "tile"), None, None),
            P(("groups", "tile")),
            P(("groups", "tile")),
            P(),
            P(),
            P(None, ("groups", "tile")),
            P(("groups", "tile"), None, None),
        ),
        out_specs=(P(None, ("groups", "tile")), P(("groups", "tile"), None, None)),
        check_vma=False,
    )
```

```python
import functools

import jax
import jax.numpy as jnp
from jax import lax
from jax.experimental import pallas as pl
from jax.experimental.pallas import tpu as pltpu
from jax.sharding import PartitionSpec as P

PBLK = 256
NEAR = 3
SG = 16
CHUNK = 128
LAYER = 4
PAIR = 2
NARROW = 3
ROUNDS = (6, 6, 4)
MIB = 1 << 20
TERMS = 32
CROSS = ((0, 0), (0, 1), (1, 0), (0, 2), (1, 1), (2, 0))


def round_sizes(slots):
    return [slots * r // sum(ROUNDS) for r in ROUNDS]


def pack_kernel(local_tiles, layers, slots, here, tiles, counts, obs_in, pix_in, *rest):
    sizes = round_sizes(slots)
    total = len(sizes)
    obs_out, pix_out = rest[: total * layers], rest[total * layers : (total + 1) * layers]
    obs, pix, obs_all, pix_all, fill, sems = rest[(total + 1) * layers :]
    loads = [
        pltpu.make_async_copy(obs_in, obs, sems.at[0]),
        pltpu.make_async_copy(pix_in, pix, sems.at[1]),
    ]
    for copy in loads:
        copy.start()
    my_layer, my_seat = lax.div(here[0], LAYER), lax.rem(here[0], LAYER)
    chunks = pix.shape[2] // CHUNK
    stride = slots + 1
    for x in range(layers):
        fill[x] = 0
    lane = lax.broadcasted_iota(jnp.int32, (8, CHUNK), 1)
    row = lax.broadcasted_iota(jnp.int32, (8, CHUNK), 0)
    for copy in loads:
        copy.wait()

    def put(b, infos):
        tile = tiles[b]
        count = counts[b]
        owner = lax.div(tile, local_tiles)
        x = lax.div(owner, LAYER) ^ my_layer
        seat = lax.rem(owner, LAYER) ^ my_seat
        spot = lax.rem(seat, PAIR) * PAIR + lax.div(seat, PAIR)
        screen = spot * local_tiles + lax.rem(tile, local_tiles)
        slot = fill[x]
        fill[x] = slot + lax.div(count + CHUNK - 1, CHUNK)
        for c in range(chunks):
            at = slot + c
            live = jnp.clip(count - c * CHUNK, 0, CHUNK)
            obs_all[x * stride + at] = obs[b, :, c * CHUNK : (c + 1) * CHUNK]
            pix_all[x * stride + at] = pix[b, :, c * CHUNK : (c + 1) * CHUNK]
            entry = jnp.where(row == 0, live, jnp.where(row == 1, tile, screen))
            here_only = (lane == at) & (row < 3)
            infos = tuple(
                jnp.where(here_only & (x == i), entry, info) for i, info in enumerate(infos)
            )
        return infos

    infos = lax.fori_loop(
        0, obs.shape[0], put, tuple(jnp.zeros((8, CHUNK), jnp.int32) for _ in range(layers))
    )
    copies = []
    for x in range(layers):
        at = x * stride
        pix_all[at + slots] = infos[x].astype(jnp.float32)
        copies.append((pix_all.at[pl.ds(at, stride)], pix_out[x]))
        for i, size in enumerate(sizes):
            copies.append((obs_all.at[pl.ds(at, size)], obs_out[i * layers + x]))
            at += size
    copies = [pltpu.make_async_copy(a, b, sems.at[i]) for i, (a, b) in enumerate(copies)]
    for copy in copies:
        copy.start()
    for copy in copies:
        copy.wait()


def pack(observations, pixel_geometry, block_counts, block_tiles, here, devices, local_tiles):
    blocks, epochs, width = observations.shape
    layers = devices // LAYER
    slots = LAYER * (2 * blocks // devices) * (width // CHUNK)
    sizes = round_sizes(slots)
    smem = pl.BlockSpec(memory_space=pltpu.SMEM)
    hbm = pl.BlockSpec(memory_space=pl.ANY)
    pix_part = jax.ShapeDtypeStruct((slots + 1, 8, CHUNK), jnp.float32)
    out = pl.pallas_call(
        functools.partial(pack_kernel, local_tiles, layers, slots),
        in_specs=[smem, smem, smem, hbm, hbm],
        out_specs=[hbm] * ((len(sizes) + 1) * layers),
        out_shape=[
            jax.ShapeDtypeStruct((size, epochs, CHUNK), observations.dtype)
            for size in sizes
            for _ in range(layers)
        ]
        + [pix_part] * layers,
        scratch_shapes=[
            pltpu.VMEM(observations.shape, observations.dtype),
            pltpu.VMEM(pixel_geometry.shape, jnp.float32),
            pltpu.VMEM((layers * (slots + 1), epochs, CHUNK), observations.dtype),
            pltpu.VMEM((layers * (slots + 1), 8, CHUNK), jnp.float32),
            pltpu.SMEM((layers,), jnp.int32),
            pltpu.SemaphoreType.DMA(((len(sizes) + 1) * layers,)),
        ],
        compiler_params=pltpu.CompilerParams(vmem_limit_bytes=10 * MIB),
        name="pack",
    )(here, block_tiles, block_counts, observations, pixel_geometry)
    rounds = len(sizes)
    return [out[i * layers : (i + 1) * layers] for i in range(rounds)], out[rounds * layers :]


def split(values):
    parts = []
    for _ in range(3):
        part = lax.reduce_precision(values, 8, 7)
        parts.append(part)
        values = values - part
    return parts


def kernel_split(values):
    parts = []
    for _ in range(3):
        part = values.astype(jnp.bfloat16).astype(jnp.float32)
        parts.append(part)
        values = values - part
    return parts


def fit_kernel(first, final, layers, slots, groups, *refs):
    info, cutoffs, places, spots, origin = refs[:5]
    rest = refs[5:]
    obs_in, pix_in = [], []
    for _ in groups:
        obs_in.append(rest[:layers])
        pix_in.append(rest[layers : 2 * layers])
        rest = rest[2 * layers :]
    patches, forms = rest[:2]
    rest = rest[1:]
    if first:
        screen_parts, stress_parts = rest[1 : 1 + LAYER], rest[1 + LAYER : 1 + 2 * LAYER]
        rest = rest[1 + 2 * LAYER :]
        grad, screen_grad, screens, stress = rest[:4]
        rest = rest[4:]
    else:
        screens, stress = rest[1:3]
        grad, screen_grad = rest[5:7]
        rest = rest[7:]
    outs = rest[:3] if final else ()
    rest = rest[len(outs) :]
    obs, pix = rest[:2]
    buffers = rest[2 : 2 + 9 * PAIR]
    wide, sights = rest[2 + 9 * PAIR : 2 + 10 * PAIR], rest[2 + 10 * PAIR : 2 + 11 * PAIR]
    items, sems = rest[2 + 11 * PAIR :]
    sets = [
        [buffers[3 * (PAIR * i + lane) : 3 * (PAIR * i + lane) + 3] for lane in range(PAIR)]
        for i in range(3)
    ]
    epochs = obs.shape[1]
    base = groups[0][0]
    span = sum(size for _, _, size in groups)
    local_tiles = screens.shape[0] // LAYER

    loads = []
    for x in range(layers):
        at = x * span
        for g, (_, low, size) in enumerate(groups):
            loads.append((obs_in[g][x], obs.at[pl.ds(at, size)]))
            loads.append((pix_in[g][x].at[pl.ds(low, size)], pix.at[pl.ds(at, size)]))
            at += size
    if first:
        for parts, whole in ((screen_parts, screens), (stress_parts, stress)):
            size = whole.shape[0] // LAYER
            for i, part in enumerate(parts):
                loads.append((part, whole.at[pl.ds(i * size, size)]))
    loads = [pltpu.make_async_copy(a, b, sems.at[i]) for i, (a, b) in enumerate(loads)]
    for copy in loads:
        copy.start()
    if first:
        grad[...] = jnp.zeros_like(grad)
        screen_grad[...] = jnp.zeros_like(screen_grad)

    def info_of(slot, kind):
        x = lax.div(slot, span)
        return info[(x * 3 + kind) * slots + base + lax.rem(slot, span)]

    def list_slot(slot, total):
        items[total] = slot
        return total + jnp.where(info_of(slot, 0) > 0, 1, 0)

    total = lax.fori_loop(0, layers * span, list_slot, 0)
    for copy in loads:
        copy.wait()

    def item_of(i):
        slot = items[jnp.minimum(i, total - 1)]
        tile = info_of(slot, 1)
        return slot, [cutoffs[tile * NEAR + k] for k in range(NEAR)]

    def spread(rows, lane):
        columns = rows.T
        for i in range(2):
            wide[lane][i] = jnp.broadcast_to(columns[:, i : i + 1], (CHUNK, CHUNK))
        le, ln = rows[4:5], rows[5:6]
        along = le * (rows[0:1] - origin[0]) + ln * (rows[1:2] - origin[1])
        row = lax.broadcasted_iota(jnp.int32, (8, CHUNK), 0)
        factors = jnp.where(
            row == 0, along, jnp.where(row == 1, le, jnp.where(row == 2, ln, rows[6:7]))
        )
        parts = kernel_split(factors)
        low = row < 4
        tiles = []
        for first_part, second_part in zip(CROSS[::2], CROSS[1::2]):
            upper = jnp.concatenate([parts[second_part[0]][:4]] * 2, axis=0)
            tiles.append(jnp.where(low, parts[first_part[0]], upper))
        tiles.append(jnp.zeros((8, CHUNK), jnp.float32))
        sights[lane][...] = jnp.concatenate(tiles, axis=0).T.astype(jnp.bfloat16)

    def make_strips(near, k, begin, end, lane, green):
        patch = [
            jnp.broadcast_to(patches[near[k], r : r + 1], (8, PBLK)) for r in range(3)
        ]
        alongs = jnp.dot(
            sights[lane][begin:end], forms[near[k]], preferred_element_type=jnp.float32
        )
        for low in range(begin, end, 16):
            along = alongs[low - begin : low - begin + 16]
            inverses = []
            for at in (low, low + 8):
                east, north = (
                    jnp.concatenate([wide[lane][i, at : at + 8]] * (PBLK // CHUNK), axis=1)
                    for i in range(2)
                )
                dx = east - patch[0]
                dy = north - patch[1]
                inverses.append(lax.rsqrt(dx * dx + dy * dy + patch[2]))
            inverse = jnp.concatenate(inverses, axis=0)
            green[low : low + 16, k * PBLK : (k + 1) * PBLK] = (
                along * inverse * inverse * inverse
            ).astype(jnp.bfloat16)

    def make_hats(rows, hats):
        node = lax.broadcasted_iota(jnp.int32, (SG, CHUNK), 0).astype(jnp.float32)
        across = jnp.maximum(0.0, 1.0 - jnp.abs(rows[2:3] - node))
        upward = jnp.maximum(0.0, 1.0 - jnp.abs(rows[3:4] - node))
        for a in range(SG):
            hats[a * SG : (a + 1) * SG] = (across[a : a + 1] * upward).astype(jnp.bfloat16)

    def make_head(i, lane, buffers):
        slot, near = item_of(i)
        rows = pix[slot]
        make_hats(rows, buffers[1])
        spread(rows, lane)
        return near

    def predict(i, buffers):
        green, hats = buffers[:2]
        slot, near = item_of(i)
        model = jnp.dot(
            screens[info_of(slot, 2)], hats[...], preferred_element_type=jnp.float32
        )
        for k in range(NEAR):
            model += lax.dot_general(
                stress[pl.ds(pl.multiple_of(spots[near[k]], 16), epochs), :],
                green[:, k * PBLK : (k + 1) * PBLK],
                (((1,), (1,)), ((), ())),
                preferred_element_type=jnp.float32,
            )
        return model

    def weigh(i, model, buffers):
        slot, _ = item_of(i)
        live = jnp.where(i < total, info_of(slot, 0), 0)
        lane = lax.broadcasted_iota(jnp.int32, (1, CHUNK), 1)
        scale = jnp.where(lane < live, pix[slot, 7:8, :], 0.0)
        buffers[2][...] = ((model - obs[slot].astype(jnp.float32)) * scale).astype(jnp.bfloat16)

    def add_patch(near, k, buffers):
        grad[places[near[k]]] += jnp.dot(
            buffers[2][...],
            buffers[0][:, k * PBLK : (k + 1) * PBLK],
            preferred_element_type=jnp.float32,
        )

    def add_screen(slot, buffers):
        screen_grad[info_of(slot, 2)] += lax.dot_general(
            buffers[2][...],
            buffers[1][...],
            (((1,), (1,)), ((), ())),
            preferred_element_type=jnp.float32,
        )

    lanes = range(PAIR)
    half = CHUNK // 2

    def make_pair(j, buffers):
        for lane in lanes:
            near = make_head(PAIR * j + lane, lane, buffers[lane])
            for k in range(NEAR):
                for low in (0, half):
                    make_strips(near, k, low, low + half, lane, buffers[lane][0])

    def model_pair(j, buffers):
        for lane in lanes:
            model = predict(PAIR * j + lane, buffers[lane])
            weigh(PAIR * j + lane, model, buffers[lane])

    def turn(j, using, middle, making):
        now = [item_of(PAIR * j + lane) for lane in lanes]
        coming = [PAIR * (j + 1) + lane for lane in lanes]
        near = [
            make_head(PAIR * (j + 2) + lane, lane, making[lane]) for lane in lanes
        ]
        models = [predict(coming[lane], middle[lane]) for lane in lanes]

        def strips(k, lane):
            for low in (0, half):
                make_strips(near[lane], k, low, low + half, lane, making[lane][0])

        def adds(k):
            for lane in lanes:
                add_patch(now[lane][1], k, using[lane])

        strips(0, 0)
        adds(0)
        strips(0, 1)
        adds(1)
        strips(1, 0)
        for lane in lanes:
            weigh(coming[lane], models[lane], middle[lane])
        strips(1, 1)
        adds(2)
        strips(2, 0)
        for lane in lanes:
            add_screen(now[lane][0], using[lane])
        strips(2, 1)

    @pl.when(total > 0)
    def _():
        pairs = lax.div(total + PAIR - 1, PAIR)
        make_pair(0, sets[0])
        make_pair(1, sets[1])
        model_pair(0, sets[0])

        def step(i, _):
            for at in range(3):
                j = 3 * i + at

                @pl.when(j < pairs)
                def _():
                    turn(j, sets[at], sets[(at + 1) % 3], sets[(at + 2) % 3])

            return 0

        lax.fori_loop(0, lax.div(pairs + 2, 3), step, 0)

    if final:
        half = grad.shape[0] // 2
        outs[0][...] = grad[half:].astype(outs[0].dtype)
        for i, out in enumerate(outs[1:]):
            low = (PAIR + i) * local_tiles
            out[...] = screen_grad[low : low + local_tiles].astype(out.dtype)


def fit(tables, groups, patches, forms, screens, stress, state, first, final):
    layers = len(groups[0][1])
    slots = tables[0].shape[0] // (3 * layers)
    smem = pl.BlockSpec(memory_space=pltpu.SMEM)
    vmem = pl.BlockSpec(memory_space=pltpu.VMEM)
    hbm = pl.BlockSpec(memory_space=pl.ANY)
    spans = tuple((base, low, obs[0].shape[0]) for base, obs, _, low in groups)
    arrays = [a for _, obs, pix, _ in groups for a in (*obs, *pix)]
    span = sum(size for _, _, size in spans)
    blocks, epochs = state[0].shape[0], state[0].shape[1]
    out_shape = [jax.ShapeDtypeStruct(a.shape, a.dtype) for a in state]
    if first:
        state = ()
        for parts in (screens, stress):
            shape = (LAYER * parts[0].shape[0],) + parts[0].shape[1:]
            out_shape.append(jax.ShapeDtypeStruct(shape, parts[0].dtype))
    else:
        screens, stress = [screens], [stress]
    if final:
        out_shape.append(jax.ShapeDtypeStruct((blocks // 2, epochs, PBLK), jnp.bfloat16))
        shape = (state[1].shape[0] // LAYER,) + state[1].shape[1:]
        out_shape += [jax.ShapeDtypeStruct(shape, jnp.bfloat16)] * 2
    before = len(tables) + len(arrays) + 2 + len(screens) + len(stress)
    return pl.pallas_call(
        functools.partial(fit_kernel, first, final, layers, slots, spans),
        in_specs=[smem] * len(tables)
        + [hbm] * len(arrays)
        + [vmem] * 2
        + [hbm if first else vmem] * (len(screens) + len(stress))
        + [vmem] * len(state),
        out_specs=[vmem] * len(out_shape),
        out_shape=out_shape,
        scratch_shapes=[
            pltpu.VMEM((layers * span, epochs, CHUNK), arrays[0].dtype),
            pltpu.VMEM((layers * span, 8, CHUNK), jnp.float32),
        ]
        + [
            pltpu.VMEM((CHUNK, NEAR * PBLK), jnp.bfloat16),
            pltpu.VMEM((SG * SG, CHUNK), jnp.bfloat16),
            pltpu.VMEM((epochs, CHUNK), jnp.bfloat16),
        ]
        * (3 * PAIR)
        + [pltpu.VMEM((2, CHUNK, CHUNK), jnp.float32)] * PAIR
        + [pltpu.VMEM((CHUNK, TERMS), jnp.bfloat16)] * PAIR
        + [
            pltpu.SMEM((layers * span + 1,), jnp.int32),
            pltpu.SemaphoreType.DMA((2 * layers * len(groups) + 2 * LAYER,)),
        ],
        input_output_aliases={} if first else {before: 0, before + 1: 1},
        compiler_params=pltpu.CompilerParams(vmem_limit_bytes=8 * MIB),
        cost_estimate=pl.CostEstimate(
            flops=layers * span * 4 * epochs * CHUNK * (NEAR + 1) * PBLK,
            bytes_accessed=20 * MIB,
            transcendentals=layers * span * CHUNK * NEAR * PBLK,
        ),
        name="fit",
    )(*tables, *arrays, patches, forms, *screens, *stress, *state)


def partner(values, devices, distance):
    return lax.ppermute(values, "tile", [(i, i ^ distance) for i in range(devices)])


def orders(devices):
    stages = devices.bit_length() - 1
    high = list(range(stages - 1, 1, -1))
    return [1] + high, high + [1]


def block_places(devices, here, blocks, local, epochs):
    block = jnp.arange(blocks)
    other = (block // local) ^ here
    seat = block % local
    half = local // 2
    turned = []
    for order in orders(devices):
        spot = 0
        for bit in order:
            spot = spot * 2 + ((other >> bit) & 1)
        turned.append(spot)
    chips = devices // 2
    upper = seat // half
    spot = jnp.where(upper == 0, turned[0], turned[1])
    place = (((other & 1) * 2 + upper) * chips + spot) * half + seat % half
    stages = devices.bit_length() - 1
    held = sum(((other >> (stages - 1 - s)) & 1) << s for s in range(stages))
    return place.astype(jnp.int32), ((held * local + seat) * epochs).astype(jnp.int32)


def halve(kept, given, there, devices):
    total = kept + partner(given, devices, 1).astype(jnp.float32)
    middle = total.shape[0] // 2
    parts = [total[:middle], total[middle:]]
    both = orders(devices)
    stages = len(both[0])
    back = partner(there, devices, PAIR)
    for stage in range(stages):
        got = []
        for side in range(2):
            given = parts[side][parts[side].shape[0] // 2 :]
            if stages - stage <= NARROW:
                given = given.astype(jnp.bfloat16)
            got.append(partner(given, devices, 1 << both[side][stage]))
        for side in range(2):
            if side:
                parts[0], got[1] = lax.optimization_barrier((parts[0], got[1]))
            size = parts[side].shape[0] // 2
            parts[side] = parts[side][:size] + got[side].astype(jnp.float32)
    return jnp.concatenate(parts, axis=0), back


def on_device(
    observations,
    pixel_geometry,
    block_counts,
    block_tiles,
    cutoff_lists,
    patch_geometry,
    stress,
    screens,
):
    devices = lax.axis_size("tile")
    here = lax.axis_index("tile")
    blocks, epochs, width = observations.shape
    local_tiles = screens.shape[0]
    layers = devices // LAYER
    local = stress.shape[1] // PBLK

    slots = LAYER * (2 * blocks // devices) * (width // CHUNK)
    sizes = round_sizes(slots)

    held = jnp.swapaxes(stress.reshape(epochs, local, PBLK), 0, 1).reshape(-1, PBLK)
    other = partner(held, devices, devices // 2)
    across_screens = partner(screens, devices, PAIR)
    obs, pix = pack(
        observations,
        pixel_geometry,
        block_counts,
        block_tiles,
        jnp.reshape(here, (1,)).astype(jnp.int32),
        devices,
        local_tiles,
    )

    def exchange(parts):
        return [parts[0]] + [partner(parts[x], devices, x * LAYER) for x in range(1, layers)]

    other, pix = lax.optimization_barrier((other, pix))
    pix = exchange(pix)
    distance = devices // 2
    while distance >= LAYER:
        if distance < devices // 2:
            other = partner(held, devices, distance)
        held = jnp.concatenate([held, other], axis=0)
        distance //= 2
    held, pix, across_screens = lax.optimization_barrier((held, pix, across_screens))
    got = [exchange(o) for o in obs]
    across = partner(held, devices, PAIR)
    across, got[0][1] = lax.optimization_barrier((across, got[0][1]))
    all_stress = [held, across, partner(held, devices, 1), partner(across, devices, 1)]
    all_screens = [
        screens,
        across_screens,
        partner(screens, devices, 1),
        partner(across_screens, devices, 1),
    ]

    patch_blocks = devices * local
    east, north, depth, compliance = patch_geometry
    origin = patch_geometry[:2, 0]
    strength = compliance * depth * depth
    faces = split(
        jnp.stack(
            [
                strength,
                -strength * (east - origin[0]),
                -strength * (north - origin[1]),
                strength * depth,
            ]
        )
    )
    forms = jnp.concatenate(
        [faces[second] for _, second in CROSS] + [jnp.zeros((8,) + east.shape, jnp.float32)]
    ).astype(jnp.bfloat16)
    forms = jnp.swapaxes(forms.reshape(TERMS, patch_blocks, PBLK), 0, 1)
    patches = jnp.stack([east, north, depth * depth])
    patches = jnp.swapaxes(patches.reshape(3, patch_blocks, PBLK), 0, 1)
    places, spots = block_places(devices, here, patch_blocks, local, epochs)
    info = jnp.stack([p[slots, :3, :slots] for p in pix]).astype(jnp.int32).reshape(-1)
    tables = (info, cutoff_lists.reshape(-1), places, spots, origin)

    state = (
        jax.ShapeDtypeStruct((patch_blocks, epochs, PBLK), jnp.float32),
        jax.ShapeDtypeStruct((LAYER * local_tiles,) + screens.shape[1:], jnp.float32),
    )
    base = 0
    for i, size in enumerate(sizes):
        first, final = i == 0, i == len(sizes) - 1
        groups = [(base, got[i], pix, base)]
        state = fit(
            tables,
            groups,
            patches,
            forms,
            all_screens,
            all_stress,
            state[:2],
            first,
            final,
        )
        if first:
            all_screens, all_stress = state[2:]
        base += size
    grad, screen_grad, given, next_door, diagonal = state
    own, far = screen_grad[:local_tiles], screen_grad[local_tiles : PAIR * local_tiles]
    there = (far + partner(diagonal, devices, 1).astype(jnp.float32)).astype(jnp.bfloat16)
    grad, back = halve(grad[: grad.shape[0] // 2], given, there, devices)
    screen_gradient = (
        own + partner(next_door, devices, 1).astype(jnp.float32) + back.astype(jnp.float32)
    )
    return (jnp.swapaxes(grad, 0, 1).reshape(epochs, local * PBLK), screen_gradient)


def solution(mesh):
    return jax.shard_map(
        on_device,
        mesh=mesh,
        in_specs=(
            P(("groups", "tile"), None, None),
            P(("groups", "tile"), None, None),
            P(("groups", "tile")),
            P(("groups", "tile")),
            P(),
            P(),
            P(None, ("groups", "tile")),
            P(("groups", "tile"), None, None),
        ),
        out_specs=(P(None, ("groups", "tile")), P(("groups", "tile"), None, None)),
        check_vma=False,
    )
```

```python
import functools

import jax
import jax.numpy as jnp
from jax import lax
from jax.experimental import pallas as pl
from jax.experimental.pallas import tpu as pltpu
from jax.sharding import PartitionSpec as P

PBLK = 256
NEAR = 3
SG = 16
CHUNK = 128
LAYER = 4
PAIR = 2
NARROW = 3
ROUNDS = (6, 6, 4)
MIB = 1 << 20
TERMS = 32
CROSS = ((0, 0), (0, 1), (1, 0), (0, 2), (1, 1), (2, 0))


def round_sizes(slots):
    return [slots * r // sum(ROUNDS) for r in ROUNDS]


def pack_kernel(local_tiles, layers, slots, here, tiles, counts, obs_in, pix_in, *rest):
    sizes = round_sizes(slots)
    total = len(sizes)
    obs_out, pix_out = rest[: total * layers], rest[total * layers : (total + 1) * layers]
    obs, pix, obs_all, pix_all, fill, sems = rest[(total + 1) * layers :]
    loads = [
        pltpu.make_async_copy(obs_in, obs, sems.at[0]),
        pltpu.make_async_copy(pix_in, pix, sems.at[1]),
    ]
    for copy in loads:
        copy.start()
    my_layer, my_seat = lax.div(here[0], LAYER), lax.rem(here[0], LAYER)
    chunks = pix.shape[2] // CHUNK
    stride = slots + 1
    for x in range(layers):
        fill[x] = 0
    lane = lax.broadcasted_iota(jnp.int32, (8, CHUNK), 1)
    row = lax.broadcasted_iota(jnp.int32, (8, CHUNK), 0)
    for copy in loads:
        copy.wait()

    def put(b, infos):
        tile = tiles[b]
        count = counts[b]
        owner = lax.div(tile, local_tiles)
        x = lax.div(owner, LAYER) ^ my_layer
        seat = lax.rem(owner, LAYER) ^ my_seat
        spot = lax.rem(seat, PAIR) * PAIR + lax.div(seat, PAIR)
        screen = spot * local_tiles + lax.rem(tile, local_tiles)
        slot = fill[x]
        fill[x] = slot + lax.div(count + CHUNK - 1, CHUNK)
        for c in range(chunks):
            at = slot + c
            live = jnp.clip(count - c * CHUNK, 0, CHUNK)
            obs_all[x * stride + at] = obs[b, :, c * CHUNK : (c + 1) * CHUNK]
            pix_all[x * stride + at] = pix[b, :, c * CHUNK : (c + 1) * CHUNK]
            entry = jnp.where(row == 0, live, jnp.where(row == 1, tile, screen))
            here_only = (lane == at) & (row < 3)
            infos = tuple(
                jnp.where(here_only & (x == i), entry, info) for i, info in enumerate(infos)
            )
        return infos

    infos = lax.fori_loop(
        0, obs.shape[0], put, tuple(jnp.zeros((8, CHUNK), jnp.int32) for _ in range(layers))
    )
    copies = []
    for x in range(layers):
        at = x * stride
        pix_all[at + slots] = infos[x].astype(jnp.float32)
        copies.append((pix_all.at[pl.ds(at, stride)], pix_out[x]))
        for i, size in enumerate(sizes):
            copies.append((obs_all.at[pl.ds(at, size)], obs_out[i * layers + x]))
            at += size
    copies = [pltpu.make_async_copy(a, b, sems.at[i]) for i, (a, b) in enumerate(copies)]
    for copy in copies:
        copy.start()
    for copy in copies:
        copy.wait()


def pack(observations, pixel_geometry, block_counts, block_tiles, here, devices, local_tiles):
    blocks, epochs, width = observations.shape
    layers = devices // LAYER
    slots = LAYER * (2 * blocks // devices) * (width // CHUNK)
    sizes = round_sizes(slots)
    smem = pl.BlockSpec(memory_space=pltpu.SMEM)
    hbm = pl.BlockSpec(memory_space=pl.ANY)
    pix_part = jax.ShapeDtypeStruct((slots + 1, 8, CHUNK), jnp.float32)
    out = pl.pallas_call(
        functools.partial(pack_kernel, local_tiles, layers, slots),
        in_specs=[smem, smem, smem, hbm, hbm],
        out_specs=[hbm] * ((len(sizes) + 1) * layers),
        out_shape=[
            jax.ShapeDtypeStruct((size, epochs, CHUNK), observations.dtype)
            for size in sizes
            for _ in range(layers)
        ]
        + [pix_part] * layers,
        scratch_shapes=[
            pltpu.VMEM(observations.shape, observations.dtype),
            pltpu.VMEM(pixel_geometry.shape, jnp.float32),
            pltpu.VMEM((layers * (slots + 1), epochs, CHUNK), observations.dtype),
            pltpu.VMEM((layers * (slots + 1), 8, CHUNK), jnp.float32),
            pltpu.SMEM((layers,), jnp.int32),
            pltpu.SemaphoreType.DMA(((len(sizes) + 1) * layers,)),
        ],
        compiler_params=pltpu.CompilerParams(vmem_limit_bytes=10 * MIB),
        name="pack",
    )(here, block_tiles, block_counts, observations, pixel_geometry)
    rounds = len(sizes)
    return [out[i * layers : (i + 1) * layers] for i in range(rounds)], out[rounds * layers :]


def split(values):
    parts = []
    for _ in range(3):
        part = lax.reduce_precision(values, 8, 7)
        parts.append(part)
        values = values - part
    return parts


def kernel_split(values):
    parts = []
    for _ in range(3):
        part = values.astype(jnp.bfloat16).astype(jnp.float32)
        parts.append(part)
        values = values - part
    return parts


def fit_kernel(first, final, layers, slots, groups, *refs):
    info, cutoffs, places, spots, origin = refs[:5]
    rest = refs[5:]
    obs_in, pix_in = [], []
    for _ in groups:
        obs_in.append(rest[:layers])
        pix_in.append(rest[layers : 2 * layers])
        rest = rest[2 * layers :]
    patches, forms = rest[:2]
    rest = rest[1:]
    if first:
        screen_parts, stress_parts = rest[1 : 1 + PAIR], rest[1 + PAIR : 1 + 2 * PAIR]
        rest = rest[1 + 2 * PAIR :]
        grad, screen_grad, screens, stress = rest[:4]
        rest = rest[4:]
    else:
        screens, stress = rest[1:3]
        grad, screen_grad = rest[5:7]
        rest = rest[7:]
    outs = rest[:3] if final else ()
    rest = rest[len(outs) :]
    obs, pix = rest[:2]
    buffers = rest[2 : 2 + 9 * PAIR]
    wide, sights = rest[2 + 9 * PAIR : 2 + 10 * PAIR], rest[2 + 10 * PAIR : 2 + 11 * PAIR]
    items, sems = rest[2 + 11 * PAIR :]
    sets = [
        [buffers[3 * (PAIR * i + lane) : 3 * (PAIR * i + lane) + 3] for lane in range(PAIR)]
        for i in range(3)
    ]
    epochs = obs.shape[1]
    base = groups[0][0]
    span = sum(size for _, _, size in groups)
    local_tiles = screens.shape[0] // LAYER

    loads = []
    for x in range(layers):
        at = x * span
        for g, (_, low, size) in enumerate(groups):
            loads.append((obs_in[g][x], obs.at[pl.ds(at, size)]))
            loads.append((pix_in[g][x].at[pl.ds(low, size)], pix.at[pl.ds(at, size)]))
            at += size
    if first:
        for parts, whole in ((screen_parts, screens), (stress_parts, stress)):
            size = whole.shape[0] // PAIR
            for i, part in enumerate(parts):
                loads.append((part, whole.at[pl.ds(i * size, size)]))
    loads = [pltpu.make_async_copy(a, b, sems.at[i]) for i, (a, b) in enumerate(loads)]
    for copy in loads:
        copy.start()
    if first:
        grad[...] = jnp.zeros_like(grad)
        screen_grad[...] = jnp.zeros_like(screen_grad)

    def info_of(slot, kind):
        x = lax.div(slot, span)
        return info[(x * 3 + kind) * slots + base + lax.rem(slot, span)]

    def list_slot(slot, total):
        items[total] = slot
        return total + jnp.where(info_of(slot, 0) > 0, 1, 0)

    total = lax.fori_loop(0, layers * span, list_slot, 0)
    for copy in loads:
        copy.wait()

    def item_of(i):
        slot = items[jnp.minimum(i, total - 1)]
        tile = info_of(slot, 1)
        return slot, [cutoffs[tile * NEAR + k] for k in range(NEAR)]

    def spread(rows, lane):
        columns = rows.T
        for i in range(2):
            wide[lane][i] = jnp.broadcast_to(columns[:, i : i + 1], (CHUNK, CHUNK))
        le, ln = rows[4:5], rows[5:6]
        along = le * (rows[0:1] - origin[0]) + ln * (rows[1:2] - origin[1])
        row = lax.broadcasted_iota(jnp.int32, (8, CHUNK), 0)
        factors = jnp.where(
            row == 0, along, jnp.where(row == 1, le, jnp.where(row == 2, ln, rows[6:7]))
        )
        parts = kernel_split(factors)
        low = row < 4
        tiles = []
        for first_part, second_part in zip(CROSS[::2], CROSS[1::2]):
            upper = jnp.concatenate([parts[second_part[0]][:4]] * 2, axis=0)
            tiles.append(jnp.where(low, parts[first_part[0]], upper))
        tiles.append(jnp.zeros((8, CHUNK), jnp.float32))
        sights[lane][...] = jnp.concatenate(tiles, axis=0).T.astype(jnp.bfloat16)

    def make_strips(near, k, begin, end, lane, green):
        patch = [
            jnp.broadcast_to(patches[near[k], r : r + 1], (8, PBLK)) for r in range(3)
        ]
        alongs = jnp.dot(
            sights[lane][begin:end], forms[near[k]], preferred_element_type=jnp.float32
        )
        for low in range(begin, end, 16):
            along = alongs[low - begin : low - begin + 16]
            inverses = []
            for at in (low, low + 8):
                east, north = (
                    jnp.concatenate([wide[lane][i, at : at + 8]] * (PBLK // CHUNK), axis=1)
                    for i in range(2)
                )
                dx = east - patch[0]
                dy = north - patch[1]
                inverses.append(lax.rsqrt(dx * dx + dy * dy + patch[2]))
            inverse = jnp.concatenate(inverses, axis=0)
            green[low : low + 16, k * PBLK : (k + 1) * PBLK] = (
                along * inverse * inverse * inverse
            ).astype(jnp.bfloat16)

    def make_hats(rows, hats):
        node = lax.broadcasted_iota(jnp.int32, (SG, CHUNK), 0).astype(jnp.float32)
        across = jnp.maximum(0.0, 1.0 - jnp.abs(rows[2:3] - node))
        upward = jnp.maximum(0.0, 1.0 - jnp.abs(rows[3:4] - node))
        for a in range(SG):
            hats[a * SG : (a + 1) * SG] = (across[a : a + 1] * upward).astype(jnp.bfloat16)

    def make_head(i, lane, buffers):
        slot, near = item_of(i)
        rows = pix[slot]
        make_hats(rows, buffers[1])
        spread(rows, lane)
        return near

    def predict(i, buffers):
        green, hats = buffers[:2]
        slot, near = item_of(i)
        model = jnp.dot(
            screens[info_of(slot, 2)], hats[...], preferred_element_type=jnp.float32
        )
        for k in range(NEAR):
            model += lax.dot_general(
                stress[pl.ds(pl.multiple_of(spots[near[k]], 16), epochs), :],
                green[:, k * PBLK : (k + 1) * PBLK],
                (((1,), (1,)), ((), ())),
                preferred_element_type=jnp.float32,
            )
        return model

    def weigh(i, model, buffers):
        slot, _ = item_of(i)
        live = jnp.where(i < total, info_of(slot, 0), 0)
        lane = lax.broadcasted_iota(jnp.int32, (1, CHUNK), 1)
        scale = jnp.where(lane < live, pix[slot, 7:8, :], 0.0)
        buffers[2][...] = ((model - obs[slot].astype(jnp.float32)) * scale).astype(jnp.bfloat16)

    def add_patch(near, k, buffers):
        grad[places[near[k]]] += jnp.dot(
            buffers[2][...],
            buffers[0][:, k * PBLK : (k + 1) * PBLK],
            preferred_element_type=jnp.float32,
        )

    def add_screen(slot, buffers):
        screen_grad[info_of(slot, 2)] += lax.dot_general(
            buffers[2][...],
            buffers[1][...],
            (((1,), (1,)), ((), ())),
            preferred_element_type=jnp.float32,
        )

    lanes = range(PAIR)
    half = CHUNK // 2

    def make_pair(j, buffers):
        for lane in lanes:
            near = make_head(PAIR * j + lane, lane, buffers[lane])
            for k in range(NEAR):
                for low in (0, half):
                    make_strips(near, k, low, low + half, lane, buffers[lane][0])

    def model_pair(j, buffers):
        for lane in lanes:
            model = predict(PAIR * j + lane, buffers[lane])
            weigh(PAIR * j + lane, model, buffers[lane])

    def turn(j, using, middle, making):
        now = [item_of(PAIR * j + lane) for lane in lanes]
        coming = [PAIR * (j + 1) + lane for lane in lanes]
        near = [
            make_head(PAIR * (j + 2) + lane, lane, making[lane]) for lane in lanes
        ]
        models = [predict(coming[lane], middle[lane]) for lane in lanes]

        def strips(k, lane):
            for low in (0, half):
                make_strips(near[lane], k, low, low + half, lane, making[lane][0])

        def adds(k):
            for lane in lanes:
                add_patch(now[lane][1], k, using[lane])

        strips(0, 0)
        adds(0)
        strips(0, 1)
        adds(1)
        strips(1, 0)
        for lane in lanes:
            weigh(coming[lane], models[lane], middle[lane])
        strips(1, 1)
        adds(2)
        strips(2, 0)
        for lane in lanes:
            add_screen(now[lane][0], using[lane])
        strips(2, 1)

    @pl.when(total > 0)
    def _():
        pairs = lax.div(total + PAIR - 1, PAIR)
        make_pair(0, sets[0])
        make_pair(1, sets[1])
        model_pair(0, sets[0])

        def step(i, _):
            for at in range(3):
                j = 3 * i + at

                @pl.when(j < pairs)
                def _():
                    turn(j, sets[at], sets[(at + 1) % 3], sets[(at + 2) % 3])

            return 0

        lax.fori_loop(0, lax.div(pairs + 2, 3), step, 0)

    if final:
        half = grad.shape[0] // 2
        outs[0][...] = grad[half:].astype(outs[0].dtype)
        for i, out in enumerate(outs[1:]):
            low = (PAIR + i) * local_tiles
            out[...] = screen_grad[low : low + local_tiles].astype(out.dtype)


def fit(tables, groups, patches, forms, screens, stress, state, first, final):
    layers = len(groups[0][1])
    slots = tables[0].shape[0] // (3 * layers)
    smem = pl.BlockSpec(memory_space=pltpu.SMEM)
    vmem = pl.BlockSpec(memory_space=pltpu.VMEM)
    hbm = pl.BlockSpec(memory_space=pl.ANY)
    spans = tuple((base, low, obs[0].shape[0]) for base, obs, _, low in groups)
    arrays = [a for _, obs, pix, _ in groups for a in (*obs, *pix)]
    span = sum(size for _, _, size in spans)
    blocks, epochs = state[0].shape[0], state[0].shape[1]
    out_shape = [jax.ShapeDtypeStruct(a.shape, a.dtype) for a in state]
    if first:
        state = ()
        for parts in (screens, stress):
            shape = (PAIR * parts[0].shape[0],) + parts[0].shape[1:]
            out_shape.append(jax.ShapeDtypeStruct(shape, parts[0].dtype))
    else:
        screens, stress = [screens], [stress]
    if final:
        out_shape.append(jax.ShapeDtypeStruct((blocks // 2, epochs, PBLK), jnp.bfloat16))
        shape = (state[1].shape[0] // LAYER,) + state[1].shape[1:]
        out_shape += [jax.ShapeDtypeStruct(shape, jnp.bfloat16)] * 2
    before = len(tables) + len(arrays) + 2 + len(screens) + len(stress)
    return pl.pallas_call(
        functools.partial(fit_kernel, first, final, layers, slots, spans),
        in_specs=[smem] * len(tables)
        + [hbm] * len(arrays)
        + [vmem] * 2
        + [hbm if first else vmem] * (len(screens) + len(stress))
        + [vmem] * len(state),
        out_specs=[vmem] * len(out_shape),
        out_shape=out_shape,
        scratch_shapes=[
            pltpu.VMEM((layers * span, epochs, CHUNK), arrays[0].dtype),
            pltpu.VMEM((layers * span, 8, CHUNK), jnp.float32),
        ]
        + [
            pltpu.VMEM((CHUNK, NEAR * PBLK), jnp.bfloat16),
            pltpu.VMEM((SG * SG, CHUNK), jnp.bfloat16),
            pltpu.VMEM((epochs, CHUNK), jnp.bfloat16),
        ]
        * (3 * PAIR)
        + [pltpu.VMEM((2, CHUNK, CHUNK), jnp.float32)] * PAIR
        + [pltpu.VMEM((CHUNK, TERMS), jnp.bfloat16)] * PAIR
        + [
            pltpu.SMEM((layers * span + 1,), jnp.int32),
            pltpu.SemaphoreType.DMA((2 * layers * len(groups) + 2 * LAYER,)),
        ],
        input_output_aliases={} if first else {before: 0, before + 1: 1},
        compiler_params=pltpu.CompilerParams(vmem_limit_bytes=8 * MIB),
        cost_estimate=pl.CostEstimate(
            flops=layers * span * 4 * epochs * CHUNK * (NEAR + 1) * PBLK,
            bytes_accessed=1024,
            transcendentals=layers * span * CHUNK * NEAR * PBLK,
        ),
        name="fit",
    )(*tables, *arrays, patches, forms, *screens, *stress, *state)


def partner(values, devices, distance):
    return lax.ppermute(values, "tile", [(i, i ^ distance) for i in range(devices)])


def orders(devices):
    stages = devices.bit_length() - 1
    high = list(range(2, stages))
    return [1] + high, high + [1]


def block_places(devices, here, blocks, local, epochs):
    block = jnp.arange(blocks)
    other = (block // local) ^ here
    seat = block % local
    half = local // 2
    turned = []
    for order in orders(devices):
        spot = 0
        for bit in order:
            spot = spot * 2 + ((other >> bit) & 1)
        turned.append(spot)
    chips = devices // 2
    upper = seat // half
    spot = jnp.where(upper == 0, turned[0], turned[1])
    place = (((other & 1) * 2 + upper) * chips + spot) * half + seat % half
    stages = devices.bit_length() - 1
    held = sum(((other >> (stages - 1 - s)) & 1) << s for s in range(stages))
    return place.astype(jnp.int32), ((held * local + seat) * epochs).astype(jnp.int32)


def halve(kept, given, there, devices):
    total = kept + partner(given, devices, 1).astype(jnp.float32)
    middle = total.shape[0] // 2
    parts = [total[:middle], total[middle:]]
    both = orders(devices)
    stages = len(both[0])
    back = None
    for stage in range(stages):
        got = []
        for side in range(2):
            given = parts[side][parts[side].shape[0] // 2 :]
            if stages - stage <= NARROW:
                given = given.astype(jnp.bfloat16)
            got.append(partner(given, devices, 1 << both[side][stage]))
        for side in range(2):
            if side:
                _, got[1] = lax.optimization_barrier((parts[0], got[1]))
            size = parts[side].shape[0] // 2
            parts[side] = parts[side][:size] + got[side].astype(jnp.float32)
            if back is None:
                _, there = lax.optimization_barrier((parts[0], there))
                back = partner(there, devices, PAIR)
    return jnp.concatenate(parts, axis=0), back


def on_device(
    observations,
    pixel_geometry,
    block_counts,
    block_tiles,
    cutoff_lists,
    patch_geometry,
    stress,
    screens,
):
    devices = lax.axis_size("tile")
    here = lax.axis_index("tile")
    blocks, epochs, width = observations.shape
    local_tiles = screens.shape[0]
    layers = devices // LAYER
    local = stress.shape[1] // PBLK

    slots = LAYER * (2 * blocks // devices) * (width // CHUNK)
    sizes = round_sizes(slots)

    held = jnp.swapaxes(stress.reshape(epochs, local, PBLK), 0, 1).reshape(-1, PBLK)
    other = partner(held, devices, devices // 2)
    across_screens = partner(screens, devices, PAIR)
    obs, pix = pack(
        observations,
        pixel_geometry,
        block_counts,
        block_tiles,
        jnp.reshape(here, (1,)).astype(jnp.int32),
        devices,
        local_tiles,
    )

    def exchange(parts):
        got = [partner(parts[x], devices, x * LAYER) for x in range(layers - 1, 0, -1)]
        return [parts[0]] + got[::-1]

    other, pix = lax.optimization_barrier((other, pix))
    pix = exchange(pix)
    distance = devices // 2
    while distance >= LAYER:
        if distance < devices // 2:
            other = partner(held, devices, distance)
        held = jnp.concatenate([held, other], axis=0)
        distance //= 2
    held, pix, across_screens = lax.optimization_barrier((held, pix, across_screens))
    got = [exchange(o) for o in obs]
    across = partner(held, devices, PAIR)
    across, got[0][1] = lax.optimization_barrier((across, got[0][1]))
    held = jnp.concatenate([held, across], axis=0)
    all_stress = [held, partner(held, devices, 1)]
    near_screens = jnp.concatenate([screens, across_screens], axis=0)
    all_screens = [near_screens, partner(near_screens, devices, 1)]

    patch_blocks = devices * local
    east, north, depth, compliance = patch_geometry
    origin = patch_geometry[:2, 0]
    strength = compliance * depth * depth
    faces = split(
        jnp.stack(
            [
                strength,
                -strength * (east - origin[0]),
                -strength * (north - origin[1]),
                strength * depth,
            ]
        )
    )
    forms = jnp.concatenate(
        [faces[second] for _, second in CROSS] + [jnp.zeros((8,) + east.shape, jnp.float32)]
    ).astype(jnp.bfloat16)
    forms = jnp.swapaxes(forms.reshape(TERMS, patch_blocks, PBLK), 0, 1)
    patches = jnp.stack([east, north, depth * depth])
    patches = jnp.swapaxes(patches.reshape(3, patch_blocks, PBLK), 0, 1)
    places, spots = block_places(devices, here, patch_blocks, local, epochs)
    info = jnp.stack([p[slots, :3, :slots] for p in pix]).astype(jnp.int32).reshape(-1)
    tables = (info, cutoff_lists.reshape(-1), places, spots, origin)

    state = (
        jax.ShapeDtypeStruct((patch_blocks, epochs, PBLK), jnp.float32),
        jax.ShapeDtypeStruct((LAYER * local_tiles,) + screens.shape[1:], jnp.float32),
    )
    base = 0
    for i, size in enumerate(sizes):
        first, final = i == 0, i == len(sizes) - 1
        groups = [(base, got[i], pix, base)]
        state = fit(
            tables,
            groups,
            patches,
            forms,
            all_screens,
            all_stress,
            state[:2],
            first,
            final,
        )
        if first:
            all_screens, all_stress = state[2:]
        base += size
    grad, screen_grad, given, next_door, diagonal = state
    own, far = screen_grad[:local_tiles], screen_grad[local_tiles : PAIR * local_tiles]
    there = (far + partner(diagonal, devices, 1).astype(jnp.float32)).astype(jnp.bfloat16)
    grad, back = halve(grad[: grad.shape[0] // 2], given, there, devices)
    screen_gradient = (
        own + partner(next_door, devices, 1).astype(jnp.float32) + back.astype(jnp.float32)
    )
    return (jnp.swapaxes(grad, 0, 1).reshape(epochs, local * PBLK), screen_gradient)


def solution(mesh):
    return jax.shard_map(
        on_device,
        mesh=mesh,
        in_specs=(
            P(("groups", "tile"), None, None),
            P(("groups", "tile"), None, None),
            P(("groups", "tile")),
            P(("groups", "tile")),
            P(),
            P(),
            P(None, ("groups", "tile")),
            P(("groups", "tile"), None, None),
        ),
        out_specs=(P(None, ("groups", "tile")), P(("groups", "tile"), None, None)),
        check_vma=False,
    )
```

```python
import functools

import jax
import jax.numpy as jnp
from jax import lax
from jax.experimental import pallas as pl
from jax.experimental.pallas import tpu as pltpu
from jax.sharding import PartitionSpec as P

PBLK = 256
NEAR = 3
SG = 16
CHUNK = 128
LAYER = 4
PAIR = 2
NARROW = 3
ROUNDS = (6, 6, 4)
MIB = 1 << 20
TERMS = 32
CROSS = ((0, 0), (0, 1), (1, 0), (0, 2), (1, 1), (2, 0))


def round_sizes(slots):
    return [slots * r // sum(ROUNDS) for r in ROUNDS]


def pack_kernel(local_tiles, layers, slots, here, tiles, counts, obs_in, pix_in, *rest):
    sizes = round_sizes(slots)
    total = len(sizes)
    obs_out, pix_out = rest[: total * layers], rest[total * layers : (total + 1) * layers]
    obs, pix, obs_all, pix_all, fill, sems = rest[(total + 1) * layers :]
    loads = [
        pltpu.make_async_copy(obs_in, obs, sems.at[0]),
        pltpu.make_async_copy(pix_in, pix, sems.at[1]),
    ]
    for copy in loads:
        copy.start()
    my_layer, my_seat = lax.div(here[0], LAYER), lax.rem(here[0], LAYER)
    chunks = pix.shape[2] // CHUNK
    stride = slots + 1
    for x in range(layers):
        fill[x] = 0
    lane = lax.broadcasted_iota(jnp.int32, (8, CHUNK), 1)
    row = lax.broadcasted_iota(jnp.int32, (8, CHUNK), 0)
    for copy in loads:
        copy.wait()

    def put(b, infos):
        tile = tiles[b]
        count = counts[b]
        owner = lax.div(tile, local_tiles)
        x = lax.div(owner, LAYER) ^ my_layer
        seat = lax.rem(owner, LAYER) ^ my_seat
        spot = lax.rem(seat, PAIR) * PAIR + lax.div(seat, PAIR)
        screen = spot * local_tiles + lax.rem(tile, local_tiles)
        slot = fill[x]
        fill[x] = slot + lax.div(count + CHUNK - 1, CHUNK)
        for c in range(chunks):
            at = slot + c
            live = jnp.clip(count - c * CHUNK, 0, CHUNK)
            obs_all[x * stride + at] = obs[b, :, c * CHUNK : (c + 1) * CHUNK]
            pix_all[x * stride + at] = pix[b, :, c * CHUNK : (c + 1) * CHUNK]
            entry = jnp.where(row == 0, live, jnp.where(row == 1, tile, screen))
            here_only = (lane == at) & (row < 3)
            infos = tuple(
                jnp.where(here_only & (x == i), entry, info) for i, info in enumerate(infos)
            )
        return infos

    infos = lax.fori_loop(
        0, obs.shape[0], put, tuple(jnp.zeros((8, CHUNK), jnp.int32) for _ in range(layers))
    )
    copies = []
    for x in range(layers):
        at = x * stride
        pix_all[at + slots] = infos[x].astype(jnp.float32)
        copies.append((pix_all.at[pl.ds(at, stride)], pix_out[x]))
        for i, size in enumerate(sizes):
            copies.append((obs_all.at[pl.ds(at, size)], obs_out[i * layers + x]))
            at += size
    copies = [pltpu.make_async_copy(a, b, sems.at[i]) for i, (a, b) in enumerate(copies)]
    for copy in copies:
        copy.start()
    for copy in copies:
        copy.wait()


def pack(observations, pixel_geometry, block_counts, block_tiles, here, devices, local_tiles):
    blocks, epochs, width = observations.shape
    layers = devices // LAYER
    slots = LAYER * (2 * blocks // devices) * (width // CHUNK)
    sizes = round_sizes(slots)
    smem = pl.BlockSpec(memory_space=pltpu.SMEM)
    hbm = pl.BlockSpec(memory_space=pl.ANY)
    pix_part = jax.ShapeDtypeStruct((slots + 1, 8, CHUNK), jnp.float32)
    out = pl.pallas_call(
        functools.partial(pack_kernel, local_tiles, layers, slots),
        in_specs=[smem, smem, smem, hbm, hbm],
        out_specs=[hbm] * ((len(sizes) + 1) * layers),
        out_shape=[
            jax.ShapeDtypeStruct((size, epochs, CHUNK), observations.dtype)
            for size in sizes
            for _ in range(layers)
        ]
        + [pix_part] * layers,
        scratch_shapes=[
            pltpu.VMEM(observations.shape, observations.dtype),
            pltpu.VMEM(pixel_geometry.shape, jnp.float32),
            pltpu.VMEM((layers * (slots + 1), epochs, CHUNK), observations.dtype),
            pltpu.VMEM((layers * (slots + 1), 8, CHUNK), jnp.float32),
            pltpu.SMEM((layers,), jnp.int32),
            pltpu.SemaphoreType.DMA(((len(sizes) + 1) * layers,)),
        ],
        compiler_params=pltpu.CompilerParams(vmem_limit_bytes=9 * MIB),
        name="pack",
    )(here, block_tiles, block_counts, observations, pixel_geometry)
    rounds = len(sizes)
    return [out[i * layers : (i + 1) * layers] for i in range(rounds)], out[rounds * layers :]


def split(values):
    parts = []
    for _ in range(3):
        part = lax.reduce_precision(values, 8, 7)
        parts.append(part)
        values = values - part
    return parts


def kernel_split(values):
    parts = []
    for _ in range(3):
        part = values.astype(jnp.bfloat16).astype(jnp.float32)
        parts.append(part)
        values = values - part
    return parts


def fit_kernel(first, final, layers, slots, groups, *refs):
    info, cutoffs, places, spots, origin = refs[:5]
    rest = refs[5:]
    obs_in, pix_in = [], []
    for _ in groups:
        obs_in.append(rest[:layers])
        pix_in.append(rest[layers : 2 * layers])
        rest = rest[2 * layers :]
    patches, forms = rest[:2]
    rest = rest[1:]
    if first:
        screen_parts, stress_parts = rest[1 : 1 + PAIR], rest[1 + PAIR : 1 + 2 * PAIR]
        rest = rest[1 + 2 * PAIR :]
        grad, screen_grad, screens, stress = rest[:4]
        rest = rest[4:]
    else:
        screens, stress = rest[1:3]
        grad, screen_grad = rest[5:7]
        rest = rest[7:]
    outs = rest[:3] if final else ()
    rest = rest[len(outs) :]
    obs, pix = rest[:2]
    buffers = rest[2 : 2 + 9 * PAIR]
    wide, sights = rest[2 + 9 * PAIR : 2 + 10 * PAIR], rest[2 + 10 * PAIR : 2 + 11 * PAIR]
    items, sems = rest[2 + 11 * PAIR :]
    sets = [
        [buffers[3 * (PAIR * i + lane) : 3 * (PAIR * i + lane) + 3] for lane in range(PAIR)]
        for i in range(3)
    ]
    epochs = obs.shape[1]
    base = groups[0][0]
    span = sum(size for _, _, size in groups)
    local_tiles = screens.shape[0] // LAYER

    loads = []
    for x in range(layers):
        at = x * span
        for g, (_, low, size) in enumerate(groups):
            loads.append((obs_in[g][x], obs.at[pl.ds(at, size)]))
            loads.append((pix_in[g][x].at[pl.ds(low, size)], pix.at[pl.ds(at, size)]))
            at += size
    if first:
        for parts, whole in ((screen_parts, screens), (stress_parts, stress)):
            size = whole.shape[0] // PAIR
            for i, part in enumerate(parts):
                loads.append((part, whole.at[pl.ds(i * size, size)]))
    loads = [pltpu.make_async_copy(a, b, sems.at[i]) for i, (a, b) in enumerate(loads)]
    for copy in loads:
        copy.start()
    if first:
        grad[...] = jnp.zeros_like(grad)
        screen_grad[...] = jnp.zeros_like(screen_grad)

    def info_of(slot, kind):
        x = lax.div(slot, span)
        return info[(x * 3 + kind) * slots + base + lax.rem(slot, span)]

    def list_slot(slot, total):
        items[total] = slot
        return total + jnp.where(info_of(slot, 0) > 0, 1, 0)

    total = lax.fori_loop(0, layers * span, list_slot, 0)
    for copy in loads:
        copy.wait()

    def item_of(i):
        slot = items[jnp.minimum(i, total - 1)]
        tile = info_of(slot, 1)
        return slot, [cutoffs[tile * NEAR + k] for k in range(NEAR)]

    def spread(rows, lane):
        columns = rows.T
        for i in range(2):
            wide[lane][i] = jnp.broadcast_to(columns[:, i : i + 1], (CHUNK, CHUNK))
        le, ln = rows[4:5], rows[5:6]
        along = le * (rows[0:1] - origin[0]) + ln * (rows[1:2] - origin[1])
        row = lax.broadcasted_iota(jnp.int32, (8, CHUNK), 0)
        factors = jnp.where(
            row == 0, along, jnp.where(row == 1, le, jnp.where(row == 2, ln, rows[6:7]))
        )
        parts = kernel_split(factors)
        low = row < 4
        tiles = []
        for first_part, second_part in zip(CROSS[::2], CROSS[1::2]):
            upper = jnp.concatenate([parts[second_part[0]][:4]] * 2, axis=0)
            tiles.append(jnp.where(low, parts[first_part[0]], upper))
        tiles.append(jnp.zeros((8, CHUNK), jnp.float32))
        sights[lane][...] = jnp.concatenate(tiles, axis=0).T.astype(jnp.bfloat16)

    def make_strips(near, k, begin, end, lane, green):
        patch = [
            jnp.broadcast_to(patches[near[k], r : r + 1], (8, PBLK)) for r in range(3)
        ]
        alongs = jnp.dot(
            sights[lane][begin:end], forms[near[k]], preferred_element_type=jnp.float32
        )
        for low in range(begin, end, 16):
            along = alongs[low - begin : low - begin + 16]
            inverses = []
            for at in (low, low + 8):
                east, north = (
                    jnp.concatenate([wide[lane][i, at : at + 8]] * (PBLK // CHUNK), axis=1)
                    for i in range(2)
                )
                dx = east - patch[0]
                dy = north - patch[1]
                inverses.append(lax.rsqrt(dx * dx + dy * dy + patch[2]))
            inverse = jnp.concatenate(inverses, axis=0)
            green[low : low + 16, k * PBLK : (k + 1) * PBLK] = (
                along * inverse * inverse * inverse
            ).astype(jnp.bfloat16)

    def make_hats(rows, hats):
        node = lax.broadcasted_iota(jnp.int32, (SG, CHUNK), 0).astype(jnp.float32)
        across = jnp.maximum(0.0, 1.0 - jnp.abs(rows[2:3] - node))
        upward = jnp.maximum(0.0, 1.0 - jnp.abs(rows[3:4] - node))
        for a in range(SG):
            hats[a * SG : (a + 1) * SG] = (across[a : a + 1] * upward).astype(jnp.bfloat16)

    def make_head(i, lane, buffers):
        slot, near = item_of(i)
        rows = pix[slot]
        make_hats(rows, buffers[1])
        spread(rows, lane)
        return near

    def predict(i, buffers):
        green, hats = buffers[:2]
        slot, near = item_of(i)
        model = jnp.dot(
            screens[info_of(slot, 2)], hats[...], preferred_element_type=jnp.float32
        )
        for k in range(NEAR):
            model += lax.dot_general(
                stress[pl.ds(pl.multiple_of(spots[near[k]], 16), epochs), :],
                green[:, k * PBLK : (k + 1) * PBLK],
                (((1,), (1,)), ((), ())),
                preferred_element_type=jnp.float32,
            )
        return model

    def weigh(i, model, buffers):
        slot, _ = item_of(i)
        live = jnp.where(i < total, info_of(slot, 0), 0)
        lane = lax.broadcasted_iota(jnp.int32, (1, CHUNK), 1)
        scale = jnp.where(lane < live, pix[slot, 7:8, :], 0.0)
        buffers[2][...] = ((model - obs[slot].astype(jnp.float32)) * scale).astype(jnp.bfloat16)

    def add_patch(near, k, buffers):
        grad[places[near[k]]] += jnp.dot(
            buffers[2][...],
            buffers[0][:, k * PBLK : (k + 1) * PBLK],
            preferred_element_type=jnp.float32,
        )

    def add_screen(slot, buffers):
        screen_grad[info_of(slot, 2)] += lax.dot_general(
            buffers[2][...],
            buffers[1][...],
            (((1,), (1,)), ((), ())),
            preferred_element_type=jnp.float32,
        )

    lanes = range(PAIR)
    half = CHUNK // 2

    def make_pair(j, buffers):
        for lane in lanes:
            near = make_head(PAIR * j + lane, lane, buffers[lane])
            for k in range(NEAR):
                for low in (0, half):
                    make_strips(near, k, low, low + half, lane, buffers[lane][0])

    def model_pair(j, buffers):
        for lane in lanes:
            model = predict(PAIR * j + lane, buffers[lane])
            weigh(PAIR * j + lane, model, buffers[lane])

    def turn(j, using, middle, making):
        now = [item_of(PAIR * j + lane) for lane in lanes]
        coming = [PAIR * (j + 1) + lane for lane in lanes]
        near = [
            make_head(PAIR * (j + 2) + lane, lane, making[lane]) for lane in lanes
        ]
        models = [predict(coming[lane], middle[lane]) for lane in lanes]

        def strips(k, lane):
            for low in (0, half):
                make_strips(near[lane], k, low, low + half, lane, making[lane][0])

        def adds(k):
            for lane in lanes:
                add_patch(now[lane][1], k, using[lane])

        strips(0, 0)
        adds(0)
        strips(0, 1)
        adds(1)
        strips(1, 0)
        for lane in lanes:
            weigh(coming[lane], models[lane], middle[lane])
        strips(1, 1)
        adds(2)
        strips(2, 0)
        for lane in lanes:
            add_screen(now[lane][0], using[lane])
        strips(2, 1)

    @pl.when(total > 0)
    def _():
        pairs = lax.div(total + PAIR - 1, PAIR)
        make_pair(0, sets[0])
        make_pair(1, sets[1])
        model_pair(0, sets[0])

        def step(i, _):
            for at in range(3):
                j = 3 * i + at

                @pl.when(j < pairs)
                def _():
                    turn(j, sets[at], sets[(at + 1) % 3], sets[(at + 2) % 3])

            return 0

        lax.fori_loop(0, lax.div(pairs + 2, 3), step, 0)

    if final:
        half = grad.shape[0] // 2
        outs[0][...] = grad[half:].astype(outs[0].dtype)
        for i, out in enumerate(outs[1:]):
            low = (PAIR + i) * local_tiles
            out[...] = screen_grad[low : low + local_tiles].astype(out.dtype)


def fit(tables, groups, patches, forms, screens, stress, state, first, final):
    layers = len(groups[0][1])
    slots = tables[0].shape[0] // (3 * layers)
    smem = pl.BlockSpec(memory_space=pltpu.SMEM)
    vmem = pl.BlockSpec(memory_space=pltpu.VMEM)
    hbm = pl.BlockSpec(memory_space=pl.ANY)
    spans = tuple((base, low, obs[0].shape[0]) for base, obs, _, low in groups)
    arrays = [a for _, obs, pix, _ in groups for a in (*obs, *pix)]
    span = sum(size for _, _, size in spans)
    blocks, epochs = state[0].shape[0], state[0].shape[1]
    out_shape = [jax.ShapeDtypeStruct(a.shape, a.dtype) for a in state]
    if first:
        state = ()
        for parts in (screens, stress):
            shape = (PAIR * parts[0].shape[0],) + parts[0].shape[1:]
            out_shape.append(jax.ShapeDtypeStruct(shape, parts[0].dtype))
    else:
        screens, stress = [screens], [stress]
    if final:
        out_shape.append(jax.ShapeDtypeStruct((blocks // 2, epochs, PBLK), jnp.bfloat16))
        shape = (state[1].shape[0] // LAYER,) + state[1].shape[1:]
        out_shape += [jax.ShapeDtypeStruct(shape, jnp.bfloat16)] * 2
    before = len(tables) + len(arrays) + 2 + len(screens) + len(stress)
    return pl.pallas_call(
        functools.partial(fit_kernel, first, final, layers, slots, spans),
        in_specs=[smem] * len(tables)
        + [hbm] * len(arrays)
        + [vmem] * 2
        + [hbm if first else vmem] * (len(screens) + len(stress))
        + [vmem] * len(state),
        out_specs=[vmem] * len(out_shape),
        out_shape=out_shape,
        scratch_shapes=[
            pltpu.VMEM((layers * span, epochs, CHUNK), arrays[0].dtype),
            pltpu.VMEM((layers * span, 8, CHUNK), jnp.float32),
        ]
        + [
            pltpu.VMEM((CHUNK, NEAR * PBLK), jnp.bfloat16),
            pltpu.VMEM((SG * SG, CHUNK), jnp.bfloat16),
            pltpu.VMEM((epochs, CHUNK), jnp.bfloat16),
        ]
        * (3 * PAIR)
        + [pltpu.VMEM((2, CHUNK, CHUNK), jnp.float32)] * PAIR
        + [pltpu.VMEM((CHUNK, TERMS), jnp.bfloat16)] * PAIR
        + [
            pltpu.SMEM((layers * span + 1,), jnp.int32),
            pltpu.SemaphoreType.DMA((2 * layers * len(groups) + 2 * LAYER,)),
        ],
        input_output_aliases={} if first else {before: 0, before + 1: 1},
        compiler_params=pltpu.CompilerParams(vmem_limit_bytes=6 * MIB),
        cost_estimate=pl.CostEstimate(
            flops=layers * span * 4 * epochs * CHUNK * (NEAR + 1) * PBLK,
            bytes_accessed=1024,
            transcendentals=layers * span * CHUNK * NEAR * PBLK,
        ),
        name="fit",
    )(*tables, *arrays, patches, forms, *screens, *stress, *state)


def partner(values, devices, distance):
    return lax.ppermute(values, "tile", [(i, i ^ distance) for i in range(devices)])


def orders(devices):
    stages = devices.bit_length() - 1
    high = list(range(2, stages))
    return [1] + high, high + [1]


def block_places(devices, here, blocks, local, epochs):
    block = jnp.arange(blocks)
    other = (block // local) ^ here
    seat = block % local
    half = local // 2
    turned = []
    for order in orders(devices):
        spot = 0
        for bit in order:
            spot = spot * 2 + ((other >> bit) & 1)
        turned.append(spot)
    chips = devices // 2
    upper = seat // half
    spot = jnp.where(upper == 0, turned[0], turned[1])
    place = (((other & 1) * 2 + upper) * chips + spot) * half + seat % half
    stages = devices.bit_length() - 1
    held = sum(((other >> (stages - 1 - s)) & 1) << s for s in range(stages))
    return place.astype(jnp.int32), ((held * local + seat) * epochs).astype(jnp.int32)


def halve(kept, given, there, devices):
    total = kept + partner(given, devices, 1).astype(jnp.float32)
    middle = total.shape[0] // 2
    parts = [total[:middle], total[middle:]]
    both = orders(devices)
    stages = len(both[0])
    back = None
    for stage in range(stages):
        got = []
        for side in range(2):
            given = parts[side][parts[side].shape[0] // 2 :]
            if stages - stage <= NARROW:
                given = given.astype(jnp.bfloat16)
            got.append(partner(given, devices, 1 << both[side][stage]))
        for side in range(2):
            if side:
                _, got[1] = lax.optimization_barrier((parts[0], got[1]))
            size = parts[side].shape[0] // 2
            parts[side] = parts[side][:size] + got[side].astype(jnp.float32)
            if back is None:
                _, there = lax.optimization_barrier((parts[0], there))
                back = partner(there, devices, PAIR)
    return jnp.concatenate(parts, axis=0), back


def on_device(
    observations,
    pixel_geometry,
    block_counts,
    block_tiles,
    cutoff_lists,
    patch_geometry,
    stress,
    screens,
):
    devices = lax.axis_size("tile")
    here = lax.axis_index("tile")
    blocks, epochs, width = observations.shape
    local_tiles = screens.shape[0]
    layers = devices // LAYER
    local = stress.shape[1] // PBLK

    slots = LAYER * (2 * blocks // devices) * (width // CHUNK)
    sizes = round_sizes(slots)

    held = jnp.swapaxes(stress.reshape(epochs, local, PBLK), 0, 1).reshape(-1, PBLK)
    other = partner(held, devices, devices // 2)
    across_screens = partner(screens, devices, PAIR)
    obs, pix = pack(
        observations,
        pixel_geometry,
        block_counts,
        block_tiles,
        jnp.reshape(here, (1,)).astype(jnp.int32),
        devices,
        local_tiles,
    )

    def exchange(parts):
        got = [partner(parts[x], devices, x * LAYER) for x in range(layers - 1, 0, -1)]
        return [parts[0]] + got[::-1]

    other, pix = lax.optimization_barrier((other, pix))
    pix = exchange(pix)
    distance = devices // 2
    while distance >= LAYER:
        if distance < devices // 2:
            other = partner(held, devices, distance)
        held = jnp.concatenate([held, other], axis=0)
        distance //= 2
    patch_blocks = devices * local
    east, north, depth, compliance = patch_geometry
    origin = patch_geometry[:2, 0]
    strength = compliance * depth * depth
    faces = split(
        jnp.stack(
            [
                strength,
                -strength * (east - origin[0]),
                -strength * (north - origin[1]),
                strength * depth,
            ]
        )
    )
    forms = jnp.concatenate(
        [faces[second] for _, second in CROSS] + [jnp.zeros((8,) + east.shape, jnp.float32)]
    ).astype(jnp.bfloat16)
    forms = jnp.swapaxes(forms.reshape(TERMS, patch_blocks, PBLK), 0, 1)
    patches = jnp.stack([east, north, depth * depth])
    patches = jnp.swapaxes(patches.reshape(3, patch_blocks, PBLK), 0, 1)
    cutoffs = cutoff_lists.reshape(-1)
    held, pix[1], across_screens = lax.optimization_barrier((held, pix[1], across_screens))
    across_screens, forms, patches, cutoffs = lax.optimization_barrier(
        (across_screens, forms, patches, cutoffs)
    )
    got = [exchange(o) for o in obs]
    across = partner(held, devices, PAIR)
    across, pix, got[0] = lax.optimization_barrier((across, pix, got[0]))
    held = jnp.concatenate([held, across], axis=0)
    all_stress = [held, partner(held, devices, 1)]
    near_screens = jnp.concatenate([screens, across_screens], axis=0)
    all_screens = [near_screens, partner(near_screens, devices, 1)]

    places, spots = block_places(devices, here, patch_blocks, local, epochs)
    info = jnp.stack([p[slots, :3, :slots] for p in pix]).astype(jnp.int32).reshape(-1)
    tables = (info, cutoffs, places, spots, origin)

    state = (
        jax.ShapeDtypeStruct((patch_blocks, epochs, PBLK), jnp.float32),
        jax.ShapeDtypeStruct((LAYER * local_tiles,) + screens.shape[1:], jnp.float32),
    )
    base = 0
    for i, size in enumerate(sizes):
        first, final = i == 0, i == len(sizes) - 1
        groups = [(base, got[i], pix, base)]
        state = fit(
            tables,
            groups,
            patches,
            forms,
            all_screens,
            all_stress,
            state[:2],
            first,
            final,
        )
        if first:
            all_screens, all_stress = state[2:]
        base += size
    grad, screen_grad, given, next_door, diagonal = state
    own, far = screen_grad[:local_tiles], screen_grad[local_tiles : PAIR * local_tiles]
    there = (far + partner(diagonal, devices, 1).astype(jnp.float32)).astype(jnp.bfloat16)
    grad, back = halve(grad[: grad.shape[0] // 2], given, there, devices)
    screen_gradient = (
        own + partner(next_door, devices, 1).astype(jnp.float32) + back.astype(jnp.float32)
    )
    return (jnp.swapaxes(grad, 0, 1).reshape(epochs, local * PBLK), screen_gradient)


def solution(mesh):
    return jax.shard_map(
        on_device,
        mesh=mesh,
        in_specs=(
            P(("groups", "tile"), None, None),
            P(("groups", "tile"), None, None),
            P(("groups", "tile")),
            P(("groups", "tile")),
            P(),
            P(),
            P(None, ("groups", "tile")),
            P(("groups", "tile"), None, None),
        ),
        out_specs=(P(None, ("groups", "tile")), P(("groups", "tile"), None, None)),
        check_vma=False,
    )
```

```python
import functools

import jax
import jax.numpy as jnp
from jax import lax
from jax.experimental import pallas as pl
from jax.experimental.pallas import tpu as pltpu
from jax.sharding import PartitionSpec as P

PBLK = 256
NEAR = 3
SG = 16
CHUNK = 128
LAYER = 4
PAIR = 2
NARROW = 3
ROUNDS = (6, 6, 4)
MIB = 1 << 20
TERMS = 32
CROSS = ((0, 0), (0, 1), (1, 0), (0, 2), (1, 1), (2, 0))


def round_sizes(slots):
    return [slots * r // sum(ROUNDS) for r in ROUNDS]


def pack_kernel(local_tiles, layers, slots, here, tiles, counts, obs_in, pix_in, *rest):
    sizes = round_sizes(slots)
    total = len(sizes)
    obs_out, pix_out = rest[: total * layers], rest[total * layers : (total + 1) * layers]
    obs, pix, obs_all, pix_all, fill, sems = rest[(total + 1) * layers :]
    loads = [
        pltpu.make_async_copy(obs_in, obs, sems.at[0]),
        pltpu.make_async_copy(pix_in, pix, sems.at[1]),
    ]
    for copy in loads:
        copy.start()
    my_layer, my_seat = lax.div(here[0], LAYER), lax.rem(here[0], LAYER)
    chunks = pix.shape[2] // CHUNK
    stride = slots + 1
    for x in range(layers):
        fill[x] = 0
    lane = lax.broadcasted_iota(jnp.int32, (8, CHUNK), 1)
    row = lax.broadcasted_iota(jnp.int32, (8, CHUNK), 0)
    for copy in loads:
        copy.wait()

    def put(b, infos):
        tile = tiles[b]
        count = counts[b]
        owner = lax.div(tile, local_tiles)
        x = lax.div(owner, LAYER) ^ my_layer
        seat = lax.rem(owner, LAYER) ^ my_seat
        spot = lax.rem(seat, PAIR) * PAIR + lax.div(seat, PAIR)
        screen = spot * local_tiles + lax.rem(tile, local_tiles)
        slot = fill[x]
        fill[x] = slot + lax.div(count + CHUNK - 1, CHUNK)
        for c in range(chunks):
            at = slot + c
            live = jnp.clip(count - c * CHUNK, 0, CHUNK)
            obs_all[x * stride + at] = obs[b, :, c * CHUNK : (c + 1) * CHUNK]
            pix_all[x * stride + at] = pix[b, :, c * CHUNK : (c + 1) * CHUNK]
            entry = jnp.where(row == 0, live, jnp.where(row == 1, tile, screen))
            here_only = (lane == at) & (row < 3)
            infos = tuple(
                jnp.where(here_only & (x == i), entry, info) for i, info in enumerate(infos)
            )
        return infos

    infos = lax.fori_loop(
        0, obs.shape[0], put, tuple(jnp.zeros((8, CHUNK), jnp.int32) for _ in range(layers))
    )
    copies = []
    for x in range(layers):
        at = x * stride
        pix_all[at + slots] = infos[x].astype(jnp.float32)
        copies.append((pix_all.at[pl.ds(at, stride)], pix_out[x]))
        for i, size in enumerate(sizes):
            copies.append((obs_all.at[pl.ds(at, size)], obs_out[i * layers + x]))
            at += size
    copies = [pltpu.make_async_copy(a, b, sems.at[i]) for i, (a, b) in enumerate(copies)]
    for copy in copies:
        copy.start()
    for copy in copies:
        copy.wait()


def pack(observations, pixel_geometry, block_counts, block_tiles, here, devices, local_tiles):
    blocks, epochs, width = observations.shape
    layers = devices // LAYER
    slots = LAYER * (2 * blocks // devices) * (width // CHUNK)
    sizes = round_sizes(slots)
    smem = pl.BlockSpec(memory_space=pltpu.SMEM)
    hbm = pl.BlockSpec(memory_space=pl.ANY)
    pix_part = jax.ShapeDtypeStruct((slots + 1, 8, CHUNK), jnp.float32)
    out = pl.pallas_call(
        functools.partial(pack_kernel, local_tiles, layers, slots),
        in_specs=[smem, smem, smem, hbm, hbm],
        out_specs=[hbm] * ((len(sizes) + 1) * layers),
        out_shape=[
            jax.ShapeDtypeStruct((size, epochs, CHUNK), observations.dtype)
            for size in sizes
            for _ in range(layers)
        ]
        + [pix_part] * layers,
        scratch_shapes=[
            pltpu.VMEM(observations.shape, observations.dtype),
            pltpu.VMEM(pixel_geometry.shape, jnp.float32),
            pltpu.VMEM((layers * (slots + 1), epochs, CHUNK), observations.dtype),
            pltpu.VMEM((layers * (slots + 1), 8, CHUNK), jnp.float32),
            pltpu.SMEM((layers,), jnp.int32),
            pltpu.SemaphoreType.DMA(((len(sizes) + 1) * layers,)),
        ],
        compiler_params=pltpu.CompilerParams(vmem_limit_bytes=10 * MIB),
        name="pack",
    )(here, block_tiles, block_counts, observations, pixel_geometry)
    rounds = len(sizes)
    return [out[i * layers : (i + 1) * layers] for i in range(rounds)], out[rounds * layers :]


def split(values):
    parts = []
    for _ in range(3):
        part = lax.reduce_precision(values, 8, 7)
        parts.append(part)
        values = values - part
    return parts


def kernel_split(values):
    parts = []
    for _ in range(3):
        part = values.astype(jnp.bfloat16).astype(jnp.float32)
        parts.append(part)
        values = values - part
    return parts


def fit_kernel(first, final, layers, slots, groups, *refs):
    info, cutoffs, places, spots, origin = refs[:5]
    rest = refs[5:]
    obs_in, pix_in = [], []
    for _ in groups:
        obs_in.append(rest[:layers])
        pix_in.append(rest[layers : 2 * layers])
        rest = rest[2 * layers :]
    patches, forms = rest[:2]
    rest = rest[1:]
    if first:
        screen_parts, stress_parts = rest[1 : 1 + PAIR], rest[1 + PAIR : 1 + 2 * PAIR]
        rest = rest[1 + 2 * PAIR :]
        grad, screen_grad, screens, stress = rest[:4]
        rest = rest[4:]
    else:
        screens, stress = rest[1:3]
        grad, screen_grad = rest[5:7]
        rest = rest[7:]
    outs = rest[:3] if final else ()
    rest = rest[len(outs) :]
    obs, pix = rest[:2]
    buffers = rest[2 : 2 + 9 * PAIR]
    wide, sights = rest[2 + 9 * PAIR : 2 + 10 * PAIR], rest[2 + 10 * PAIR : 2 + 11 * PAIR]
    items, sems = rest[2 + 11 * PAIR :]
    sets = [
        [buffers[3 * (PAIR * i + lane) : 3 * (PAIR * i + lane) + 3] for lane in range(PAIR)]
        for i in range(3)
    ]
    epochs = obs.shape[1]
    base = groups[0][0]
    span = sum(size for _, _, size in groups)
    local_tiles = screens.shape[0] // LAYER

    loads = []
    for x in range(layers):
        at = x * span
        for g, (_, low, size) in enumerate(groups):
            loads.append((obs_in[g][x], obs.at[pl.ds(at, size)]))
            loads.append((pix_in[g][x].at[pl.ds(low, size)], pix.at[pl.ds(at, size)]))
            at += size
    if first:
        for parts, whole in ((screen_parts, screens), (stress_parts, stress)):
            size = whole.shape[0] // PAIR
            for i, part in enumerate(parts):
                loads.append((part, whole.at[pl.ds(i * size, size)]))
    loads = [pltpu.make_async_copy(a, b, sems.at[i]) for i, (a, b) in enumerate(loads)]
    for copy in loads:
        copy.start()
    if first:
        grad[...] = jnp.zeros_like(grad)
        screen_grad[...] = jnp.zeros_like(screen_grad)

    def info_of(slot, kind):
        x = lax.div(slot, span)
        return info[(x * 3 + kind) * slots + base + lax.rem(slot, span)]

    def list_slot(slot, total):
        items[total] = slot
        return total + jnp.where(info_of(slot, 0) > 0, 1, 0)

    total = lax.fori_loop(0, layers * span, list_slot, 0)
    for copy in loads:
        copy.wait()

    def item_of(i):
        slot = items[jnp.minimum(i, total - 1)]
        tile = info_of(slot, 1)
        return slot, [cutoffs[tile * NEAR + k] for k in range(NEAR)]

    def spread(rows, lane):
        columns = rows.T
        for i in range(2):
            wide[lane][i] = jnp.broadcast_to(columns[:, i : i + 1], (CHUNK, CHUNK))
        le, ln = rows[4:5], rows[5:6]
        along = le * (rows[0:1] - origin[0]) + ln * (rows[1:2] - origin[1])
        row = lax.broadcasted_iota(jnp.int32, (8, CHUNK), 0)
        factors = jnp.where(
            row == 0, along, jnp.where(row == 1, le, jnp.where(row == 2, ln, rows[6:7]))
        )
        parts = kernel_split(factors)
        low = row < 4
        tiles = []
        for first_part, second_part in zip(CROSS[::2], CROSS[1::2]):
            upper = jnp.concatenate([parts[second_part[0]][:4]] * 2, axis=0)
            tiles.append(jnp.where(low, parts[first_part[0]], upper))
        tiles.append(jnp.zeros((8, CHUNK), jnp.float32))
        sights[lane][...] = jnp.concatenate(tiles, axis=0).T.astype(jnp.bfloat16)

    def make_strips(near, k, begin, end, lane, green):
        patch = [
            jnp.broadcast_to(patches[near[k], r : r + 1], (8, PBLK)) for r in range(3)
        ]
        alongs = jnp.dot(
            sights[lane][begin:end], forms[near[k]], preferred_element_type=jnp.float32
        )
        for low in range(begin, end, 16):
            along = alongs[low - begin : low - begin + 16]
            inverses = []
            for at in (low, low + 8):
                east, north = (
                    jnp.concatenate([wide[lane][i, at : at + 8]] * (PBLK // CHUNK), axis=1)
                    for i in range(2)
                )
                dx = east - patch[0]
                dy = north - patch[1]
                inverses.append(lax.rsqrt(dx * dx + dy * dy + patch[2]))
            inverse = jnp.concatenate(inverses, axis=0)
            green[low : low + 16, k * PBLK : (k + 1) * PBLK] = (
                along * inverse * inverse * inverse
            ).astype(jnp.bfloat16)

    def make_hats(rows, hats):
        node = lax.broadcasted_iota(jnp.int32, (SG, CHUNK), 0).astype(jnp.float32)
        across = jnp.maximum(0.0, 1.0 - jnp.abs(rows[2:3] - node))
        upward = jnp.maximum(0.0, 1.0 - jnp.abs(rows[3:4] - node))
        for a in range(SG):
            hats[a * SG : (a + 1) * SG] = (across[a : a + 1] * upward).astype(jnp.bfloat16)

    def make_head(i, lane, buffers):
        slot, near = item_of(i)
        rows = pix[slot]
        make_hats(rows, buffers[1])
        spread(rows, lane)
        return near

    def predict(i, buffers):
        green, hats = buffers[:2]
        slot, near = item_of(i)
        model = jnp.dot(
            screens[info_of(slot, 2)], hats[...], preferred_element_type=jnp.float32
        )
        for k in range(NEAR):
            model += lax.dot_general(
                stress[pl.ds(pl.multiple_of(spots[near[k]], 16), epochs), :],
                green[:, k * PBLK : (k + 1) * PBLK],
                (((1,), (1,)), ((), ())),
                preferred_element_type=jnp.float32,
            )
        return model

    def weigh(i, model, buffers):
        slot, _ = item_of(i)
        live = jnp.where(i < total, info_of(slot, 0), 0)
        lane = lax.broadcasted_iota(jnp.int32, (1, CHUNK), 1)
        scale = jnp.where(lane < live, pix[slot, 7:8, :], 0.0)
        buffers[2][...] = ((model - obs[slot].astype(jnp.float32)) * scale).astype(jnp.bfloat16)

    def add_patch(near, k, buffers):
        grad[places[near[k]]] += jnp.dot(
            buffers[2][...],
            buffers[0][:, k * PBLK : (k + 1) * PBLK],
            preferred_element_type=jnp.float32,
        )

    def add_screen(slot, buffers):
        screen_grad[info_of(slot, 2)] += lax.dot_general(
            buffers[2][...],
            buffers[1][...],
            (((1,), (1,)), ((), ())),
            preferred_element_type=jnp.float32,
        )

    lanes = range(PAIR)
    half = CHUNK // 2

    def make_pair(j, buffers):
        for lane in lanes:
            near = make_head(PAIR * j + lane, lane, buffers[lane])
            for k in range(NEAR):
                for low in (0, half):
                    make_strips(near, k, low, low + half, lane, buffers[lane][0])

    def model_pair(j, buffers):
        for lane in lanes:
            model = predict(PAIR * j + lane, buffers[lane])
            weigh(PAIR * j + lane, model, buffers[lane])

    def turn(j, using, middle, making):
        now = [item_of(PAIR * j + lane) for lane in lanes]
        coming = [PAIR * (j + 1) + lane for lane in lanes]
        near = [
            make_head(PAIR * (j + 2) + lane, lane, making[lane]) for lane in lanes
        ]
        models = [predict(coming[lane], middle[lane]) for lane in lanes]

        def strips(k, lane):
            for low in (0, half):
                make_strips(near[lane], k, low, low + half, lane, making[lane][0])

        def adds(k):
            for lane in lanes:
                add_patch(now[lane][1], k, using[lane])

        strips(0, 0)
        adds(0)
        strips(0, 1)
        adds(1)
        strips(1, 0)
        for lane in lanes:
            weigh(coming[lane], models[lane], middle[lane])
        strips(1, 1)
        adds(2)
        strips(2, 0)
        for lane in lanes:
            add_screen(now[lane][0], using[lane])
        strips(2, 1)

    @pl.when(total > 0)
    def _():
        pairs = lax.div(total + PAIR - 1, PAIR)
        make_pair(0, sets[0])
        make_pair(1, sets[1])
        model_pair(0, sets[0])

        def step(i, _):
            for at in range(3):
                j = 3 * i + at

                @pl.when(j < pairs)
                def _():
                    turn(j, sets[at], sets[(at + 1) % 3], sets[(at + 2) % 3])

            return 0

        lax.fori_loop(0, lax.div(pairs + 2, 3), step, 0)

    if final:
        half = grad.shape[0] // 2
        outs[0][...] = grad[half:].astype(outs[0].dtype)
        for i, out in enumerate(outs[1:]):
            low = (PAIR + i) * local_tiles
            out[...] = screen_grad[low : low + local_tiles].astype(out.dtype)


def fit(tables, groups, patches, forms, screens, stress, state, first, final):
    layers = len(groups[0][1])
    slots = tables[0].shape[0] // (3 * layers)
    smem = pl.BlockSpec(memory_space=pltpu.SMEM)
    vmem = pl.BlockSpec(memory_space=pltpu.VMEM)
    hbm = pl.BlockSpec(memory_space=pl.ANY)
    spans = tuple((base, low, obs[0].shape[0]) for base, obs, _, low in groups)
    arrays = [a for _, obs, pix, _ in groups for a in (*obs, *pix)]
    span = sum(size for _, _, size in spans)
    blocks, epochs = state[0].shape[0], state[0].shape[1]
    out_shape = [jax.ShapeDtypeStruct(a.shape, a.dtype) for a in state]
    if first:
        state = ()
        for parts in (screens, stress):
            shape = (PAIR * parts[0].shape[0],) + parts[0].shape[1:]
            out_shape.append(jax.ShapeDtypeStruct(shape, parts[0].dtype))
    else:
        screens, stress = [screens], [stress]
    if final:
        out_shape.append(jax.ShapeDtypeStruct((blocks // 2, epochs, PBLK), jnp.bfloat16))
        shape = (state[1].shape[0] // LAYER,) + state[1].shape[1:]
        out_shape += [jax.ShapeDtypeStruct(shape, jnp.bfloat16)] * 2
    before = len(tables) + len(arrays) + 2 + len(screens) + len(stress)
    return pl.pallas_call(
        functools.partial(fit_kernel, first, final, layers, slots, spans),
        in_specs=[smem] * len(tables)
        + [hbm] * len(arrays)
        + [vmem] * 2
        + [hbm if first else vmem] * (len(screens) + len(stress))
        + [vmem] * len(state),
        out_specs=[vmem] * len(out_shape),
        out_shape=out_shape,
        scratch_shapes=[
            pltpu.VMEM((layers * span, epochs, CHUNK), arrays[0].dtype),
            pltpu.VMEM((layers * span, 8, CHUNK), jnp.float32),
        ]
        + [
            pltpu.VMEM((CHUNK, NEAR * PBLK), jnp.bfloat16),
            pltpu.VMEM((SG * SG, CHUNK), jnp.bfloat16),
            pltpu.VMEM((epochs, CHUNK), jnp.bfloat16),
        ]
        * (3 * PAIR)
        + [pltpu.VMEM((2, CHUNK, CHUNK), jnp.float32)] * PAIR
        + [pltpu.VMEM((CHUNK, TERMS), jnp.bfloat16)] * PAIR
        + [
            pltpu.SMEM((layers * span + 1,), jnp.int32),
            pltpu.SemaphoreType.DMA((2 * layers * len(groups) + 2 * LAYER,)),
        ],
        input_output_aliases={} if first else {before: 0, before + 1: 1},
        compiler_params=pltpu.CompilerParams(vmem_limit_bytes=8 * MIB),
        cost_estimate=pl.CostEstimate(
            flops=layers * span * 4 * epochs * CHUNK * (NEAR + 1) * PBLK,
            bytes_accessed=1024,
            transcendentals=layers * span * CHUNK * NEAR * PBLK,
        ),
        name="fit",
    )(*tables, *arrays, patches, forms, *screens, *stress, *state)


def partner(values, devices, distance):
    return lax.ppermute(values, "tile", [(i, i ^ distance) for i in range(devices)])


def orders(devices):
    stages = devices.bit_length() - 1
    high = list(range(2, stages))
    return [1] + high, high + [1]


def block_places(devices, here, blocks, local, epochs):
    block = jnp.arange(blocks)
    other = (block // local) ^ here
    seat = block % local
    half = local // 2
    turned = []
    for order in orders(devices):
        spot = 0
        for bit in order:
            spot = spot * 2 + ((other >> bit) & 1)
        turned.append(spot)
    chips = devices // 2
    upper = seat // half
    spot = jnp.where(upper == 0, turned[0], turned[1])
    place = (((other & 1) * 2 + upper) * chips + spot) * half + seat % half
    stages = devices.bit_length() - 1
    held = sum(((other >> (stages - 1 - s)) & 1) << s for s in range(stages))
    return place.astype(jnp.int32), ((held * local + seat) * epochs).astype(jnp.int32)


def halve(kept, given, there, devices):
    total = kept + partner(given, devices, 1).astype(jnp.float32)
    middle = total.shape[0] // 2
    parts = [total[:middle], total[middle:]]
    both = orders(devices)
    stages = len(both[0])
    back = None
    for stage in range(stages):
        got = []
        for side in range(2):
            given = parts[side][parts[side].shape[0] // 2 :]
            if stages - stage <= NARROW:
                given = given.astype(jnp.bfloat16)
            got.append(partner(given, devices, 1 << both[side][stage]))
        for side in range(2):
            if side:
                _, got[1] = lax.optimization_barrier((parts[0], got[1]))
            size = parts[side].shape[0] // 2
            parts[side] = parts[side][:size] + got[side].astype(jnp.float32)
            if back is None:
                _, there = lax.optimization_barrier((parts[0], there))
                back = partner(there, devices, PAIR)
    return jnp.concatenate(parts, axis=0), back


def on_device(
    observations,
    pixel_geometry,
    block_counts,
    block_tiles,
    cutoff_lists,
    patch_geometry,
    stress,
    screens,
):
    devices = lax.axis_size("tile")
    here = lax.axis_index("tile")
    blocks, epochs, width = observations.shape
    local_tiles = screens.shape[0]
    layers = devices // LAYER
    local = stress.shape[1] // PBLK

    slots = LAYER * (2 * blocks // devices) * (width // CHUNK)
    sizes = round_sizes(slots)

    held = jnp.swapaxes(stress.reshape(epochs, local, PBLK), 0, 1).reshape(-1, PBLK)
    other = partner(held, devices, devices // 2)
    across_screens = partner(screens, devices, PAIR)
    obs, pix = pack(
        observations,
        pixel_geometry,
        block_counts,
        block_tiles,
        jnp.reshape(here, (1,)).astype(jnp.int32),
        devices,
        local_tiles,
    )

    def exchange(parts):
        got = [partner(parts[x], devices, x * LAYER) for x in range(layers - 1, 0, -1)]
        return [parts[0]] + got[::-1]

    other, pix = lax.optimization_barrier((other, pix))
    pix = exchange(pix)
    distance = devices // 2
    while distance >= LAYER:
        if distance < devices // 2:
            other = partner(held, devices, distance)
        held = jnp.concatenate([held, other], axis=0)
        distance //= 2
    patch_blocks = devices * local
    east, north, depth, compliance = patch_geometry
    origin = patch_geometry[:2, 0]
    strength = compliance * depth * depth
    faces = split(
        jnp.stack(
            [
                strength,
                -strength * (east - origin[0]),
                -strength * (north - origin[1]),
                strength * depth,
            ]
        )
    )
    forms = jnp.concatenate(
        [faces[second] for _, second in CROSS] + [jnp.zeros((8,) + east.shape, jnp.float32)]
    ).astype(jnp.bfloat16)
    forms = jnp.swapaxes(forms.reshape(TERMS, patch_blocks, PBLK), 0, 1)
    patches = jnp.stack([east, north, depth * depth])
    patches = jnp.swapaxes(patches.reshape(3, patch_blocks, PBLK), 0, 1)
    cutoffs = cutoff_lists.reshape(-1)
    held, pix, across_screens = lax.optimization_barrier((held, pix, across_screens))
    across_screens, forms, patches, cutoffs = lax.optimization_barrier(
        (across_screens, forms, patches, cutoffs)
    )
    got = [exchange(o) for o in obs]
    across = partner(held, devices, PAIR)
    across, got[0] = lax.optimization_barrier((across, got[0]))
    held = jnp.concatenate([held, across], axis=0)
    all_stress = [held, partner(held, devices, 1)]
    near_screens = jnp.concatenate([screens, across_screens], axis=0)
    all_screens = [near_screens, partner(near_screens, devices, 1)]

    places, spots = block_places(devices, here, patch_blocks, local, epochs)
    info = jnp.stack([p[slots, :3, :slots] for p in pix]).astype(jnp.int32).reshape(-1)
    tables = (info, cutoffs, places, spots, origin)

    state = (
        jax.ShapeDtypeStruct((patch_blocks, epochs, PBLK), jnp.float32),
        jax.ShapeDtypeStruct((LAYER * local_tiles,) + screens.shape[1:], jnp.float32),
    )
    base = 0
    for i, size in enumerate(sizes):
        first, final = i == 0, i == len(sizes) - 1
        groups = [(base, got[i], pix, base)]
        state = fit(
            tables,
            groups,
            patches,
            forms,
            all_screens,
            all_stress,
            state[:2],
            first,
            final,
        )
        if first:
            all_screens, all_stress = state[2:]
        base += size
    grad, screen_grad, given, next_door, diagonal = state
    own, far = screen_grad[:local_tiles], screen_grad[local_tiles : PAIR * local_tiles]
    there = (far + partner(diagonal, devices, 1).astype(jnp.float32)).astype(jnp.bfloat16)
    grad, back = halve(grad[: grad.shape[0] // 2], given, there, devices)
    screen_gradient = (
        own + partner(next_door, devices, 1).astype(jnp.float32) + back.astype(jnp.float32)
    )
    return (jnp.swapaxes(grad, 0, 1).reshape(epochs, local * PBLK), screen_gradient)


def solution(mesh):
    return jax.shard_map(
        on_device,
        mesh=mesh,
        in_specs=(
            P(("groups", "tile"), None, None),
            P(("groups", "tile"), None, None),
            P(("groups", "tile")),
            P(("groups", "tile")),
            P(),
            P(),
            P(None, ("groups", "tile")),
            P(("groups", "tile"), None, None),
        ),
        out_specs=(P(None, ("groups", "tile")), P(("groups", "tile"), None, None)),
        check_vma=False,
    )
```

```python
import functools

import jax
import jax.numpy as jnp
from jax import lax
from jax.experimental import pallas as pl
from jax.experimental.pallas import tpu as pltpu
from jax.sharding import PartitionSpec as P

PBLK = 256
NEAR = 3
SG = 16
CHUNK = 128
LAYER = 4
PAIR = 2
NARROW = 3
ROUNDS = (6, 10)
MIB = 1 << 20
TERMS = 32
CROSS = ((0, 0), (0, 1), (1, 0), (0, 2), (1, 1), (2, 0))


def round_sizes(slots):
    return [slots * r // sum(ROUNDS) for r in ROUNDS]


def pack_kernel(local_tiles, layers, slots, here, tiles, counts, obs_in, pix_in, *rest):
    sizes = round_sizes(slots)
    total = len(sizes)
    obs_out, pix_out = rest[: total * layers], rest[total * layers : (total + 1) * layers]
    obs, pix, obs_all, pix_all, fill, sems = rest[(total + 1) * layers :]
    loads = [
        pltpu.make_async_copy(obs_in, obs, sems.at[0]),
        pltpu.make_async_copy(pix_in, pix, sems.at[1]),
    ]
    for copy in loads:
        copy.start()
    my_layer, my_seat = lax.div(here[0], LAYER), lax.rem(here[0], LAYER)
    chunks = pix.shape[2] // CHUNK
    stride = slots + 1
    for x in range(layers):
        fill[x] = 0
    lane = lax.broadcasted_iota(jnp.int32, (8, CHUNK), 1)
    row = lax.broadcasted_iota(jnp.int32, (8, CHUNK), 0)
    for copy in loads:
        copy.wait()

    def put(b, infos):
        tile = tiles[b]
        count = counts[b]
        owner = lax.div(tile, local_tiles)
        x = lax.div(owner, LAYER) ^ my_layer
        seat = lax.rem(owner, LAYER) ^ my_seat
        spot = lax.rem(seat, PAIR) * PAIR + lax.div(seat, PAIR)
        screen = spot * local_tiles + lax.rem(tile, local_tiles)
        slot = fill[x]
        fill[x] = slot + lax.div(count + CHUNK - 1, CHUNK)
        for c in range(chunks):
            at = slot + c
            live = jnp.clip(count - c * CHUNK, 0, CHUNK)
            obs_all[x * stride + at] = obs[b, :, c * CHUNK : (c + 1) * CHUNK]
            pix_all[x * stride + at] = pix[b, :, c * CHUNK : (c + 1) * CHUNK]
            entry = jnp.where(row == 0, live, jnp.where(row == 1, tile, screen))
            here_only = (lane == at) & (row < 3)
            infos = tuple(
                jnp.where(here_only & (x == i), entry, info) for i, info in enumerate(infos)
            )
        return infos

    infos = lax.fori_loop(
        0, obs.shape[0], put, tuple(jnp.zeros((8, CHUNK), jnp.int32) for _ in range(layers))
    )
    copies = []
    for x in range(layers):
        at = x * stride
        pix_all[at + slots] = infos[x].astype(jnp.float32)
        copies.append((pix_all.at[pl.ds(at, stride)], pix_out[x]))
        for i, size in enumerate(sizes):
            copies.append((obs_all.at[pl.ds(at, size)], obs_out[i * layers + x]))
            at += size
    copies = [pltpu.make_async_copy(a, b, sems.at[i]) for i, (a, b) in enumerate(copies)]
    for copy in copies:
        copy.start()
    for copy in copies:
        copy.wait()


def pack(observations, pixel_geometry, block_counts, block_tiles, here, devices, local_tiles):
    blocks, epochs, width = observations.shape
    layers = devices // LAYER
    slots = LAYER * (2 * blocks // devices) * (width // CHUNK)
    sizes = round_sizes(slots)
    smem = pl.BlockSpec(memory_space=pltpu.SMEM)
    hbm = pl.BlockSpec(memory_space=pl.ANY)
    pix_part = jax.ShapeDtypeStruct((slots + 1, 8, CHUNK), jnp.float32)
    out = pl.pallas_call(
        functools.partial(pack_kernel, local_tiles, layers, slots),
        in_specs=[smem, smem, smem, hbm, hbm],
        out_specs=[hbm] * ((len(sizes) + 1) * layers),
        out_shape=[
            jax.ShapeDtypeStruct((size, epochs, CHUNK), observations.dtype)
            for size in sizes
            for _ in range(layers)
        ]
        + [pix_part] * layers,
        scratch_shapes=[
            pltpu.VMEM(observations.shape, observations.dtype),
            pltpu.VMEM(pixel_geometry.shape, jnp.float32),
            pltpu.VMEM((layers * (slots + 1), epochs, CHUNK), observations.dtype),
            pltpu.VMEM((layers * (slots + 1), 8, CHUNK), jnp.float32),
            pltpu.SMEM((layers,), jnp.int32),
            pltpu.SemaphoreType.DMA(((len(sizes) + 1) * layers,)),
        ],
        compiler_params=pltpu.CompilerParams(vmem_limit_bytes=10 * MIB),
        name="pack",
    )(here, block_tiles, block_counts, observations, pixel_geometry)
    rounds = len(sizes)
    return [out[i * layers : (i + 1) * layers] for i in range(rounds)], out[rounds * layers :]


def split(values):
    parts = []
    for _ in range(3):
        part = lax.reduce_precision(values, 8, 7)
        parts.append(part)
        values = values - part
    return parts


def kernel_split(values):
    parts = []
    for _ in range(3):
        part = values.astype(jnp.bfloat16).astype(jnp.float32)
        parts.append(part)
        values = values - part
    return parts


def fit_kernel(first, final, layers, slots, groups, *refs):
    info, cutoffs, places, spots, origin = refs[:5]
    rest = refs[5:]
    obs_in, pix_in = [], []
    for _ in groups:
        obs_in.append(rest[:layers])
        pix_in.append(rest[layers : 2 * layers])
        rest = rest[2 * layers :]
    patches, forms = rest[:2]
    rest = rest[1:]
    if first:
        screen_parts, stress_parts = rest[1 : 1 + LAYER], rest[1 + LAYER : 1 + 2 * LAYER]
        rest = rest[1 + 2 * LAYER :]
        grad, screen_grad, screens, stress = rest[:4]
        rest = rest[4:]
    else:
        screens, stress = rest[1:3]
        grad, screen_grad = rest[5:7]
        rest = rest[7:]
    outs = rest[:3] if final else ()
    rest = rest[len(outs) :]
    obs, pix = rest[:2]
    buffers = rest[2 : 2 + 9 * PAIR]
    wide, sights = rest[2 + 9 * PAIR : 2 + 10 * PAIR], rest[2 + 10 * PAIR : 2 + 11 * PAIR]
    items, sems = rest[2 + 11 * PAIR :]
    sets = [
        [buffers[3 * (PAIR * i + lane) : 3 * (PAIR * i + lane) + 3] for lane in range(PAIR)]
        for i in range(3)
    ]
    epochs = obs.shape[1]
    base = groups[0][0]
    span = sum(size for _, _, size in groups)
    local_tiles = screens.shape[0] // LAYER

    loads = []
    for x in range(layers):
        at = x * span
        for g, (_, low, size) in enumerate(groups):
            loads.append((obs_in[g][x], obs.at[pl.ds(at, size)]))
            loads.append((pix_in[g][x].at[pl.ds(low, size)], pix.at[pl.ds(at, size)]))
            at += size
    if first:
        for parts, whole in ((screen_parts, screens), (stress_parts, stress)):
            size = whole.shape[0] // LAYER
            for i, part in enumerate(parts):
                loads.append((part, whole.at[pl.ds(i * size, size)]))
    loads = [pltpu.make_async_copy(a, b, sems.at[i]) for i, (a, b) in enumerate(loads)]
    for copy in loads:
        copy.start()
    if first:
        grad[...] = jnp.zeros_like(grad)
        screen_grad[...] = jnp.zeros_like(screen_grad)

    def info_of(slot, kind):
        x = lax.div(slot, span)
        return info[(x * 3 + kind) * slots + base + lax.rem(slot, span)]

    def list_slot(slot, total):
        items[total] = slot
        return total + jnp.where(info_of(slot, 0) > 0, 1, 0)

    total = lax.fori_loop(0, layers * span, list_slot, 0)
    for copy in loads:
        copy.wait()

    def item_of(i):
        slot = items[jnp.minimum(i, total - 1)]
        tile = info_of(slot, 1)
        return slot, [cutoffs[tile * NEAR + k] for k in range(NEAR)]

    def spread(rows, lane):
        columns = rows.T
        for i in range(2):
            wide[lane][i] = jnp.broadcast_to(columns[:, i : i + 1], (CHUNK, CHUNK))
        le, ln = rows[4:5], rows[5:6]
        along = le * (rows[0:1] - origin[0]) + ln * (rows[1:2] - origin[1])
        row = lax.broadcasted_iota(jnp.int32, (8, CHUNK), 0)
        factors = jnp.where(
            row == 0, along, jnp.where(row == 1, le, jnp.where(row == 2, ln, rows[6:7]))
        )
        parts = kernel_split(factors)
        low = row < 4
        tiles = []
        for first_part, second_part in zip(CROSS[::2], CROSS[1::2]):
            upper = jnp.concatenate([parts[second_part[0]][:4]] * 2, axis=0)
            tiles.append(jnp.where(low, parts[first_part[0]], upper))
        tiles.append(jnp.zeros((8, CHUNK), jnp.float32))
        sights[lane][...] = jnp.concatenate(tiles, axis=0).T.astype(jnp.bfloat16)

    def make_strips(near, k, begin, end, lane, green):
        patch = [
            jnp.broadcast_to(patches[near[k], r : r + 1], (8, PBLK)) for r in range(3)
        ]
        alongs = jnp.dot(
            sights[lane][begin:end], forms[near[k]], preferred_element_type=jnp.float32
        )
        for low in range(begin, end, 16):
            along = alongs[low - begin : low - begin + 16]
            inverses = []
            for at in (low, low + 8):
                east, north = (
                    jnp.concatenate([wide[lane][i, at : at + 8]] * (PBLK // CHUNK), axis=1)
                    for i in range(2)
                )
                dx = east - patch[0]
                dy = north - patch[1]
                inverses.append(lax.rsqrt(dx * dx + dy * dy + patch[2]))
            inverse = jnp.concatenate(inverses, axis=0)
            green[low : low + 16, k * PBLK : (k + 1) * PBLK] = (
                along * inverse * inverse * inverse
            ).astype(jnp.bfloat16)

    def make_hats(rows, hats):
        node = lax.broadcasted_iota(jnp.int32, (SG, CHUNK), 0).astype(jnp.float32)
        across = jnp.maximum(0.0, 1.0 - jnp.abs(rows[2:3] - node))
        upward = jnp.maximum(0.0, 1.0 - jnp.abs(rows[3:4] - node))
        for a in range(SG):
            hats[a * SG : (a + 1) * SG] = (across[a : a + 1] * upward).astype(jnp.bfloat16)

    def make_head(i, lane, buffers):
        slot, near = item_of(i)
        rows = pix[slot]
        make_hats(rows, buffers[1])
        spread(rows, lane)
        return near

    def predict(i, buffers):
        green, hats = buffers[:2]
        slot, near = item_of(i)
        model = jnp.dot(
            screens[info_of(slot, 2)], hats[...], preferred_element_type=jnp.float32
        )
        for k in range(NEAR):
            model += lax.dot_general(
                stress[pl.ds(pl.multiple_of(spots[near[k]], 16), epochs), :],
                green[:, k * PBLK : (k + 1) * PBLK],
                (((1,), (1,)), ((), ())),
                preferred_element_type=jnp.float32,
            )
        return model

    def weigh(i, model, buffers):
        slot, _ = item_of(i)
        live = jnp.where(i < total, info_of(slot, 0), 0)
        lane = lax.broadcasted_iota(jnp.int32, (1, CHUNK), 1)
        scale = jnp.where(lane < live, pix[slot, 7:8, :], 0.0)
        buffers[2][...] = ((model - obs[slot].astype(jnp.float32)) * scale).astype(jnp.bfloat16)

    def add_patch(near, k, buffers):
        grad[places[near[k]]] += jnp.dot(
            buffers[2][...],
            buffers[0][:, k * PBLK : (k + 1) * PBLK],
            preferred_element_type=jnp.float32,
        )

    def add_screen(slot, buffers):
        screen_grad[info_of(slot, 2)] += lax.dot_general(
            buffers[2][...],
            buffers[1][...],
            (((1,), (1,)), ((), ())),
            preferred_element_type=jnp.float32,
        )

    lanes = range(PAIR)
    half = CHUNK // 2

    def make_pair(j, buffers):
        for lane in lanes:
            near = make_head(PAIR * j + lane, lane, buffers[lane])
            for k in range(NEAR):
                for low in (0, half):
                    make_strips(near, k, low, low + half, lane, buffers[lane][0])

    def model_pair(j, buffers):
        for lane in lanes:
            model = predict(PAIR * j + lane, buffers[lane])
            weigh(PAIR * j + lane, model, buffers[lane])

    def turn(j, using, middle, making):
        now = [item_of(PAIR * j + lane) for lane in lanes]
        coming = [PAIR * (j + 1) + lane for lane in lanes]
        near = [
            make_head(PAIR * (j + 2) + lane, lane, making[lane]) for lane in lanes
        ]
        models = [predict(coming[lane], middle[lane]) for lane in lanes]

        def strips(k, lane):
            for low in (0, half):
                make_strips(near[lane], k, low, low + half, lane, making[lane][0])

        def adds(k):
            for lane in lanes:
                add_patch(now[lane][1], k, using[lane])

        strips(0, 0)
        adds(0)
        strips(0, 1)
        adds(1)
        strips(1, 0)
        for lane in lanes:
            weigh(coming[lane], models[lane], middle[lane])
        strips(1, 1)
        adds(2)
        strips(2, 0)
        for lane in lanes:
            add_screen(now[lane][0], using[lane])
        strips(2, 1)

    @pl.when(total > 0)
    def _():
        pairs = lax.div(total + PAIR - 1, PAIR)
        make_pair(0, sets[0])
        make_pair(1, sets[1])
        model_pair(0, sets[0])

        def step(i, _):
            for at in range(3):
                j = 3 * i + at

                @pl.when(j < pairs)
                def _():
                    turn(j, sets[at], sets[(at + 1) % 3], sets[(at + 2) % 3])

            return 0

        lax.fori_loop(0, lax.div(pairs + 2, 3), step, 0)

    if final:
        half = grad.shape[0] // 2
        outs[0][...] = grad[half:].astype(outs[0].dtype)
        for i, out in enumerate(outs[1:]):
            low = (PAIR + i) * local_tiles
            out[...] = screen_grad[low : low + local_tiles].astype(out.dtype)


def fit(tables, groups, patches, forms, screens, stress, state, first, final):
    layers = len(groups[0][1])
    slots = tables[0].shape[0] // (3 * layers)
    smem = pl.BlockSpec(memory_space=pltpu.SMEM)
    vmem = pl.BlockSpec(memory_space=pltpu.VMEM)
    hbm = pl.BlockSpec(memory_space=pl.ANY)
    spans = tuple((base, low, obs[0].shape[0]) for base, obs, _, low in groups)
    arrays = [a for _, obs, pix, _ in groups for a in (*obs, *pix)]
    span = sum(size for _, _, size in spans)
    blocks, epochs = state[0].shape[0], state[0].shape[1]
    out_shape = [jax.ShapeDtypeStruct(a.shape, a.dtype) for a in state]
    if first:
        state = ()
        for parts in (screens, stress):
            shape = (LAYER * parts[0].shape[0],) + parts[0].shape[1:]
            out_shape.append(jax.ShapeDtypeStruct(shape, parts[0].dtype))
    else:
        screens, stress = [screens], [stress]
    if final:
        out_shape.append(jax.ShapeDtypeStruct((blocks // 2, epochs, PBLK), jnp.bfloat16))
        shape = (state[1].shape[0] // LAYER,) + state[1].shape[1:]
        out_shape += [jax.ShapeDtypeStruct(shape, jnp.bfloat16)] * 2
    before = len(tables) + len(arrays) + 2 + len(screens) + len(stress)
    return pl.pallas_call(
        functools.partial(fit_kernel, first, final, layers, slots, spans),
        in_specs=[smem] * len(tables)
        + [hbm] * len(arrays)
        + [vmem] * 2
        + [hbm if first else vmem] * (len(screens) + len(stress))
        + [vmem] * len(state),
        out_specs=[vmem] * len(out_shape),
        out_shape=out_shape,
        scratch_shapes=[
            pltpu.VMEM((layers * span, epochs, CHUNK), arrays[0].dtype),
            pltpu.VMEM((layers * span, 8, CHUNK), jnp.float32),
        ]
        + [
            pltpu.VMEM((CHUNK, NEAR * PBLK), jnp.bfloat16),
            pltpu.VMEM((SG * SG, CHUNK), jnp.bfloat16),
            pltpu.VMEM((epochs, CHUNK), jnp.bfloat16),
        ]
        * (3 * PAIR)
        + [pltpu.VMEM((2, CHUNK, CHUNK), jnp.float32)] * PAIR
        + [pltpu.VMEM((CHUNK, TERMS), jnp.bfloat16)] * PAIR
        + [
            pltpu.SMEM((layers * span + 1,), jnp.int32),
            pltpu.SemaphoreType.DMA((2 * layers * len(groups) + 2 * LAYER,)),
        ],
        input_output_aliases={} if first else {before: 0, before + 1: 1},
        compiler_params=pltpu.CompilerParams(vmem_limit_bytes=8 * MIB),
        cost_estimate=pl.CostEstimate(
            flops=layers * span * 4 * epochs * CHUNK * (NEAR + 1) * PBLK,
            bytes_accessed=1024,
            transcendentals=layers * span * CHUNK * NEAR * PBLK,
        ),
        name="fit",
    )(*tables, *arrays, patches, forms, *screens, *stress, *state)


def partner(values, devices, distance):
    return lax.ppermute(values, "tile", [(i, i ^ distance) for i in range(devices)])


def orders(devices):
    stages = devices.bit_length() - 1
    high = list(range(2, stages))
    return [1] + high, high + [1]


def block_places(devices, here, blocks, local, epochs):
    block = jnp.arange(blocks)
    other = (block // local) ^ here
    seat = block % local
    half = local // 2
    turned = []
    for order in orders(devices):
        spot = 0
        for bit in order:
            spot = spot * 2 + ((other >> bit) & 1)
        turned.append(spot)
    chips = devices // 2
    upper = seat // half
    spot = jnp.where(upper == 0, turned[0], turned[1])
    place = (((other & 1) * 2 + upper) * chips + spot) * half + seat % half
    stages = devices.bit_length() - 1
    held = sum(((other >> (stages - 1 - s)) & 1) << s for s in range(stages))
    return place.astype(jnp.int32), ((held * local + seat) * epochs).astype(jnp.int32)


def halve(kept, given, there, devices):
    total = kept + partner(given, devices, 1).astype(jnp.float32)
    middle = total.shape[0] // 2
    parts = [total[:middle], total[middle:]]
    both = orders(devices)
    stages = len(both[0])
    back = None
    for stage in range(stages):
        got = []
        for side in range(2):
            given = parts[side][parts[side].shape[0] // 2 :]
            if stages - stage <= NARROW:
                given = given.astype(jnp.bfloat16)
            got.append(partner(given, devices, 1 << both[side][stage]))
        for side in range(2):
            if side:
                _, got[1] = lax.optimization_barrier((parts[0], got[1]))
            size = parts[side].shape[0] // 2
            parts[side] = parts[side][:size] + got[side].astype(jnp.float32)
            if back is None:
                _, there = lax.optimization_barrier((parts[0], there))
                back = partner(there, devices, PAIR)
    return jnp.concatenate(parts, axis=0), back


def on_device(
    observations,
    pixel_geometry,
    block_counts,
    block_tiles,
    cutoff_lists,
    patch_geometry,
    stress,
    screens,
):
    devices = lax.axis_size("tile")
    here = lax.axis_index("tile")
    blocks, epochs, width = observations.shape
    local_tiles = screens.shape[0]
    layers = devices // LAYER
    local = stress.shape[1] // PBLK

    slots = LAYER * (2 * blocks // devices) * (width // CHUNK)
    sizes = round_sizes(slots)

    held = jnp.swapaxes(stress.reshape(epochs, local, PBLK), 0, 1).reshape(-1, PBLK)
    other = partner(held, devices, devices // 2)
    across_screens = partner(screens, devices, PAIR)
    obs, pix = pack(
        observations,
        pixel_geometry,
        block_counts,
        block_tiles,
        jnp.reshape(here, (1,)).astype(jnp.int32),
        devices,
        local_tiles,
    )

    def exchange(parts):
        got = [partner(parts[x], devices, x * LAYER) for x in range(layers - 1, 0, -1)]
        return [parts[0]] + got[::-1]

    distance = devices // 2
    while distance >= LAYER:
        if distance < devices // 2:
            other = partner(held, devices, distance)
        held = jnp.concatenate([held, other], axis=0)
        if distance == devices // 2:
            held, pix = lax.optimization_barrier((held, pix))
            pix = exchange(pix)
        distance //= 2
    patch_blocks = devices * local
    east, north, depth, compliance = patch_geometry
    origin = patch_geometry[:2, 0]
    strength = compliance * depth * depth
    faces = split(
        jnp.stack(
            [
                strength,
                -strength * (east - origin[0]),
                -strength * (north - origin[1]),
                strength * depth,
            ]
        )
    )
    forms = jnp.concatenate(
        [faces[second] for _, second in CROSS] + [jnp.zeros((8,) + east.shape, jnp.float32)]
    ).astype(jnp.bfloat16)
    forms = jnp.swapaxes(forms.reshape(TERMS, patch_blocks, PBLK), 0, 1)
    patches = jnp.stack([east, north, depth * depth])
    patches = jnp.swapaxes(patches.reshape(3, patch_blocks, PBLK), 0, 1)
    cutoffs = cutoff_lists.reshape(-1)
    held, pix, across_screens = lax.optimization_barrier((held, pix, across_screens))
    places, spots = block_places(devices, here, patch_blocks, local, epochs)
    info = jnp.stack([p[slots, :3, :slots] for p in pix]).astype(jnp.int32).reshape(-1)
    across_screens, forms, patches, cutoffs, info, places, spots = lax.optimization_barrier(
        (across_screens, forms, patches, cutoffs, info, places, spots)
    )
    got = [exchange(o) for o in obs]
    across = partner(held, devices, PAIR)
    across, got[0] = lax.optimization_barrier((across, got[0]))
    all_stress = [held, across, partner(held, devices, 1), partner(across, devices, 1)]
    all_screens = [
        screens,
        across_screens,
        partner(screens, devices, 1),
        partner(across_screens, devices, 1),
    ]

    tables = (info, cutoffs, places, spots, origin)

    state = (
        jax.ShapeDtypeStruct((patch_blocks, epochs, PBLK), jnp.float32),
        jax.ShapeDtypeStruct((LAYER * local_tiles,) + screens.shape[1:], jnp.float32),
    )
    base = 0
    for i, size in enumerate(sizes):
        first, final = i == 0, i == len(sizes) - 1
        groups = [(base, got[i], pix, base)]
        state = fit(
            tables,
            groups,
            patches,
            forms,
            all_screens,
            all_stress,
            state[:2],
            first,
            final,
        )
        if first:
            all_screens, all_stress = state[2:]
        base += size
    grad, screen_grad, given, next_door, diagonal = state
    own, far = screen_grad[:local_tiles], screen_grad[local_tiles : PAIR * local_tiles]
    there = (far + partner(diagonal, devices, 1).astype(jnp.float32)).astype(jnp.bfloat16)
    grad, back = halve(grad[: grad.shape[0] // 2], given, there, devices)
    screen_gradient = (
        own + partner(next_door, devices, 1).astype(jnp.float32) + back.astype(jnp.float32)
    )
    return (jnp.swapaxes(grad, 0, 1).reshape(epochs, local * PBLK), screen_gradient)


def solution(mesh):
    return jax.shard_map(
        on_device,
        mesh=mesh,
        in_specs=(
            P(("groups", "tile"), None, None),
            P(("groups", "tile"), None, None),
            P(("groups", "tile")),
            P(("groups", "tile")),
            P(),
            P(),
            P(None, ("groups", "tile")),
            P(("groups", "tile"), None, None),
        ),
        out_specs=(P(None, ("groups", "tile")), P(("groups", "tile"), None, None)),
        check_vma=False,
    )
```

```python
import functools

import jax
import jax.numpy as jnp
from jax import lax
from jax.experimental import pallas as pl
from jax.experimental.pallas import tpu as pltpu
from jax.sharding import PartitionSpec as P

PBLK = 256
NEAR = 3
SG = 16
CHUNK = 128
LAYER = 4
PAIR = 2
NARROW = 3
ROUNDS = (6, 6, 4)
MIB = 1 << 20
COLUMNS = (0, 1, 4, 5, 6)


def round_sizes(slots):
    return [slots * r // sum(ROUNDS) for r in ROUNDS]


def pack_kernel(local_tiles, layers, slots, here, tiles, counts, obs_in, pix_in, *rest):
    sizes = round_sizes(slots)
    total = len(sizes)
    obs_out, pix_out = rest[: total * layers], rest[total * layers : (total + 1) * layers]
    obs, pix, obs_all, pix_all, fill, sems = rest[(total + 1) * layers :]
    loads = [
        pltpu.make_async_copy(obs_in, obs, sems.at[0]),
        pltpu.make_async_copy(pix_in, pix, sems.at[1]),
    ]
    for copy in loads:
        copy.start()
    my_layer, my_seat = lax.div(here[0], LAYER), lax.rem(here[0], LAYER)
    chunks = pix.shape[2] // CHUNK
    stride = slots + 1
    for x in range(layers):
        fill[x] = 0
    lane = lax.broadcasted_iota(jnp.int32, (8, CHUNK), 1)
    row = lax.broadcasted_iota(jnp.int32, (8, CHUNK), 0)
    for copy in loads:
        copy.wait()

    def put(b, infos):
        tile = tiles[b]
        count = counts[b]
        owner = lax.div(tile, local_tiles)
        x = lax.div(owner, LAYER) ^ my_layer
        seat = lax.rem(owner, LAYER) ^ my_seat
        spot = lax.rem(seat, PAIR) * PAIR + lax.div(seat, PAIR)
        screen = spot * local_tiles + lax.rem(tile, local_tiles)
        slot = fill[x]
        fill[x] = slot + lax.div(count + CHUNK - 1, CHUNK)
        for c in range(chunks):
            at = slot + c
            live = jnp.clip(count - c * CHUNK, 0, CHUNK)
            obs_all[x * stride + at] = obs[b, :, c * CHUNK : (c + 1) * CHUNK]
            pix_all[x * stride + at] = pix[b, :, c * CHUNK : (c + 1) * CHUNK]
            entry = jnp.where(row == 0, live, jnp.where(row == 1, tile, screen))
            here_only = (lane == at) & (row < 3)
            infos = tuple(
                jnp.where(here_only & (x == i), entry, info) for i, info in enumerate(infos)
            )
        return infos

    infos = lax.fori_loop(
        0, obs.shape[0], put, tuple(jnp.zeros((8, CHUNK), jnp.int32) for _ in range(layers))
    )
    copies = []
    for x in range(layers):
        at = x * stride
        pix_all[at + slots] = infos[x].astype(jnp.float32)
        copies.append((pix_all.at[pl.ds(at, stride)], pix_out[x]))
        for i, size in enumerate(sizes):
            copies.append((obs_all.at[pl.ds(at, size)], obs_out[i * layers + x]))
            at += size
    copies = [pltpu.make_async_copy(a, b, sems.at[i]) for i, (a, b) in enumerate(copies)]
    for copy in copies:
        copy.start()
    for copy in copies:
        copy.wait()


def pack(observations, pixel_geometry, block_counts, block_tiles, here, devices, local_tiles):
    blocks, epochs, width = observations.shape
    layers = devices // LAYER
    slots = LAYER * (2 * blocks // devices) * (width // CHUNK)
    sizes = round_sizes(slots)
    smem = pl.BlockSpec(memory_space=pltpu.SMEM)
    hbm = pl.BlockSpec(memory_space=pl.ANY)
    pix_part = jax.ShapeDtypeStruct((slots + 1, 8, CHUNK), jnp.float32)
    out = pl.pallas_call(
        functools.partial(pack_kernel, local_tiles, layers, slots),
        in_specs=[smem, smem, smem, hbm, hbm],
        out_specs=[hbm] * ((len(sizes) + 1) * layers),
        out_shape=[
            jax.ShapeDtypeStruct((size, epochs, CHUNK), observations.dtype)
            for size in sizes
            for _ in range(layers)
        ]
        + [pix_part] * layers,
        scratch_shapes=[
            pltpu.VMEM(observations.shape, observations.dtype),
            pltpu.VMEM(pixel_geometry.shape, jnp.float32),
            pltpu.VMEM((layers * (slots + 1), epochs, CHUNK), observations.dtype),
            pltpu.VMEM((layers * (slots + 1), 8, CHUNK), jnp.float32),
            pltpu.SMEM((layers,), jnp.int32),
            pltpu.SemaphoreType.DMA(((len(sizes) + 1) * layers,)),
        ],
        compiler_params=pltpu.CompilerParams(vmem_limit_bytes=10 * MIB),
        name="pack",
    )(here, block_tiles, block_counts, observations, pixel_geometry)
    rounds = len(sizes)
    return [out[i * layers : (i + 1) * layers] for i in range(rounds)], out[rounds * layers :]


def fit_kernel(first, final, layers, slots, groups, *refs):
    info, cutoffs, places, spots = refs[:4]
    rest = refs[4:]
    obs_in, pix_in = [], []
    for _ in groups:
        obs_in.append(rest[:layers])
        pix_in.append(rest[layers : 2 * layers])
        rest = rest[2 * layers :]
    patches = rest[0]
    if first:
        screen_parts, stress_parts = rest[1 : 1 + LAYER], rest[1 + LAYER : 1 + 2 * LAYER]
        rest = rest[1 + 2 * LAYER :]
        grad, screen_grad, screens, stress = rest[:4]
        rest = rest[4:]
    else:
        screens, stress = rest[1:3]
        grad, screen_grad = rest[5:7]
        rest = rest[7:]
    outs = rest[:3] if final else ()
    rest = rest[len(outs) :]
    obs, pix = rest[:2]
    buffers = rest[2 : 2 + 9 * PAIR]
    wide = rest[2 + 9 * PAIR : 2 + 10 * PAIR]
    items, sems = rest[2 + 10 * PAIR :]
    sets = [
        [buffers[3 * (PAIR * i + lane) : 3 * (PAIR * i + lane) + 3] for lane in range(PAIR)]
        for i in range(3)
    ]
    epochs = obs.shape[1]
    base = groups[0][0]
    span = sum(size for _, _, size in groups)
    local_tiles = screens.shape[0] // LAYER

    loads = []
    for x in range(layers):
        at = x * span
        for g, (_, low, size) in enumerate(groups):
            loads.append((obs_in[g][x], obs.at[pl.ds(at, size)]))
            loads.append((pix_in[g][x].at[pl.ds(low, size)], pix.at[pl.ds(at, size)]))
            at += size
    if first:
        for parts, whole in ((screen_parts, screens), (stress_parts, stress)):
            size = whole.shape[0] // LAYER
            for i, part in enumerate(parts):
                loads.append((part, whole.at[pl.ds(i * size, size)]))
    loads = [pltpu.make_async_copy(a, b, sems.at[i]) for i, (a, b) in enumerate(loads)]
    for copy in loads:
        copy.start()
    if first:
        grad[...] = jnp.zeros_like(grad)
        screen_grad[...] = jnp.zeros_like(screen_grad)

    def info_of(slot, kind):
        x = lax.div(slot, span)
        return info[(x * 3 + kind) * slots + base + lax.rem(slot, span)]

    def list_slot(slot, total):
        items[total] = slot
        return total + jnp.where(info_of(slot, 0) > 0, 1, 0)

    total = lax.fori_loop(0, layers * span, list_slot, 0)
    for copy in loads:
        copy.wait()

    def item_of(i):
        slot = items[jnp.minimum(i, total - 1)]
        tile = info_of(slot, 1)
        return slot, [cutoffs[tile * NEAR + k] for k in range(NEAR)]

    def spread(rows, lane):
        columns = rows.T
        for i, c in enumerate(COLUMNS):
            wide[lane][i] = jnp.broadcast_to(columns[:, c : c + 1], (CHUNK, CHUNK))

    def make_strips(near, k, begin, end, lane, green):
        patch = [
            jnp.broadcast_to(patches[near[k], r : r + 1], (8, PBLK)) for r in range(5)
        ]
        for low in range(begin, end, 16):
            strips = []
            for at in (low, low + 8):
                east, north, le, ln, lu = (
                    jnp.concatenate([wide[lane][i, at : at + 8]] * (PBLK // CHUNK), axis=1)
                    for i in range(len(COLUMNS))
                )
                dx = east - patch[0]
                dy = north - patch[1]
                inverse = lax.rsqrt(dx * dx + dy * dy + patch[3])
                along = le * dx + ln * dy + lu * patch[2]
                strips.append(patch[4] * along * inverse * inverse * inverse)
            green[low : low + 16, k * PBLK : (k + 1) * PBLK] = jnp.concatenate(
                strips, axis=0
            ).astype(jnp.bfloat16)

    def make_hats(rows, hats):
        node = lax.broadcasted_iota(jnp.int32, (SG, CHUNK), 0).astype(jnp.float32)
        across = jnp.maximum(0.0, 1.0 - jnp.abs(rows[2:3] - node))
        upward = jnp.maximum(0.0, 1.0 - jnp.abs(rows[3:4] - node))
        for a in range(SG):
            hats[a * SG : (a + 1) * SG] = (across[a : a + 1] * upward).astype(jnp.bfloat16)

    def make_head(i, lane, buffers):
        slot, near = item_of(i)
        rows = pix[slot]
        make_hats(rows, buffers[1])
        spread(rows, lane)
        return near

    def predict(i, buffers):
        green, hats = buffers[:2]
        slot, near = item_of(i)
        model = jnp.dot(
            screens[info_of(slot, 2)], hats[...], preferred_element_type=jnp.float32
        )
        for k in range(NEAR):
            model += lax.dot_general(
                stress[pl.ds(pl.multiple_of(spots[near[k]], 16), epochs), :],
                green[:, k * PBLK : (k + 1) * PBLK],
                (((1,), (1,)), ((), ())),
                preferred_element_type=jnp.float32,
            )
        return model

    def weigh(i, model, buffers):
        slot, _ = item_of(i)
        live = jnp.where(i < total, info_of(slot, 0), 0)
        lane = lax.broadcasted_iota(jnp.int32, (1, CHUNK), 1)
        scale = jnp.where(lane < live, pix[slot, 7:8, :], 0.0)
        buffers[2][...] = ((model - obs[slot].astype(jnp.float32)) * scale).astype(jnp.bfloat16)

    def add_patch(near, k, buffers):
        grad[places[near[k]]] += jnp.dot(
            buffers[2][...],
            buffers[0][:, k * PBLK : (k + 1) * PBLK],
            preferred_element_type=jnp.float32,
        )

    def add_screen(slot, buffers):
        screen_grad[info_of(slot, 2)] += lax.dot_general(
            buffers[2][...],
            buffers[1][...],
            (((1,), (1,)), ((), ())),
            preferred_element_type=jnp.float32,
        )

    lanes = range(PAIR)
    half = CHUNK // 2

    def make_pair(j, buffers):
        for lane in lanes:
            near = make_head(PAIR * j + lane, lane, buffers[lane])
            for k in range(NEAR):
                for low in (0, half):
                    make_strips(near, k, low, low + half, lane, buffers[lane][0])

    def model_pair(j, buffers):
        for lane in lanes:
            model = predict(PAIR * j + lane, buffers[lane])
            weigh(PAIR * j + lane, model, buffers[lane])

    def turn(j, using, middle, making):
        now = [item_of(PAIR * j + lane) for lane in lanes]
        coming = [PAIR * (j + 1) + lane for lane in lanes]
        near = [
            make_head(PAIR * (j + 2) + lane, lane, making[lane]) for lane in lanes
        ]
        models = [predict(coming[lane], middle[lane]) for lane in lanes]

        def strips(k, lane):
            for low in (0, half):
                make_strips(near[lane], k, low, low + half, lane, making[lane][0])

        def adds(k):
            for lane in lanes:
                add_patch(now[lane][1], k, using[lane])

        strips(0, 0)
        adds(0)
        strips(0, 1)
        adds(1)
        strips(1, 0)
        for lane in lanes:
            weigh(coming[lane], models[lane], middle[lane])
        strips(1, 1)
        adds(2)
        strips(2, 0)
        for lane in lanes:
            add_screen(now[lane][0], using[lane])
        strips(2, 1)

    @pl.when(total > 0)
    def _():
        pairs = lax.div(total + PAIR - 1, PAIR)
        make_pair(0, sets[0])
        make_pair(1, sets[1])
        model_pair(0, sets[0])

        def step(i, _):
            for at in range(3):
                j = 3 * i + at

                @pl.when(j < pairs)
                def _():
                    turn(j, sets[at], sets[(at + 1) % 3], sets[(at + 2) % 3])

            return 0

        lax.fori_loop(0, lax.div(pairs + 2, 3), step, 0)

    if final:
        half = grad.shape[0] // 2
        outs[0][...] = grad[half:].astype(outs[0].dtype)
        for i, out in enumerate(outs[1:]):
            low = (PAIR + i) * local_tiles
            out[...] = screen_grad[low : low + local_tiles].astype(out.dtype)


def fit(tables, groups, patches, screens, stress, state, first, final):
    layers = len(groups[0][1])
    slots = tables[0].shape[0] // (3 * layers)
    smem = pl.BlockSpec(memory_space=pltpu.SMEM)
    vmem = pl.BlockSpec(memory_space=pltpu.VMEM)
    hbm = pl.BlockSpec(memory_space=pl.ANY)
    spans = tuple((base, low, obs[0].shape[0]) for base, obs, _, low in groups)
    arrays = [a for _, obs, pix, _ in groups for a in (*obs, *pix)]
    span = sum(size for _, _, size in spans)
    blocks, epochs = state[0].shape[0], state[0].shape[1]
    out_shape = [jax.ShapeDtypeStruct(a.shape, a.dtype) for a in state]
    if first:
        state = ()
        for parts in (screens, stress):
            shape = (LAYER * parts[0].shape[0],) + parts[0].shape[1:]
            out_shape.append(jax.ShapeDtypeStruct(shape, parts[0].dtype))
    else:
        screens, stress = [screens], [stress]
    if final:
        out_shape.append(jax.ShapeDtypeStruct((blocks // 2, epochs, PBLK), jnp.bfloat16))
        shape = (state[1].shape[0] // LAYER,) + state[1].shape[1:]
        out_shape += [jax.ShapeDtypeStruct(shape, jnp.bfloat16)] * 2
    before = len(tables) + len(arrays) + 1 + len(screens) + len(stress)
    return pl.pallas_call(
        functools.partial(fit_kernel, first, final, layers, slots, spans),
        in_specs=[smem] * len(tables)
        + [hbm] * len(arrays)
        + [vmem]
        + [hbm if first else vmem] * (len(screens) + len(stress))
        + [vmem] * len(state),
        out_specs=[vmem] * len(out_shape),
        out_shape=out_shape,
        scratch_shapes=[
            pltpu.VMEM((layers * span, epochs, CHUNK), arrays[0].dtype),
            pltpu.VMEM((layers * span, 8, CHUNK), jnp.float32),
        ]
        + [
            pltpu.VMEM((CHUNK, NEAR * PBLK), jnp.bfloat16),
            pltpu.VMEM((SG * SG, CHUNK), jnp.bfloat16),
            pltpu.VMEM((epochs, CHUNK), jnp.bfloat16),
        ]
        * (3 * PAIR)
        + [pltpu.VMEM((len(COLUMNS), CHUNK, CHUNK), jnp.float32)] * PAIR
        + [
            pltpu.SMEM((layers * span + 1,), jnp.int32),
            pltpu.SemaphoreType.DMA((2 * layers * len(groups) + 2 * LAYER,)),
        ],
        input_output_aliases={} if first else {before: 0, before + 1: 1},
        compiler_params=pltpu.CompilerParams(vmem_limit_bytes=8 * MIB),
        cost_estimate=pl.CostEstimate(
            flops=layers * span * 4 * epochs * CHUNK * (NEAR + 1) * PBLK,
            bytes_accessed=1024,
            transcendentals=layers * span * CHUNK * NEAR * PBLK,
        ),
        name="fit",
    )(*tables, *arrays, patches, *screens, *stress, *state)


def partner(values, devices, distance):
    return lax.ppermute(values, "tile", [(i, i ^ distance) for i in range(devices)])


def orders(devices):
    stages = devices.bit_length() - 1
    high = list(range(2, stages))
    return [1] + high, high + [1]


def block_places(devices, here, blocks, local, epochs):
    block = jnp.arange(blocks)
    other = (block // local) ^ here
    seat = block % local
    half = local // 2
    turned = []
    for order in orders(devices):
        spot = 0
        for bit in order:
            spot = spot * 2 + ((other >> bit) & 1)
        turned.append(spot)
    chips = devices // 2
    upper = seat // half
    spot = jnp.where(upper == 0, turned[0], turned[1])
    place = (((other & 1) * 2 + upper) * chips + spot) * half + seat % half
    stages = devices.bit_length() - 1
    held = sum(((other >> (stages - 1 - s)) & 1) << s for s in range(stages))
    return place.astype(jnp.int32), ((held * local + seat) * epochs).astype(jnp.int32)


def halve(kept, given, there, devices):
    total = kept + partner(given, devices, 1).astype(jnp.float32)
    middle = total.shape[0] // 2
    parts = [total[:middle], total[middle:]]
    both = orders(devices)
    stages = len(both[0])
    back = None
    for stage in range(stages):
        got = []
        for side in range(2):
            given = parts[side][parts[side].shape[0] // 2 :]
            if stages - stage <= NARROW:
                given = given.astype(jnp.bfloat16)
            got.append(partner(given, devices, 1 << both[side][stage]))
        for side in range(2):
            if side:
                _, got[1] = lax.optimization_barrier((parts[0], got[1]))
            size = parts[side].shape[0] // 2
            parts[side] = parts[side][:size] + got[side].astype(jnp.float32)
            if back is None:
                _, there = lax.optimization_barrier((parts[0], there))
                back = partner(there, devices, PAIR)
    return jnp.concatenate(parts, axis=0), back


def on_device(
    observations,
    pixel_geometry,
    block_counts,
    block_tiles,
    cutoff_lists,
    patch_geometry,
    stress,
    screens,
):
    devices = lax.axis_size("tile")
    here = lax.axis_index("tile")
    blocks, epochs, width = observations.shape
    local_tiles = screens.shape[0]
    layers = devices // LAYER
    local = stress.shape[1] // PBLK

    slots = LAYER * (2 * blocks // devices) * (width // CHUNK)
    sizes = round_sizes(slots)

    held = jnp.swapaxes(stress.reshape(epochs, local, PBLK), 0, 1).reshape(-1, PBLK)
    other = partner(held, devices, devices // 2)
    across_screens = partner(screens, devices, PAIR)
    obs, pix = pack(
        observations,
        pixel_geometry,
        block_counts,
        block_tiles,
        jnp.reshape(here, (1,)).astype(jnp.int32),
        devices,
        local_tiles,
    )

    def exchange(parts):
        got = [partner(parts[x], devices, x * LAYER) for x in range(layers - 1, 0, -1)]
        return [parts[0]] + got[::-1]

    distance = devices // 2
    while distance >= LAYER:
        if distance < devices // 2:
            other = partner(held, devices, distance)
        held = jnp.concatenate([held, other], axis=0)
        if distance == devices // 2:
            held, pix = lax.optimization_barrier((held, pix))
            pix = exchange(pix)
        distance //= 2
    patch_blocks = devices * local
    east, north, depth, compliance = patch_geometry
    patches = jnp.stack([east, north, depth, depth * depth, compliance * depth * depth])
    patches = jnp.swapaxes(patches.reshape(5, patch_blocks, PBLK), 0, 1)
    cutoffs = cutoff_lists.reshape(-1)
    held, pix, across_screens = lax.optimization_barrier((held, pix, across_screens))
    places, spots = block_places(devices, here, patch_blocks, local, epochs)
    info = jnp.stack([p[slots, :3, :slots] for p in pix]).astype(jnp.int32).reshape(-1)
    across_screens, patches, cutoffs, info, places, spots = lax.optimization_barrier(
        (across_screens, patches, cutoffs, info, places, spots)
    )
    got = [exchange(o) for o in obs]
    across = partner(held, devices, PAIR)
    across, got[0] = lax.optimization_barrier((across, got[0]))
    all_stress = [held, across, partner(held, devices, 1), partner(across, devices, 1)]
    all_screens = [
        screens,
        across_screens,
        partner(screens, devices, 1),
        partner(across_screens, devices, 1),
    ]

    tables = (info, cutoffs, places, spots)

    state = (
        jax.ShapeDtypeStruct((patch_blocks, epochs, PBLK), jnp.float32),
        jax.ShapeDtypeStruct((LAYER * local_tiles,) + screens.shape[1:], jnp.float32),
    )
    base = 0
    for i, size in enumerate(sizes):
        first, final = i == 0, i == len(sizes) - 1
        groups = [(base, got[i], pix, base)]
        state = fit(
            tables,
            groups,
            patches,
            all_screens,
            all_stress,
            state[:2],
            first,
            final,
        )
        if first:
            all_screens, all_stress = state[2:]
        base += size
    grad, screen_grad, given, next_door, diagonal = state
    own, far = screen_grad[:local_tiles], screen_grad[local_tiles : PAIR * local_tiles]
    there = (far + partner(diagonal, devices, 1).astype(jnp.float32)).astype(jnp.bfloat16)
    grad, back = halve(grad[: grad.shape[0] // 2], given, there, devices)
    screen_gradient = (
        own + partner(next_door, devices, 1).astype(jnp.float32) + back.astype(jnp.float32)
    )
    return (jnp.swapaxes(grad, 0, 1).reshape(epochs, local * PBLK), screen_gradient)


def solution(mesh):
    return jax.shard_map(
        on_device,
        mesh=mesh,
        in_specs=(
            P(("groups", "tile"), None, None),
            P(("groups", "tile"), None, None),
            P(("groups", "tile")),
            P(("groups", "tile")),
            P(),
            P(),
            P(None, ("groups", "tile")),
            P(("groups", "tile"), None, None),
        ),
        out_specs=(P(None, ("groups", "tile")), P(("groups", "tile"), None, None)),
        check_vma=False,
    )
```

```python
import functools

import jax
import jax.numpy as jnp
from jax import lax
from jax.experimental import pallas as pl
from jax.experimental.pallas import tpu as pltpu
from jax.sharding import PartitionSpec as P

PBLK = 256
NEAR = 3
SG = 16
CHUNK = 128
LAYER = 4
PAIR = 2
NARROW = 3
ROUNDS = (6, 6, 4)
MIB = 1 << 20
TERMS = 32
CROSS = ((0, 0), (0, 1), (1, 0), (0, 2), (1, 1), (2, 0))


def round_sizes(slots):
    return [slots * r // sum(ROUNDS) for r in ROUNDS]


def pack_kernel(local_tiles, layers, slots, here, tiles, counts, obs_in, pix_in, *rest):
    sizes = round_sizes(slots)
    total = len(sizes)
    obs_out, pix_out = rest[: total * layers], rest[total * layers : (total + 1) * layers]
    obs, pix, obs_all, pix_all, fill, sems = rest[(total + 1) * layers :]
    loads = [
        pltpu.make_async_copy(obs_in, obs, sems.at[0]),
        pltpu.make_async_copy(pix_in, pix, sems.at[1]),
    ]
    for copy in loads:
        copy.start()
    my_layer, my_seat = lax.div(here[0], LAYER), lax.rem(here[0], LAYER)
    chunks = pix.shape[2] // CHUNK
    stride = slots + 1
    for x in range(layers):
        fill[x] = 0
    lane = lax.broadcasted_iota(jnp.int32, (8, CHUNK), 1)
    row = lax.broadcasted_iota(jnp.int32, (8, CHUNK), 0)
    for copy in loads:
        copy.wait()

    def put(b, infos):
        tile = tiles[b]
        count = counts[b]
        owner = lax.div(tile, local_tiles)
        x = lax.div(owner, LAYER) ^ my_layer
        seat = lax.rem(owner, LAYER) ^ my_seat
        spot = lax.rem(seat, PAIR) * PAIR + lax.div(seat, PAIR)
        screen = spot * local_tiles + lax.rem(tile, local_tiles)
        slot = fill[x]
        fill[x] = slot + lax.div(count + CHUNK - 1, CHUNK)
        for c in range(chunks):
            at = slot + c
            live = jnp.clip(count - c * CHUNK, 0, CHUNK)
            obs_all[x * stride + at] = obs[b, :, c * CHUNK : (c + 1) * CHUNK]
            pix_all[x * stride + at] = pix[b, :, c * CHUNK : (c + 1) * CHUNK]
            entry = jnp.where(row == 0, live, jnp.where(row == 1, tile, screen))
            here_only = (lane == at) & (row < 3)
            infos = tuple(
                jnp.where(here_only & (x == i), entry, info) for i, info in enumerate(infos)
            )
        return infos

    infos = lax.fori_loop(
        0, obs.shape[0], put, tuple(jnp.zeros((8, CHUNK), jnp.int32) for _ in range(layers))
    )
    copies = []
    for x in range(layers):
        at = x * stride
        pix_all[at + slots] = infos[x].astype(jnp.float32)
        copies.append((pix_all.at[pl.ds(at, stride)], pix_out[x]))
        for i, size in enumerate(sizes):
            copies.append((obs_all.at[pl.ds(at, size)], obs_out[i * layers + x]))
            at += size
    copies = [pltpu.make_async_copy(a, b, sems.at[i]) for i, (a, b) in enumerate(copies)]
    for copy in copies:
        copy.start()
    for copy in copies:
        copy.wait()


def pack(observations, pixel_geometry, block_counts, block_tiles, here, devices, local_tiles):
    blocks, epochs, width = observations.shape
    layers = devices // LAYER
    slots = LAYER * (2 * blocks // devices) * (width // CHUNK)
    sizes = round_sizes(slots)
    smem = pl.BlockSpec(memory_space=pltpu.SMEM)
    hbm = pl.BlockSpec(memory_space=pl.ANY)
    pix_part = jax.ShapeDtypeStruct((slots + 1, 8, CHUNK), jnp.float32)
    out = pl.pallas_call(
        functools.partial(pack_kernel, local_tiles, layers, slots),
        in_specs=[smem, smem, smem, hbm, hbm],
        out_specs=[hbm] * ((len(sizes) + 1) * layers),
        out_shape=[
            jax.ShapeDtypeStruct((size, epochs, CHUNK), observations.dtype)
            for size in sizes
            for _ in range(layers)
        ]
        + [pix_part] * layers,
        scratch_shapes=[
            pltpu.VMEM(observations.shape, observations.dtype),
            pltpu.VMEM(pixel_geometry.shape, jnp.float32),
            pltpu.VMEM((layers * (slots + 1), epochs, CHUNK), observations.dtype),
            pltpu.VMEM((layers * (slots + 1), 8, CHUNK), jnp.float32),
            pltpu.SMEM((layers,), jnp.int32),
            pltpu.SemaphoreType.DMA(((len(sizes) + 1) * layers,)),
        ],
        compiler_params=pltpu.CompilerParams(vmem_limit_bytes=10 * MIB),
        name="pack",
    )(here, block_tiles, block_counts, observations, pixel_geometry)
    rounds = len(sizes)
    return [out[i * layers : (i + 1) * layers] for i in range(rounds)], out[rounds * layers :]


def split(values):
    parts = []
    for _ in range(3):
        part = lax.reduce_precision(values, 8, 7)
        parts.append(part)
        values = values - part
    return parts


def kernel_split(values):
    parts = []
    for _ in range(3):
        part = values.astype(jnp.bfloat16).astype(jnp.float32)
        parts.append(part)
        values = values - part
    return parts


def fit_kernel(first, final, layers, slots, groups, *refs):
    info, cutoffs, places, spots, origin = refs[:5]
    rest = refs[5:]
    obs_in, pix_in = [], []
    for _ in groups:
        obs_in.append(rest[:layers])
        pix_in.append(rest[layers : 2 * layers])
        rest = rest[2 * layers :]
    patches, forms = rest[:2]
    rest = rest[1:]
    if first:
        screen_parts, stress_parts = rest[1 : 1 + LAYER], rest[1 + LAYER : 1 + 2 * LAYER]
        rest = rest[1 + 2 * LAYER :]
        grad, screen_grad, screens, stress = rest[:4]
        rest = rest[4:]
    else:
        screens, stress = rest[1:3]
        grad, screen_grad = rest[5:7]
        rest = rest[7:]
    outs = rest[:3] if final else ()
    rest = rest[len(outs) :]
    obs, pix = rest[:2]
    buffers = rest[2 : 2 + 15 * PAIR]
    items, sems = rest[2 + 15 * PAIR :]
    sets = [
        [buffers[5 * (PAIR * i + lane) : 5 * (PAIR * i + lane) + 5] for lane in range(PAIR)]
        for i in range(3)
    ]
    epochs = obs.shape[1]
    base = groups[0][0]
    span = sum(size for _, _, size in groups)
    local_tiles = screens.shape[0] // LAYER

    loads = []
    for x in range(layers):
        at = x * span
        for g, (_, low, size) in enumerate(groups):
            loads.append((obs_in[g][x], obs.at[pl.ds(at, size)]))
            loads.append((pix_in[g][x].at[pl.ds(low, size)], pix.at[pl.ds(at, size)]))
            at += size
    if first:
        for parts, whole in ((screen_parts, screens), (stress_parts, stress)):
            size = whole.shape[0] // LAYER
            for i, part in enumerate(parts):
                loads.append((part, whole.at[pl.ds(i * size, size)]))
    loads = [pltpu.make_async_copy(a, b, sems.at[i]) for i, (a, b) in enumerate(loads)]
    for copy in loads:
        copy.start()
    if first:
        grad[...] = jnp.zeros_like(grad)
        screen_grad[...] = jnp.zeros_like(screen_grad)

    def info_of(slot, kind):
        x = lax.div(slot, span)
        return info[(x * 3 + kind) * slots + base + lax.rem(slot, span)]

    def list_slot(slot, total):
        items[total] = slot
        return total + jnp.where(info_of(slot, 0) > 0, 1, 0)

    total = lax.fori_loop(0, layers * span, list_slot, 0)
    for copy in loads:
        copy.wait()

    def item_of(i):
        slot = items[jnp.minimum(i, total - 1)]
        tile = info_of(slot, 1)
        return slot, [cutoffs[tile * NEAR + k] for k in range(NEAR)]

    def spread(i, held):
        rows = pix[item_of(i)[0]]
        columns = rows.T
        for i in range(2):
            held[0][i] = jnp.broadcast_to(columns[:, i : i + 1], (CHUNK, CHUNK))
        le, ln = rows[4:5], rows[5:6]
        along = le * (rows[0:1] - origin[0]) + ln * (rows[1:2] - origin[1])
        row = lax.broadcasted_iota(jnp.int32, (8, CHUNK), 0)
        factors = jnp.where(
            row == 0, along, jnp.where(row == 1, le, jnp.where(row == 2, ln, rows[6:7]))
        )
        parts = kernel_split(factors)
        low = row < 4
        tiles = []
        for first_part, second_part in zip(CROSS[::2], CROSS[1::2]):
            upper = jnp.concatenate([parts[second_part[0]][:4]] * 2, axis=0)
            tiles.append(jnp.where(low, parts[first_part[0]], upper))
        tiles.append(jnp.zeros((8, CHUNK), jnp.float32))
        held[1][...] = jnp.concatenate(tiles, axis=0).T.astype(jnp.bfloat16)

    def make_strips(near, k, begin, end, held, green):
        patch = [
            jnp.broadcast_to(patches[near[k], r : r + 1], (8, PBLK)) for r in range(3)
        ]
        alongs = jnp.dot(
            held[1][begin:end], forms[near[k]], preferred_element_type=jnp.float32
        )
        for low in range(begin, end, 16):
            along = alongs[low - begin : low - begin + 16]
            inverses = []
            for at in (low, low + 8):
                east, north = (
                    jnp.concatenate([held[0][i, at : at + 8]] * (PBLK // CHUNK), axis=1)
                    for i in range(2)
                )
                dx = east - patch[0]
                dy = north - patch[1]
                inverses.append(lax.rsqrt(dx * dx + dy * dy + patch[2]))
            inverse = jnp.concatenate(inverses, axis=0)
            green[low : low + 16, k * PBLK : (k + 1) * PBLK] = (
                along * inverse * inverse * inverse
            ).astype(jnp.bfloat16)

    def make_hats(rows, hats):
        node = lax.broadcasted_iota(jnp.int32, (SG, CHUNK), 0).astype(jnp.float32)
        across = jnp.maximum(0.0, 1.0 - jnp.abs(rows[2:3] - node))
        upward = jnp.maximum(0.0, 1.0 - jnp.abs(rows[3:4] - node))
        for a in range(SG):
            hats[a * SG : (a + 1) * SG] = (across[a : a + 1] * upward).astype(jnp.bfloat16)

    def make_head(i, buffers):
        slot, near = item_of(i)
        make_hats(pix[slot], buffers[1])
        return near

    def predict(i, buffers):
        green, hats = buffers[:2]
        slot, near = item_of(i)
        model = jnp.dot(
            screens[info_of(slot, 2)], hats[...], preferred_element_type=jnp.float32
        )
        for k in range(NEAR):
            model += lax.dot_general(
                stress[pl.ds(pl.multiple_of(spots[near[k]], 16), epochs), :],
                green[:, k * PBLK : (k + 1) * PBLK],
                (((1,), (1,)), ((), ())),
                preferred_element_type=jnp.float32,
            )
        return model

    def weigh(i, model, buffers):
        slot, _ = item_of(i)
        live = jnp.where(i < total, info_of(slot, 0), 0)
        lane = lax.broadcasted_iota(jnp.int32, (1, CHUNK), 1)
        scale = jnp.where(lane < live, pix[slot, 7:8, :], 0.0)
        buffers[2][...] = ((model - obs[slot].astype(jnp.float32)) * scale).astype(jnp.bfloat16)

    def add_patch(near, k, buffers):
        grad[places[near[k]]] += jnp.dot(
            buffers[2][...],
            buffers[0][:, k * PBLK : (k + 1) * PBLK],
            preferred_element_type=jnp.float32,
        )

    def add_screen(slot, buffers):
        screen_grad[info_of(slot, 2)] += lax.dot_general(
            buffers[2][...],
            buffers[1][...],
            (((1,), (1,)), ((), ())),
            preferred_element_type=jnp.float32,
        )

    lanes = range(PAIR)
    half = CHUNK // 2

    def spread_pair(j, buffers):
        for lane in lanes:
            spread(PAIR * j + lane, buffers[lane][3:])

    def make_pair(j, buffers):
        for lane in lanes:
            near = make_head(PAIR * j + lane, buffers[lane])
            for k in range(NEAR):
                for low in (0, half):
                    make_strips(near, k, low, low + half, buffers[lane][3:], buffers[lane][0])

    def model_pair(j, buffers):
        for lane in lanes:
            model = predict(PAIR * j + lane, buffers[lane])
            weigh(PAIR * j + lane, model, buffers[lane])

    def turn(j, using, middle, making):
        now = [item_of(PAIR * j + lane) for lane in lanes]
        coming = [PAIR * (j + 1) + lane for lane in lanes]
        near = [make_head(PAIR * (j + 2) + lane, making[lane]) for lane in lanes]
        models = [predict(coming[lane], middle[lane]) for lane in lanes]

        def strips(k, lane):
            for low in (0, half):
                make_strips(
                    near[lane], k, low, low + half, making[lane][3:], making[lane][0]
                )

        def adds(k):
            for lane in lanes:
                add_patch(now[lane][1], k, using[lane])

        strips(0, 0)
        adds(0)
        spread_pair(j + 3, using)
        strips(0, 1)
        adds(1)
        strips(1, 0)
        for lane in lanes:
            weigh(coming[lane], models[lane], middle[lane])
        strips(1, 1)
        adds(2)
        strips(2, 0)
        for lane in lanes:
            add_screen(now[lane][0], using[lane])
        strips(2, 1)

    @pl.when(total > 0)
    def _():
        pairs = lax.div(total + PAIR - 1, PAIR)
        for j in range(3):
            spread_pair(j, sets[j])
        make_pair(0, sets[0])
        make_pair(1, sets[1])
        model_pair(0, sets[0])

        def step(i, _):
            for at in range(3):
                j = 3 * i + at

                @pl.when(j < pairs)
                def _():
                    turn(j, sets[at], sets[(at + 1) % 3], sets[(at + 2) % 3])

            return 0

        lax.fori_loop(0, lax.div(pairs + 2, 3), step, 0)

    if final:
        half = grad.shape[0] // 2
        outs[0][...] = grad[half:].astype(outs[0].dtype)
        for i, out in enumerate(outs[1:]):
            low = (PAIR + i) * local_tiles
            out[...] = screen_grad[low : low + local_tiles].astype(out.dtype)


def fit(tables, groups, patches, forms, screens, stress, state, first, final):
    layers = len(groups[0][1])
    slots = tables[0].shape[0] // (3 * layers)
    smem = pl.BlockSpec(memory_space=pltpu.SMEM)
    vmem = pl.BlockSpec(memory_space=pltpu.VMEM)
    hbm = pl.BlockSpec(memory_space=pl.ANY)
    spans = tuple((base, low, obs[0].shape[0]) for base, obs, _, low in groups)
    arrays = [a for _, obs, pix, _ in groups for a in (*obs, *pix)]
    span = sum(size for _, _, size in spans)
    blocks, epochs = state[0].shape[0], state[0].shape[1]
    out_shape = [jax.ShapeDtypeStruct(a.shape, a.dtype) for a in state]
    if first:
        state = ()
        for parts in (screens, stress):
            shape = (LAYER * parts[0].shape[0],) + parts[0].shape[1:]
            out_shape.append(jax.ShapeDtypeStruct(shape, parts[0].dtype))
    else:
        screens, stress = [screens], [stress]
    if final:
        out_shape.append(jax.ShapeDtypeStruct((blocks // 2, epochs, PBLK), jnp.bfloat16))
        shape = (state[1].shape[0] // LAYER,) + state[1].shape[1:]
        out_shape += [jax.ShapeDtypeStruct(shape, jnp.bfloat16)] * 2
    before = len(tables) + len(arrays) + 2 + len(screens) + len(stress)
    return pl.pallas_call(
        functools.partial(fit_kernel, first, final, layers, slots, spans),
        in_specs=[smem] * len(tables)
        + [hbm] * len(arrays)
        + [vmem] * 2
        + [hbm if first else vmem] * (len(screens) + len(stress))
        + [vmem] * len(state),
        out_specs=[vmem] * len(out_shape),
        out_shape=out_shape,
        scratch_shapes=[
            pltpu.VMEM((layers * span, epochs, CHUNK), arrays[0].dtype),
            pltpu.VMEM((layers * span, 8, CHUNK), jnp.float32),
        ]
        + [
            pltpu.VMEM((CHUNK, NEAR * PBLK), jnp.bfloat16),
            pltpu.VMEM((SG * SG, CHUNK), jnp.bfloat16),
            pltpu.VMEM((epochs, CHUNK), jnp.bfloat16),
            pltpu.VMEM((2, CHUNK, CHUNK), jnp.float32),
            pltpu.VMEM((CHUNK, TERMS), jnp.bfloat16),
        ]
        * (3 * PAIR)
        + [
            pltpu.SMEM((layers * span + 1,), jnp.int32),
            pltpu.SemaphoreType.DMA((2 * layers * len(groups) + 2 * LAYER,)),
        ],
        input_output_aliases={} if first else {before: 0, before + 1: 1},
        compiler_params=pltpu.CompilerParams(vmem_limit_bytes=8 * MIB),
        cost_estimate=pl.CostEstimate(
            flops=layers * span * 4 * epochs * CHUNK * (NEAR + 1) * PBLK,
            bytes_accessed=1024,
            transcendentals=layers * span * CHUNK * NEAR * PBLK,
        ),
        name="fit",
    )(*tables, *arrays, patches, forms, *screens, *stress, *state)


def partner(values, devices, distance):
    return lax.ppermute(values, "tile", [(i, i ^ distance) for i in range(devices)])


def orders(devices):
    stages = devices.bit_length() - 1
    high = list(range(2, stages))
    return [1] + high, high + [1]


def block_places(devices, here, blocks, local, epochs):
    block = jnp.arange(blocks)
    other = (block // local) ^ here
    seat = block % local
    half = local // 2
    turned = []
    for order in orders(devices):
        spot = 0
        for bit in order:
            spot = spot * 2 + ((other >> bit) & 1)
        turned.append(spot)
    chips = devices // 2
    upper = seat // half
    spot = jnp.where(upper == 0, turned[0], turned[1])
    place = (((other & 1) * 2 + upper) * chips + spot) * half + seat % half
    stages = devices.bit_length() - 1
    held = sum(((other >> (stages - 1 - s)) & 1) << s for s in range(stages))
    return place.astype(jnp.int32), ((held * local + seat) * epochs).astype(jnp.int32)


def halve(kept, given, there, devices):
    total = kept + partner(given, devices, 1).astype(jnp.float32)
    middle = total.shape[0] // 2
    parts = [total[:middle], total[middle:]]
    both = orders(devices)
    stages = len(both[0])
    back = None
    for stage in range(stages):
        got = []
        for side in range(2):
            given = parts[side][parts[side].shape[0] // 2 :]
            if stages - stage <= NARROW:
                given = given.astype(jnp.bfloat16)
            got.append(partner(given, devices, 1 << both[side][stage]))
        for side in range(2):
            if side:
                _, got[1] = lax.optimization_barrier((parts[0], got[1]))
            size = parts[side].shape[0] // 2
            parts[side] = parts[side][:size] + got[side].astype(jnp.float32)
            if back is None:
                _, there = lax.optimization_barrier((parts[0], there))
                back = partner(there, devices, PAIR)
    return jnp.concatenate(parts, axis=0), back


def on_device(
    observations,
    pixel_geometry,
    block_counts,
    block_tiles,
    cutoff_lists,
    patch_geometry,
    stress,
    screens,
):
    devices = lax.axis_size("tile")
    here = lax.axis_index("tile")
    blocks, epochs, width = observations.shape
    local_tiles = screens.shape[0]
    layers = devices // LAYER
    local = stress.shape[1] // PBLK

    slots = LAYER * (2 * blocks // devices) * (width // CHUNK)
    sizes = round_sizes(slots)

    held = jnp.swapaxes(stress.reshape(epochs, local, PBLK), 0, 1).reshape(-1, PBLK)
    other = partner(held, devices, devices // 2)
    across_screens = partner(screens, devices, PAIR)
    obs, pix = pack(
        observations,
        pixel_geometry,
        block_counts,
        block_tiles,
        jnp.reshape(here, (1,)).astype(jnp.int32),
        devices,
        local_tiles,
    )

    def exchange(parts):
        got = [partner(parts[x], devices, x * LAYER) for x in range(layers - 1, 0, -1)]
        return [parts[0]] + got[::-1]

    distance = devices // 2
    while distance >= LAYER:
        if distance < devices // 2:
            other = partner(held, devices, distance)
        held = jnp.concatenate([held, other], axis=0)
        if distance == devices // 2:
            held, pix = lax.optimization_barrier((held, pix))
            pix = exchange(pix)
        distance //= 2
    patch_blocks = devices * local
    east, north, depth, compliance = patch_geometry
    origin = patch_geometry[:2, 0]
    strength = compliance * depth * depth
    faces = split(
        jnp.stack(
            [
                strength,
                -strength * (east - origin[0]),
                -strength * (north - origin[1]),
                strength * depth,
            ]
        )
    )
    forms = jnp.concatenate(
        [faces[second] for _, second in CROSS] + [jnp.zeros((8,) + east.shape, jnp.float32)]
    ).astype(jnp.bfloat16)
    forms = jnp.swapaxes(forms.reshape(TERMS, patch_blocks, PBLK), 0, 1)
    patches = jnp.stack([east, north, depth * depth])
    patches = jnp.swapaxes(patches.reshape(3, patch_blocks, PBLK), 0, 1)
    cutoffs = cutoff_lists.reshape(-1)
    held, pix, across_screens = lax.optimization_barrier((held, pix, across_screens))
    places, spots = block_places(devices, here, patch_blocks, local, epochs)
    info = jnp.stack([p[slots, :3, :slots] for p in pix]).astype(jnp.int32).reshape(-1)
    across_screens, forms, patches, cutoffs, info, places, spots = lax.optimization_barrier(
        (across_screens, forms, patches, cutoffs, info, places, spots)
    )
    got = [exchange(o) for o in obs]
    across = partner(held, devices, PAIR)
    across, got[0] = lax.optimization_barrier((across, got[0]))
    all_stress = [held, across, partner(held, devices, 1), partner(across, devices, 1)]
    all_screens = [
        screens,
        across_screens,
        partner(screens, devices, 1),
        partner(across_screens, devices, 1),
    ]

    tables = (info, cutoffs, places, spots, origin)

    state = (
        jax.ShapeDtypeStruct((patch_blocks, epochs, PBLK), jnp.float32),
        jax.ShapeDtypeStruct((LAYER * local_tiles,) + screens.shape[1:], jnp.float32),
    )
    base = 0
    for i, size in enumerate(sizes):
        first, final = i == 0, i == len(sizes) - 1
        groups = [(base, got[i], pix, base)]
        state = fit(
            tables,
            groups,
            patches,
            forms,
            all_screens,
            all_stress,
            state[:2],
            first,
            final,
        )
        if first:
            all_screens, all_stress = state[2:]
        base += size
    grad, screen_grad, given, next_door, diagonal = state
    own, far = screen_grad[:local_tiles], screen_grad[local_tiles : PAIR * local_tiles]
    there = (far + partner(diagonal, devices, 1).astype(jnp.float32)).astype(jnp.bfloat16)
    grad, back = halve(grad[: grad.shape[0] // 2], given, there, devices)
    screen_gradient = (
        own + partner(next_door, devices, 1).astype(jnp.float32) + back.astype(jnp.float32)
    )
    return (jnp.swapaxes(grad, 0, 1).reshape(epochs, local * PBLK), screen_gradient)


def solution(mesh):
    return jax.shard_map(
        on_device,
        mesh=mesh,
        in_specs=(
            P(("groups", "tile"), None, None),
            P(("groups", "tile"), None, None),
            P(("groups", "tile")),
            P(("groups", "tile")),
            P(),
            P(),
            P(None, ("groups", "tile")),
            P(("groups", "tile"), None, None),
        ),
        out_specs=(P(None, ("groups", "tile")), P(("groups", "tile"), None, None)),
        check_vma=False,
    )
```

```python
import functools

import jax
import jax.numpy as jnp
from jax import lax
from jax.experimental import pallas as pl
from jax.experimental.pallas import tpu as pltpu
from jax.sharding import PartitionSpec as P

PBLK = 256
NEAR = 3
SG = 16
CHUNK = 128
LAYER = 4
PAIR = 2
NARROW = 3
ROUNDS = (4, 6, 6)
MIB = 1 << 20
TERMS = 32
CROSS = ((0, 0), (0, 1), (1, 0), (0, 2), (1, 1), (2, 0))


def round_sizes(slots):
    return [slots * r // sum(ROUNDS) for r in ROUNDS]


def pack_kernel(local_tiles, layers, slots, here, tiles, counts, obs_in, pix_in, *rest):
    sizes = round_sizes(slots)
    total = len(sizes)
    obs_out, pix_out = rest[: total * layers], rest[total * layers : (total + 1) * layers]
    obs, pix, obs_all, pix_all, fill, sems = rest[(total + 1) * layers :]
    loads = [
        pltpu.make_async_copy(obs_in, obs, sems.at[0]),
        pltpu.make_async_copy(pix_in, pix, sems.at[1]),
    ]
    for copy in loads:
        copy.start()
    my_layer, my_seat = lax.div(here[0], LAYER), lax.rem(here[0], LAYER)
    chunks = pix.shape[2] // CHUNK
    stride = slots + 1
    for x in range(layers):
        fill[x] = 0
    lane = lax.broadcasted_iota(jnp.int32, (8, CHUNK), 1)
    row = lax.broadcasted_iota(jnp.int32, (8, CHUNK), 0)
    for copy in loads:
        copy.wait()

    def put(b, infos):
        tile = tiles[b]
        count = counts[b]
        owner = lax.div(tile, local_tiles)
        x = lax.div(owner, LAYER) ^ my_layer
        seat = lax.rem(owner, LAYER) ^ my_seat
        spot = lax.rem(seat, PAIR) * PAIR + lax.div(seat, PAIR)
        screen = spot * local_tiles + lax.rem(tile, local_tiles)
        slot = fill[x]
        fill[x] = slot + lax.div(count + CHUNK - 1, CHUNK)
        for c in range(chunks):
            at = slot + c
            live = jnp.clip(count - c * CHUNK, 0, CHUNK)
            obs_all[x * stride + at] = obs[b, :, c * CHUNK : (c + 1) * CHUNK]
            pix_all[x * stride + at] = pix[b, :, c * CHUNK : (c + 1) * CHUNK]
            entry = jnp.where(row == 0, live, jnp.where(row == 1, tile, screen))
            here_only = (lane == at) & (row < 3)
            infos = tuple(
                jnp.where(here_only & (x == i), entry, info) for i, info in enumerate(infos)
            )
        return infos

    infos = lax.fori_loop(
        0, obs.shape[0], put, tuple(jnp.zeros((8, CHUNK), jnp.int32) for _ in range(layers))
    )
    copies = []
    for x in range(layers):
        at = x * stride
        pix_all[at + slots] = infos[x].astype(jnp.float32)
        copies.append((pix_all.at[pl.ds(at, stride)], pix_out[x]))
        for i, size in enumerate(sizes):
            copies.append((obs_all.at[pl.ds(at, size)], obs_out[i * layers + x]))
            at += size
    copies = [pltpu.make_async_copy(a, b, sems.at[i]) for i, (a, b) in enumerate(copies)]
    for copy in copies:
        copy.start()
    for copy in copies:
        copy.wait()


def pack(observations, pixel_geometry, block_counts, block_tiles, here, devices, local_tiles):
    blocks, epochs, width = observations.shape
    layers = devices // LAYER
    slots = LAYER * (2 * blocks // devices) * (width // CHUNK)
    sizes = round_sizes(slots)
    smem = pl.BlockSpec(memory_space=pltpu.SMEM)
    hbm = pl.BlockSpec(memory_space=pl.ANY)
    pix_part = jax.ShapeDtypeStruct((slots + 1, 8, CHUNK), jnp.float32)
    out = pl.pallas_call(
        functools.partial(pack_kernel, local_tiles, layers, slots),
        in_specs=[smem, smem, smem, hbm, hbm],
        out_specs=[hbm] * ((len(sizes) + 1) * layers),
        out_shape=[
            jax.ShapeDtypeStruct((size, epochs, CHUNK), observations.dtype)
            for size in sizes
            for _ in range(layers)
        ]
        + [pix_part] * layers,
        scratch_shapes=[
            pltpu.VMEM(observations.shape, observations.dtype),
            pltpu.VMEM(pixel_geometry.shape, jnp.float32),
            pltpu.VMEM((layers * (slots + 1), epochs, CHUNK), observations.dtype),
            pltpu.VMEM((layers * (slots + 1), 8, CHUNK), jnp.float32),
            pltpu.SMEM((layers,), jnp.int32),
            pltpu.SemaphoreType.DMA(((len(sizes) + 1) * layers,)),
        ],
        compiler_params=pltpu.CompilerParams(vmem_limit_bytes=10 * MIB),
        name="pack",
    )(here, block_tiles, block_counts, observations, pixel_geometry)
    rounds = len(sizes)
    return [out[i * layers : (i + 1) * layers] for i in range(rounds)], out[rounds * layers :]


def split(values):
    parts = []
    for _ in range(3):
        part = lax.reduce_precision(values, 8, 7)
        parts.append(part)
        values = values - part
    return parts


def kernel_split(values):
    parts = []
    for _ in range(3):
        part = values.astype(jnp.bfloat16).astype(jnp.float32)
        parts.append(part)
        values = values - part
    return parts


def fit_kernel(first, final, layers, slots, groups, *refs):
    info, cutoffs, places, spots, origin = refs[:5]
    rest = refs[5:]
    obs_in, pix_in = [], []
    for _ in groups:
        obs_in.append(rest[:layers])
        pix_in.append(rest[layers : 2 * layers])
        rest = rest[2 * layers :]
    patches, forms = rest[:2]
    rest = rest[1:]
    if first:
        screen_parts, stress_parts = rest[1 : 1 + LAYER], rest[1 + LAYER : 1 + 2 * LAYER]
        rest = rest[1 + 2 * LAYER :]
        grad, screen_grad, screens, stress = rest[:4]
        rest = rest[4:]
    else:
        screens, stress = rest[1:3]
        grad, screen_grad = rest[5:7]
        rest = rest[7:]
    outs = rest[:3] if final else ()
    rest = rest[len(outs) :]
    obs, pix = rest[:2]
    buffers = rest[2 : 2 + 15 * PAIR]
    items, sems = rest[2 + 15 * PAIR :]
    sets = [
        [buffers[5 * (PAIR * i + lane) : 5 * (PAIR * i + lane) + 5] for lane in range(PAIR)]
        for i in range(3)
    ]
    epochs = obs.shape[1]
    base = groups[0][0]
    span = sum(size for _, _, size in groups)
    local_tiles = screens.shape[0] // LAYER

    loads = []
    for x in range(layers):
        at = x * span
        for g, (_, low, size) in enumerate(groups):
            loads.append((obs_in[g][x], obs.at[pl.ds(at, size)]))
            loads.append((pix_in[g][x].at[pl.ds(low, size)], pix.at[pl.ds(at, size)]))
            at += size
    if first:
        for parts, whole in ((screen_parts, screens), (stress_parts, stress)):
            size = whole.shape[0] // LAYER
            for i, part in enumerate(parts):
                loads.append((part, whole.at[pl.ds(i * size, size)]))
    loads = [pltpu.make_async_copy(a, b, sems.at[i]) for i, (a, b) in enumerate(loads)]
    for copy in loads:
        copy.start()
    if first:
        grad[...] = jnp.zeros_like(grad)
        screen_grad[...] = jnp.zeros_like(screen_grad)

    def info_of(slot, kind):
        x = lax.div(slot, span)
        return info[(x * 3 + kind) * slots + base + lax.rem(slot, span)]

    def list_slot(slot, total):
        items[total] = slot
        return total + jnp.where(info_of(slot, 0) > 0, 1, 0)

    total = lax.fori_loop(0, layers * span, list_slot, 0)
    for copy in loads:
        copy.wait()

    def item_of(i):
        slot = items[jnp.minimum(i, total - 1)]
        tile = info_of(slot, 1)
        return slot, [cutoffs[tile * NEAR + k] for k in range(NEAR)]

    def spread(i, held):
        rows = pix[item_of(i)[0]]
        columns = rows.T
        for i in range(2):
            held[0][i] = jnp.broadcast_to(columns[:, i : i + 1], (CHUNK, CHUNK))
        le, ln = rows[4:5], rows[5:6]
        along = le * (rows[0:1] - origin[0]) + ln * (rows[1:2] - origin[1])
        row = lax.broadcasted_iota(jnp.int32, (8, CHUNK), 0)
        factors = jnp.where(
            row == 0, along, jnp.where(row == 1, le, jnp.where(row == 2, ln, rows[6:7]))
        )
        parts = kernel_split(factors)
        low = row < 4
        tiles = []
        for first_part, second_part in zip(CROSS[::2], CROSS[1::2]):
            upper = jnp.concatenate([parts[second_part[0]][:4]] * 2, axis=0)
            tiles.append(jnp.where(low, parts[first_part[0]], upper))
        tiles.append(jnp.zeros((8, CHUNK), jnp.float32))
        held[1][...] = jnp.concatenate(tiles, axis=0).T.astype(jnp.bfloat16)

    def make_strips(near, k, begin, end, held, green):
        patch = [
            jnp.broadcast_to(patches[near[k], r : r + 1], (8, PBLK)) for r in range(3)
        ]
        alongs = jnp.dot(
            held[1][begin:end], forms[near[k]], preferred_element_type=jnp.float32
        )
        for low in range(begin, end, 16):
            along = alongs[low - begin : low - begin + 16]
            inverses = []
            for at in (low, low + 8):
                east, north = (
                    jnp.concatenate([held[0][i, at : at + 8]] * (PBLK // CHUNK), axis=1)
                    for i in range(2)
                )
                dx = east - patch[0]
                dy = north - patch[1]
                inverses.append(lax.rsqrt(dx * dx + dy * dy + patch[2]))
            inverse = jnp.concatenate(inverses, axis=0)
            green[low : low + 16, k * PBLK : (k + 1) * PBLK] = (
                along * inverse * inverse * inverse
            ).astype(jnp.bfloat16)

    def make_hats(rows, hats):
        node = lax.broadcasted_iota(jnp.int32, (SG, CHUNK), 0).astype(jnp.float32)
        across = jnp.maximum(0.0, 1.0 - jnp.abs(rows[2:3] - node))
        upward = jnp.maximum(0.0, 1.0 - jnp.abs(rows[3:4] - node))
        for a in range(SG):
            hats[a * SG : (a + 1) * SG] = (across[a : a + 1] * upward).astype(jnp.bfloat16)

    def make_head(i, buffers):
        slot, near = item_of(i)
        make_hats(pix[slot], buffers[1])
        return near

    def predict(i, buffers):
        green, hats = buffers[:2]
        slot, near = item_of(i)
        model = jnp.dot(
            screens[info_of(slot, 2)], hats[...], preferred_element_type=jnp.float32
        )
        for k in range(NEAR):
            model += lax.dot_general(
                stress[pl.ds(pl.multiple_of(spots[near[k]], 16), epochs), :],
                green[:, k * PBLK : (k + 1) * PBLK],
                (((1,), (1,)), ((), ())),
                preferred_element_type=jnp.float32,
            )
        return model

    def weigh(i, model, buffers):
        slot, _ = item_of(i)
        live = jnp.where(i < total, info_of(slot, 0), 0)
        lane = lax.broadcasted_iota(jnp.int32, (1, CHUNK), 1)
        scale = jnp.where(lane < live, pix[slot, 7:8, :], 0.0)
        buffers[2][...] = ((model - obs[slot].astype(jnp.float32)) * scale).astype(jnp.bfloat16)

    def add_patch(near, k, buffers):
        grad[places[near[k]]] += jnp.dot(
            buffers[2][...],
            buffers[0][:, k * PBLK : (k + 1) * PBLK],
            preferred_element_type=jnp.float32,
        )

    def add_screen(slot, buffers):
        screen_grad[info_of(slot, 2)] += lax.dot_general(
            buffers[2][...],
            buffers[1][...],
            (((1,), (1,)), ((), ())),
            preferred_element_type=jnp.float32,
        )

    lanes = range(PAIR)
    half = CHUNK // 2

    def spread_pair(j, buffers):
        for lane in lanes:
            spread(PAIR * j + lane, buffers[lane][3:])

    def make_pair(j, buffers):
        for lane in lanes:
            near = make_head(PAIR * j + lane, buffers[lane])
            for k in range(NEAR):
                for low in (0, half):
                    make_strips(near, k, low, low + half, buffers[lane][3:], buffers[lane][0])

    def model_pair(j, buffers):
        for lane in lanes:
            model = predict(PAIR * j + lane, buffers[lane])
            weigh(PAIR * j + lane, model, buffers[lane])

    def turn(j, using, middle, making):
        now = [item_of(PAIR * j + lane) for lane in lanes]
        coming = [PAIR * (j + 1) + lane for lane in lanes]
        near = [make_head(PAIR * (j + 2) + lane, making[lane]) for lane in lanes]
        models = [predict(coming[lane], middle[lane]) for lane in lanes]

        def strips(k, lane):
            for low in (0, half):
                make_strips(
                    near[lane], k, low, low + half, making[lane][3:], making[lane][0]
                )

        def adds(k):
            for lane in lanes:
                add_patch(now[lane][1], k, using[lane])

        strips(0, 0)
        adds(0)
        spread_pair(j + 3, using)
        strips(0, 1)
        adds(1)
        strips(1, 0)
        for lane in lanes:
            weigh(coming[lane], models[lane], middle[lane])
        strips(1, 1)
        adds(2)
        strips(2, 0)
        for lane in lanes:
            add_screen(now[lane][0], using[lane])
        strips(2, 1)

    @pl.when(total > 0)
    def _():
        pairs = lax.div(total + PAIR - 1, PAIR)
        for j in range(3):
            spread_pair(j, sets[j])
        make_pair(0, sets[0])
        make_pair(1, sets[1])
        model_pair(0, sets[0])

        def step(i, _):
            for at in range(3):
                j = 3 * i + at

                @pl.when(j < pairs)
                def _():
                    turn(j, sets[at], sets[(at + 1) % 3], sets[(at + 2) % 3])

            return 0

        lax.fori_loop(0, lax.div(pairs + 2, 3), step, 0)

    if final:
        half = grad.shape[0] // 2
        outs[0][...] = grad[half:].astype(outs[0].dtype)
        for i, out in enumerate(outs[1:]):
            low = (PAIR + i) * local_tiles
            out[...] = screen_grad[low : low + local_tiles].astype(out.dtype)


def fit(tables, groups, patches, forms, screens, stress, state, first, final):
    layers = len(groups[0][1])
    slots = tables[0].shape[0] // (3 * layers)
    smem = pl.BlockSpec(memory_space=pltpu.SMEM)
    vmem = pl.BlockSpec(memory_space=pltpu.VMEM)
    hbm = pl.BlockSpec(memory_space=pl.ANY)
    spans = tuple((base, low, obs[0].shape[0]) for base, obs, _, low in groups)
    arrays = [a for _, obs, pix, _ in groups for a in (*obs, *pix)]
    span = sum(size for _, _, size in spans)
    blocks, epochs = state[0].shape[0], state[0].shape[1]
    out_shape = [jax.ShapeDtypeStruct(a.shape, a.dtype) for a in state]
    if first:
        state = ()
        for parts in (screens, stress):
            shape = (LAYER * parts[0].shape[0],) + parts[0].shape[1:]
            out_shape.append(jax.ShapeDtypeStruct(shape, parts[0].dtype))
    else:
        screens, stress = [screens], [stress]
    if final:
        out_shape.append(jax.ShapeDtypeStruct((blocks // 2, epochs, PBLK), jnp.bfloat16))
        shape = (state[1].shape[0] // LAYER,) + state[1].shape[1:]
        out_shape += [jax.ShapeDtypeStruct(shape, jnp.bfloat16)] * 2
    before = len(tables) + len(arrays) + 2 + len(screens) + len(stress)
    return pl.pallas_call(
        functools.partial(fit_kernel, first, final, layers, slots, spans),
        in_specs=[smem] * len(tables)
        + [hbm] * len(arrays)
        + [vmem] * 2
        + [hbm if first else vmem] * (len(screens) + len(stress))
        + [vmem] * len(state),
        out_specs=[vmem] * len(out_shape),
        out_shape=out_shape,
        scratch_shapes=[
            pltpu.VMEM((layers * span, epochs, CHUNK), arrays[0].dtype),
            pltpu.VMEM((layers * span, 8, CHUNK), jnp.float32),
        ]
        + [
            pltpu.VMEM((CHUNK, NEAR * PBLK), jnp.bfloat16),
            pltpu.VMEM((SG * SG, CHUNK), jnp.bfloat16),
            pltpu.VMEM((epochs, CHUNK), jnp.bfloat16),
            pltpu.VMEM((2, CHUNK, CHUNK), jnp.float32),
            pltpu.VMEM((CHUNK, TERMS), jnp.bfloat16),
        ]
        * (3 * PAIR)
        + [
            pltpu.SMEM((layers * span + 1,), jnp.int32),
            pltpu.SemaphoreType.DMA((2 * layers * len(groups) + 2 * LAYER,)),
        ],
        input_output_aliases={} if first else {before: 0, before + 1: 1},
        compiler_params=pltpu.CompilerParams(vmem_limit_bytes=8 * MIB),
        cost_estimate=pl.CostEstimate(
            flops=layers * span * 4 * epochs * CHUNK * (NEAR + 1) * PBLK,
            bytes_accessed=1024,
            transcendentals=layers * span * CHUNK * NEAR * PBLK,
        ),
        name="fit",
    )(*tables, *arrays, patches, forms, *screens, *stress, *state)


def partner(values, devices, distance):
    return lax.ppermute(values, "tile", [(i, i ^ distance) for i in range(devices)])


def orders(devices):
    stages = devices.bit_length() - 1
    high = list(range(2, stages))
    return [1] + high, high + [1]


def block_places(devices, here, blocks, local, epochs):
    block = jnp.arange(blocks)
    other = (block // local) ^ here
    seat = block % local
    half = local // 2
    turned = []
    for order in orders(devices):
        spot = 0
        for bit in order:
            spot = spot * 2 + ((other >> bit) & 1)
        turned.append(spot)
    chips = devices // 2
    upper = seat // half
    spot = jnp.where(upper == 0, turned[0], turned[1])
    place = (((other & 1) * 2 + upper) * chips + spot) * half + seat % half
    stages = devices.bit_length() - 1
    held = sum(((other >> (stages - 1 - s)) & 1) << s for s in range(stages))
    return place.astype(jnp.int32), ((held * local + seat) * epochs).astype(jnp.int32)


def halve(kept, given, there, devices):
    total = kept + partner(given, devices, 1).astype(jnp.float32)
    middle = total.shape[0] // 2
    parts = [total[:middle], total[middle:]]
    both = orders(devices)
    stages = len(both[0])
    back = None
    for stage in range(stages):
        got = []
        for side in range(2):
            given = parts[side][parts[side].shape[0] // 2 :]
            if stages - stage <= NARROW:
                given = given.astype(jnp.bfloat16)
            got.append(partner(given, devices, 1 << both[side][stage]))
        for side in range(2):
            if side:
                _, got[1] = lax.optimization_barrier((parts[0], got[1]))
            size = parts[side].shape[0] // 2
            parts[side] = parts[side][:size] + got[side].astype(jnp.float32)
            if back is None:
                _, there = lax.optimization_barrier((parts[0], there))
                back = partner(there, devices, PAIR)
    return jnp.concatenate(parts, axis=0), back


def on_device(
    observations,
    pixel_geometry,
    block_counts,
    block_tiles,
    cutoff_lists,
    patch_geometry,
    stress,
    screens,
):
    devices = lax.axis_size("tile")
    here = lax.axis_index("tile")
    blocks, epochs, width = observations.shape
    local_tiles = screens.shape[0]
    layers = devices // LAYER
    local = stress.shape[1] // PBLK

    slots = LAYER * (2 * blocks // devices) * (width // CHUNK)
    sizes = round_sizes(slots)

    held = jnp.swapaxes(stress.reshape(epochs, local, PBLK), 0, 1).reshape(-1, PBLK)
    other = partner(held, devices, devices // 2)
    across_screens = partner(screens, devices, PAIR)
    obs, pix = pack(
        observations,
        pixel_geometry,
        block_counts,
        block_tiles,
        jnp.reshape(here, (1,)).astype(jnp.int32),
        devices,
        local_tiles,
    )

    def exchange(parts):
        got = [partner(parts[x], devices, x * LAYER) for x in range(layers - 1, 0, -1)]
        return [parts[0]] + got[::-1]

    distance = devices // 2
    while distance >= LAYER:
        if distance < devices // 2:
            other = partner(held, devices, distance)
        held = jnp.concatenate([held, other], axis=0)
        if distance == devices // 2:
            _, pix = lax.optimization_barrier((held, pix))
            pix = exchange(pix)
        distance //= 2
    patch_blocks = devices * local
    east, north, depth, compliance = patch_geometry
    origin = patch_geometry[:2, 0]
    strength = compliance * depth * depth
    faces = split(
        jnp.stack(
            [
                strength,
                -strength * (east - origin[0]),
                -strength * (north - origin[1]),
                strength * depth,
            ]
        )
    )
    forms = jnp.concatenate(
        [faces[second] for _, second in CROSS] + [jnp.zeros((8,) + east.shape, jnp.float32)]
    ).astype(jnp.bfloat16)
    forms = jnp.swapaxes(forms.reshape(TERMS, patch_blocks, PBLK), 0, 1)
    patches = jnp.stack([east, north, depth * depth])
    patches = jnp.swapaxes(patches.reshape(3, patch_blocks, PBLK), 0, 1)
    cutoffs = cutoff_lists.reshape(-1)
    held, pix, across_screens = lax.optimization_barrier((held, pix, across_screens))
    places, spots = block_places(devices, here, patch_blocks, local, epochs)
    info = jnp.stack([p[slots, :3, :slots] for p in pix]).astype(jnp.int32).reshape(-1)
    across_screens, forms, patches, cutoffs, info, places, spots = lax.optimization_barrier(
        (across_screens, forms, patches, cutoffs, info, places, spots)
    )
    got = [exchange(o) for o in obs]
    across = partner(held, devices, PAIR)
    across, got[0] = lax.optimization_barrier((across, got[0]))
    all_stress = [held, across, partner(held, devices, 1), partner(across, devices, 1)]
    all_screens = [
        screens,
        across_screens,
        partner(screens, devices, 1),
        partner(across_screens, devices, 1),
    ]

    tables = (info, cutoffs, places, spots, origin)

    state = (
        jax.ShapeDtypeStruct((patch_blocks, epochs, PBLK), jnp.float32),
        jax.ShapeDtypeStruct((LAYER * local_tiles,) + screens.shape[1:], jnp.float32),
    )
    base = 0
    for i, size in enumerate(sizes):
        first, final = i == 0, i == len(sizes) - 1
        groups = [(base, got[i], pix, base)]
        state = fit(
            tables,
            groups,
            patches,
            forms,
            all_screens,
            all_stress,
            state[:2],
            first,
            final,
        )
        if first:
            all_screens, all_stress = state[2:]
        base += size
    grad, screen_grad, given, next_door, diagonal = state
    own, far = screen_grad[:local_tiles], screen_grad[local_tiles : PAIR * local_tiles]
    there = (far + partner(diagonal, devices, 1).astype(jnp.float32)).astype(jnp.bfloat16)
    grad, back = halve(grad[: grad.shape[0] // 2], given, there, devices)
    screen_gradient = (
        own + partner(next_door, devices, 1).astype(jnp.float32) + back.astype(jnp.float32)
    )
    return (jnp.swapaxes(grad, 0, 1).reshape(epochs, local * PBLK), screen_gradient)


def solution(mesh):
    return jax.shard_map(
        on_device,
        mesh=mesh,
        in_specs=(
            P(("groups", "tile"), None, None),
            P(("groups", "tile"), None, None),
            P(("groups", "tile")),
            P(("groups", "tile")),
            P(),
            P(),
            P(None, ("groups", "tile")),
            P(("groups", "tile"), None, None),
        ),
        out_specs=(P(None, ("groups", "tile")), P(("groups", "tile"), None, None)),
        check_vma=False,
    )
```

```python
import functools

import jax
import jax.numpy as jnp
from jax import lax
from jax.experimental import pallas as pl
from jax.experimental.pallas import tpu as pltpu
from jax.sharding import PartitionSpec as P

PBLK = 256
NEAR = 3
SG = 16
CHUNK = 128
LAYER = 4
PAIR = 2
NARROW = 3
ROUNDS = (4, 6, 6)
MIB = 1 << 20
TERMS = 32
CROSS = ((0, 0), (0, 1), (1, 0), (0, 2), (1, 1), (2, 0))


def round_sizes(slots):
    return [slots * r // sum(ROUNDS) for r in ROUNDS]


def pack_kernel(local_tiles, layers, slots, here, tiles, counts, obs_in, pix_in, *rest):
    sizes = round_sizes(slots)
    total = len(sizes)
    obs_out, pix_out = rest[: total * layers], rest[total * layers : (total + 1) * layers]
    obs, pix, obs_all, pix_all, fill, sems = rest[(total + 1) * layers :]
    loads = [
        pltpu.make_async_copy(obs_in, obs, sems.at[0]),
        pltpu.make_async_copy(pix_in, pix, sems.at[1]),
    ]
    for copy in loads:
        copy.start()
    my_layer, my_seat = lax.div(here[0], LAYER), lax.rem(here[0], LAYER)
    chunks = pix.shape[2] // CHUNK
    stride = slots + 1
    for x in range(layers):
        fill[x] = 0
    lane = lax.broadcasted_iota(jnp.int32, (8, CHUNK), 1)
    row = lax.broadcasted_iota(jnp.int32, (8, CHUNK), 0)
    for copy in loads:
        copy.wait()

    def put(b, infos):
        tile = tiles[b]
        count = counts[b]
        owner = lax.div(tile, local_tiles)
        x = lax.div(owner, LAYER) ^ my_layer
        seat = lax.rem(owner, LAYER) ^ my_seat
        spot = lax.rem(seat, PAIR) * PAIR + lax.div(seat, PAIR)
        screen = spot * local_tiles + lax.rem(tile, local_tiles)
        slot = fill[x]
        fill[x] = slot + lax.div(count + CHUNK - 1, CHUNK)
        for c in range(chunks):
            at = slot + c
            live = jnp.clip(count - c * CHUNK, 0, CHUNK)
            obs_all[x * stride + at] = obs[b, :, c * CHUNK : (c + 1) * CHUNK]
            pix_all[x * stride + at] = pix[b, :, c * CHUNK : (c + 1) * CHUNK]
            entry = jnp.where(row == 0, live, jnp.where(row == 1, tile, screen))
            here_only = (lane == at) & (row < 3)
            infos = tuple(
                jnp.where(here_only & (x == i), entry, info) for i, info in enumerate(infos)
            )
        return infos

    infos = lax.fori_loop(
        0, obs.shape[0], put, tuple(jnp.zeros((8, CHUNK), jnp.int32) for _ in range(layers))
    )
    copies = []
    for x in range(layers):
        at = x * stride
        pix_all[at + slots] = infos[x].astype(jnp.float32)
        copies.append((pix_all.at[pl.ds(at, stride)], pix_out[x]))
        for i, size in enumerate(sizes):
            copies.append((obs_all.at[pl.ds(at, size)], obs_out[i * layers + x]))
            at += size
    copies = [pltpu.make_async_copy(a, b, sems.at[i]) for i, (a, b) in enumerate(copies)]
    for copy in copies:
        copy.start()
    for copy in copies:
        copy.wait()


def pack(observations, pixel_geometry, block_counts, block_tiles, here, devices, local_tiles):
    blocks, epochs, width = observations.shape
    layers = devices // LAYER
    slots = LAYER * (2 * blocks // devices) * (width // CHUNK)
    sizes = round_sizes(slots)
    smem = pl.BlockSpec(memory_space=pltpu.SMEM)
    hbm = pl.BlockSpec(memory_space=pl.ANY)
    pix_part = jax.ShapeDtypeStruct((slots + 1, 8, CHUNK), jnp.float32)
    out = pl.pallas_call(
        functools.partial(pack_kernel, local_tiles, layers, slots),
        in_specs=[smem, smem, smem, hbm, hbm],
        out_specs=[hbm] * ((len(sizes) + 1) * layers),
        out_shape=[
            jax.ShapeDtypeStruct((size, epochs, CHUNK), observations.dtype)
            for size in sizes
            for _ in range(layers)
        ]
        + [pix_part] * layers,
        scratch_shapes=[
            pltpu.VMEM(observations.shape, observations.dtype),
            pltpu.VMEM(pixel_geometry.shape, jnp.float32),
            pltpu.VMEM((layers * (slots + 1), epochs, CHUNK), observations.dtype),
            pltpu.VMEM((layers * (slots + 1), 8, CHUNK), jnp.float32),
            pltpu.SMEM((layers,), jnp.int32),
            pltpu.SemaphoreType.DMA(((len(sizes) + 1) * layers,)),
        ],
        compiler_params=pltpu.CompilerParams(vmem_limit_bytes=10 * MIB),
        name="pack",
    )(here, block_tiles, block_counts, observations, pixel_geometry)
    rounds = len(sizes)
    return [out[i * layers : (i + 1) * layers] for i in range(rounds)], out[rounds * layers :]


def split(values):
    parts = []
    for _ in range(3):
        part = lax.reduce_precision(values, 8, 7)
        parts.append(part)
        values = values - part
    return parts


def kernel_split(values):
    parts = []
    for _ in range(3):
        part = values.astype(jnp.bfloat16).astype(jnp.float32)
        parts.append(part)
        values = values - part
    return parts


def fit_kernel(first, final, layers, slots, groups, *refs):
    info, cutoffs, places, spots, origin = refs[:5]
    rest = refs[5:]
    obs_in, pix_in = [], []
    for _ in groups:
        obs_in.append(rest[:layers])
        pix_in.append(rest[layers : 2 * layers])
        rest = rest[2 * layers :]
    patches, forms = rest[:2]
    rest = rest[1:]
    if first:
        screen_parts, stress_parts = rest[1 : 1 + LAYER], rest[1 + LAYER : 1 + 2 * LAYER]
        rest = rest[1 + 2 * LAYER :]
        grad, screen_grad, screens, stress = rest[:4]
        rest = rest[4:]
    else:
        screens, stress = rest[1:3]
        grad, screen_grad = rest[5:7]
        rest = rest[7:]
    outs = rest[:3] if final else ()
    rest = rest[len(outs) :]
    obs, pix = rest[:2]
    buffers = rest[2 : 2 + 15 * PAIR]
    items, sems = rest[2 + 15 * PAIR :]
    sets = [
        [buffers[5 * (PAIR * i + lane) : 5 * (PAIR * i + lane) + 5] for lane in range(PAIR)]
        for i in range(3)
    ]
    epochs = obs.shape[1]
    base = groups[0][0]
    span = sum(size for _, _, size in groups)
    local_tiles = screens.shape[0] // LAYER

    loads = []
    for x in range(layers):
        at = x * span
        for g, (_, low, size) in enumerate(groups):
            loads.append((obs_in[g][x], obs.at[pl.ds(at, size)]))
            loads.append((pix_in[g][x].at[pl.ds(low, size)], pix.at[pl.ds(at, size)]))
            at += size
    if first:
        for parts, whole in ((screen_parts, screens), (stress_parts, stress)):
            size = whole.shape[0] // LAYER
            for i, part in enumerate(parts):
                loads.append((part, whole.at[pl.ds(i * size, size)]))
    loads = [pltpu.make_async_copy(a, b, sems.at[i]) for i, (a, b) in enumerate(loads)]
    for copy in loads:
        copy.start()
    if first:
        grad[...] = jnp.zeros_like(grad)
        screen_grad[...] = jnp.zeros_like(screen_grad)

    def info_of(slot, kind):
        x = lax.div(slot, span)
        return info[(x * 3 + kind) * slots + base + lax.rem(slot, span)]

    def list_slot(slot, total):
        items[total] = slot
        return total + jnp.where(info_of(slot, 0) > 0, 1, 0)

    total = lax.fori_loop(0, layers * span, list_slot, 0)
    for copy in loads:
        copy.wait()

    def item_of(i):
        slot = items[jnp.minimum(i, total - 1)]
        tile = info_of(slot, 1)
        return slot, [cutoffs[tile * NEAR + k] for k in range(NEAR)]

    def spread(i, held):
        rows = pix[item_of(i)[0]]
        columns = rows.T
        for i in range(2):
            held[0][i] = jnp.broadcast_to(columns[:, i : i + 1], (CHUNK, CHUNK))
        le, ln = rows[4:5], rows[5:6]
        along = le * (rows[0:1] - origin[0]) + ln * (rows[1:2] - origin[1])
        row = lax.broadcasted_iota(jnp.int32, (8, CHUNK), 0)
        factors = jnp.where(
            row == 0, along, jnp.where(row == 1, le, jnp.where(row == 2, ln, rows[6:7]))
        )
        parts = kernel_split(factors)
        low = row < 4
        tiles = []
        for first_part, second_part in zip(CROSS[::2], CROSS[1::2]):
            upper = jnp.concatenate([parts[second_part[0]][:4]] * 2, axis=0)
            tiles.append(jnp.where(low, parts[first_part[0]], upper))
        tiles.append(jnp.zeros((8, CHUNK), jnp.float32))
        held[1][...] = jnp.concatenate(tiles, axis=0).T.astype(jnp.bfloat16)

    def make_strips(near, k, begin, end, held, green):
        patch = [
            jnp.broadcast_to(patches[near[k], r : r + 1], (8, PBLK)) for r in range(3)
        ]
        alongs = jnp.dot(
            held[1][begin:end], forms[near[k]], preferred_element_type=jnp.float32
        )
        for low in range(begin, end, 16):
            along = alongs[low - begin : low - begin + 16]
            inverses = []
            for at in (low, low + 8):
                east, north = (
                    jnp.concatenate([held[0][i, at : at + 8]] * (PBLK // CHUNK), axis=1)
                    for i in range(2)
                )
                dx = east - patch[0]
                dy = north - patch[1]
                inverses.append(lax.rsqrt(dx * dx + dy * dy + patch[2]))
            inverse = jnp.concatenate(inverses, axis=0)
            green[low : low + 16, k * PBLK : (k + 1) * PBLK] = (
                along * inverse * inverse * inverse
            ).astype(jnp.bfloat16)

    def make_hats(rows, hats):
        node = lax.broadcasted_iota(jnp.int32, (SG, CHUNK), 0).astype(jnp.float32)
        across = jnp.maximum(0.0, 1.0 - jnp.abs(rows[2:3] - node))
        upward = jnp.maximum(0.0, 1.0 - jnp.abs(rows[3:4] - node))
        for a in range(SG):
            hats[a * SG : (a + 1) * SG] = (across[a : a + 1] * upward).astype(jnp.bfloat16)

    def make_head(i, buffers):
        slot, near = item_of(i)
        make_hats(pix[slot], buffers[1])
        return near

    def predict(i, buffers):
        green, hats = buffers[:2]
        slot, near = item_of(i)
        model = jnp.dot(
            screens[info_of(slot, 2)], hats[...], preferred_element_type=jnp.float32
        )
        for k in range(NEAR):
            model += lax.dot_general(
                stress[pl.ds(pl.multiple_of(spots[near[k]], 16), epochs), :],
                green[:, k * PBLK : (k + 1) * PBLK],
                (((1,), (1,)), ((), ())),
                preferred_element_type=jnp.float32,
            )
        return model

    def weigh(i, model, buffers):
        slot, _ = item_of(i)
        live = jnp.where(i < total, info_of(slot, 0), 0)
        lane = lax.broadcasted_iota(jnp.int32, (1, CHUNK), 1)
        scale = jnp.where(lane < live, pix[slot, 7:8, :], 0.0)
        buffers[2][...] = ((model - obs[slot].astype(jnp.float32)) * scale).astype(jnp.bfloat16)

    def add_patch(near, k, buffers):
        grad[places[near[k]]] += jnp.dot(
            buffers[2][...],
            buffers[0][:, k * PBLK : (k + 1) * PBLK],
            preferred_element_type=jnp.float32,
        )

    def add_screen(slot, buffers):
        screen_grad[info_of(slot, 2)] += lax.dot_general(
            buffers[2][...],
            buffers[1][...],
            (((1,), (1,)), ((), ())),
            preferred_element_type=jnp.float32,
        )

    lanes = range(PAIR)
    half = CHUNK // 2

    def spread_pair(j, buffers):
        for lane in lanes:
            spread(PAIR * j + lane, buffers[lane][3:])

    def make_pair(j, buffers):
        for lane in lanes:
            near = make_head(PAIR * j + lane, buffers[lane])
            for k in range(NEAR):
                for low in (0, half):
                    make_strips(near, k, low, low + half, buffers[lane][3:], buffers[lane][0])

    def model_pair(j, buffers):
        for lane in lanes:
            model = predict(PAIR * j + lane, buffers[lane])
            weigh(PAIR * j + lane, model, buffers[lane])

    def turn(j, using, middle, making):
        now = [item_of(PAIR * j + lane) for lane in lanes]
        coming = [PAIR * (j + 1) + lane for lane in lanes]
        near = [make_head(PAIR * (j + 2) + lane, making[lane]) for lane in lanes]
        models = [predict(coming[lane], middle[lane]) for lane in lanes]

        def strips(k, lane):
            for low in (0, half):
                make_strips(
                    near[lane], k, low, low + half, making[lane][3:], making[lane][0]
                )

        def adds(k):
            for lane in lanes:
                add_patch(now[lane][1], k, using[lane])

        strips(0, 0)
        adds(0)
        spread_pair(j + 3, using)
        strips(0, 1)
        adds(1)
        strips(1, 0)
        for lane in lanes:
            weigh(coming[lane], models[lane], middle[lane])
        strips(1, 1)
        adds(2)
        strips(2, 0)
        for lane in lanes:
            add_screen(now[lane][0], using[lane])
        strips(2, 1)

    @pl.when(total > 0)
    def _():
        pairs = lax.div(total + PAIR - 1, PAIR)
        for j in range(3):
            spread_pair(j, sets[j])
        make_pair(0, sets[0])
        make_pair(1, sets[1])
        model_pair(0, sets[0])

        def step(i, _):
            for at in range(3):
                j = 3 * i + at

                @pl.when(j < pairs)
                def _():
                    turn(j, sets[at], sets[(at + 1) % 3], sets[(at + 2) % 3])

            return 0

        lax.fori_loop(0, lax.div(pairs + 2, 3), step, 0)

    if final:
        half = grad.shape[0] // 2
        outs[0][...] = grad[half:].astype(outs[0].dtype)
        for i, out in enumerate(outs[1:]):
            low = (PAIR + i) * local_tiles
            out[...] = screen_grad[low : low + local_tiles].astype(out.dtype)


def fit(tables, groups, patches, forms, screens, stress, state, first, final):
    layers = len(groups[0][1])
    slots = tables[0].shape[0] // (3 * layers)
    smem = pl.BlockSpec(memory_space=pltpu.SMEM)
    vmem = pl.BlockSpec(memory_space=pltpu.VMEM)
    hbm = pl.BlockSpec(memory_space=pl.ANY)
    spans = tuple((base, low, obs[0].shape[0]) for base, obs, _, low in groups)
    arrays = [a for _, obs, pix, _ in groups for a in (*obs, *pix)]
    span = sum(size for _, _, size in spans)
    blocks, epochs = state[0].shape[0], state[0].shape[1]
    out_shape = [jax.ShapeDtypeStruct(a.shape, a.dtype) for a in state]
    if first:
        state = ()
        for parts in (screens, stress):
            shape = (LAYER * parts[0].shape[0],) + parts[0].shape[1:]
            out_shape.append(jax.ShapeDtypeStruct(shape, parts[0].dtype))
    else:
        screens, stress = [screens], [stress]
    if final:
        out_shape.append(jax.ShapeDtypeStruct((blocks // 2, epochs, PBLK), jnp.bfloat16))
        shape = (state[1].shape[0] // LAYER,) + state[1].shape[1:]
        out_shape += [jax.ShapeDtypeStruct(shape, jnp.bfloat16)] * 2
    before = len(tables) + len(arrays) + 2 + len(screens) + len(stress)
    return pl.pallas_call(
        functools.partial(fit_kernel, first, final, layers, slots, spans),
        in_specs=[smem] * len(tables)
        + [hbm] * len(arrays)
        + [vmem] * 2
        + [hbm if first else vmem] * (len(screens) + len(stress))
        + [vmem] * len(state),
        out_specs=[vmem] * len(out_shape),
        out_shape=out_shape,
        scratch_shapes=[
            pltpu.VMEM((layers * span, epochs, CHUNK), arrays[0].dtype),
            pltpu.VMEM((layers * span, 8, CHUNK), jnp.float32),
        ]
        + [
            pltpu.VMEM((CHUNK, NEAR * PBLK), jnp.bfloat16),
            pltpu.VMEM((SG * SG, CHUNK), jnp.bfloat16),
            pltpu.VMEM((epochs, CHUNK), jnp.bfloat16),
            pltpu.VMEM((2, CHUNK, CHUNK), jnp.float32),
            pltpu.VMEM((CHUNK, TERMS), jnp.bfloat16),
        ]
        * (3 * PAIR)
        + [
            pltpu.SMEM((layers * span + 1,), jnp.int32),
            pltpu.SemaphoreType.DMA((2 * layers * len(groups) + 2 * LAYER,)),
        ],
        input_output_aliases={} if first else {before: 0, before + 1: 1},
        compiler_params=pltpu.CompilerParams(vmem_limit_bytes=8 * MIB),
        cost_estimate=pl.CostEstimate(
            flops=layers * span * 4 * epochs * CHUNK * (NEAR + 1) * PBLK,
            bytes_accessed=1024,
            transcendentals=layers * span * CHUNK * NEAR * PBLK,
        ),
        name="fit",
    )(*tables, *arrays, patches, forms, *screens, *stress, *state)


def partner(values, devices, distance):
    return lax.ppermute(values, "tile", [(i, i ^ distance) for i in range(devices)])


def orders(devices):
    stages = devices.bit_length() - 1
    high = list(range(2, stages))
    return [1] + high, high + [1]


def block_places(devices, here, blocks, local, epochs):
    block = jnp.arange(blocks)
    other = (block // local) ^ here
    seat = block % local
    half = local // 2
    turned = []
    for order in orders(devices):
        spot = 0
        for bit in order:
            spot = spot * 2 + ((other >> bit) & 1)
        turned.append(spot)
    chips = devices // 2
    upper = seat // half
    spot = jnp.where(upper == 0, turned[0], turned[1])
    place = (((other & 1) * 2 + upper) * chips + spot) * half + seat % half
    stages = devices.bit_length() - 1
    held = sum(((other >> (stages - 1 - s)) & 1) << s for s in range(stages))
    return place.astype(jnp.int32), ((held * local + seat) * epochs).astype(jnp.int32)


def halve(kept, given, there, devices):
    total = kept + partner(given, devices, 1).astype(jnp.float32)
    middle = total.shape[0] // 2
    parts = [total[:middle], total[middle:]]
    both = orders(devices)
    stages = len(both[0])
    back = None
    for stage in range(stages):
        got = []
        for side in range(2):
            given = parts[side][parts[side].shape[0] // 2 :]
            if stages - stage <= NARROW:
                given = given.astype(jnp.bfloat16)
            got.append(partner(given, devices, 1 << both[side][stage]))
        for side in range(2):
            if side:
                _, got[1] = lax.optimization_barrier((parts[0], got[1]))
            size = parts[side].shape[0] // 2
            parts[side] = parts[side][:size] + got[side].astype(jnp.float32)
            if back is None:
                _, there = lax.optimization_barrier((parts[0], there))
                back = partner(there, devices, PAIR)
    return jnp.concatenate(parts, axis=0), back


def on_device(
    observations,
    pixel_geometry,
    block_counts,
    block_tiles,
    cutoff_lists,
    patch_geometry,
    stress,
    screens,
):
    devices = lax.axis_size("tile")
    here = lax.axis_index("tile")
    blocks, epochs, width = observations.shape
    local_tiles = screens.shape[0]
    layers = devices // LAYER
    local = stress.shape[1] // PBLK

    slots = LAYER * (2 * blocks // devices) * (width // CHUNK)
    sizes = round_sizes(slots)

    held = jnp.swapaxes(stress.reshape(epochs, local, PBLK), 0, 1).reshape(-1, PBLK)
    other = partner(held, devices, devices // 2)
    across_screens = partner(screens, devices, PAIR)
    obs, pix = pack(
        observations,
        pixel_geometry,
        block_counts,
        block_tiles,
        jnp.reshape(here, (1,)).astype(jnp.int32),
        devices,
        local_tiles,
    )

    def exchange(parts):
        got = [partner(parts[x], devices, x * LAYER) for x in range(layers - 1, 0, -1)]
        return [parts[0]] + got[::-1]

    distance = devices // 2
    while distance >= LAYER:
        if distance < devices // 2:
            other = partner(held, devices, distance)
        held = jnp.concatenate([held, other], axis=0)
        if distance == devices // 2:
            _, pix = lax.optimization_barrier((held, pix))
            pix = exchange(pix)
        distance //= 2
    patch_blocks = devices * local
    east, north, depth, compliance = patch_geometry
    origin = patch_geometry[:2, 0]
    strength = compliance * depth * depth
    faces = split(
        jnp.stack(
            [
                strength,
                -strength * (east - origin[0]),
                -strength * (north - origin[1]),
                strength * depth,
            ]
        )
    )
    forms = jnp.concatenate(
        [faces[second] for _, second in CROSS] + [jnp.zeros((8,) + east.shape, jnp.float32)]
    ).astype(jnp.bfloat16)
    forms = jnp.swapaxes(forms.reshape(TERMS, patch_blocks, PBLK), 0, 1)
    patches = jnp.stack([east, north, depth * depth])
    patches = jnp.swapaxes(patches.reshape(3, patch_blocks, PBLK), 0, 1)
    cutoffs = cutoff_lists.reshape(-1)
    held, pix, across_screens = lax.optimization_barrier((held, pix, across_screens))
    places, spots = block_places(devices, here, patch_blocks, local, epochs)
    info = jnp.stack([p[slots, :3, :slots] for p in pix]).astype(jnp.int32).reshape(-1)
    across_screens, forms, patches, cutoffs, info, places, spots = lax.optimization_barrier(
        (across_screens, forms, patches, cutoffs, info, places, spots)
    )
    got = [exchange(o) for o in obs[:PAIR]]
    across = partner(held, devices, PAIR)
    across, got[0] = lax.optimization_barrier((across, got[0]))
    all_stress = [held, across, partner(held, devices, 1), partner(across, devices, 1)]
    all_screens = [
        screens,
        across_screens,
        partner(screens, devices, 1),
        partner(across_screens, devices, 1),
    ]

    tables = (info, cutoffs, places, spots, origin)

    state = (
        jax.ShapeDtypeStruct((patch_blocks, epochs, PBLK), jnp.float32),
        jax.ShapeDtypeStruct((LAYER * local_tiles,) + screens.shape[1:], jnp.float32),
    )
    base = 0
    for i, size in enumerate(sizes):
        first, final = i == 0, i == len(sizes) - 1
        groups = [(base, got[i], pix, base)]
        state = fit(
            tables,
            groups,
            patches,
            forms,
            all_screens,
            all_stress,
            state[:2],
            first,
            final,
        )
        if first:
            all_screens, all_stress = state[2:]
            for late in obs[PAIR:]:
                _, late = lax.optimization_barrier((all_screens, late))
                got.append(exchange(late))
        base += size
    grad, screen_grad, given, next_door, diagonal = state
    own, far = screen_grad[:local_tiles], screen_grad[local_tiles : PAIR * local_tiles]
    there = (far + partner(diagonal, devices, 1).astype(jnp.float32)).astype(jnp.bfloat16)
    grad, back = halve(grad[: grad.shape[0] // 2], given, there, devices)
    screen_gradient = (
        own + partner(next_door, devices, 1).astype(jnp.float32) + back.astype(jnp.float32)
    )
    return (jnp.swapaxes(grad, 0, 1).reshape(epochs, local * PBLK), screen_gradient)


def solution(mesh):
    return jax.shard_map(
        on_device,
        mesh=mesh,
        in_specs=(
            P(("groups", "tile"), None, None),
            P(("groups", "tile"), None, None),
            P(("groups", "tile")),
            P(("groups", "tile")),
            P(),
            P(),
            P(None, ("groups", "tile")),
            P(("groups", "tile"), None, None),
        ),
        out_specs=(P(None, ("groups", "tile")), P(("groups", "tile"), None, None)),
        check_vma=False,
    )
```

```python
import functools

import jax
import jax.numpy as jnp
from jax import lax
from jax.experimental import pallas as pl
from jax.experimental.pallas import tpu as pltpu
from jax.sharding import PartitionSpec as P

PBLK = 256
NEAR = 3
SG = 16
CHUNK = 128
LAYER = 4
PAIR = 2
NARROW = 3
ROUNDS = (4, 6, 6)
MIB = 1 << 20
TERMS = 32
CROSS = ((0, 0), (0, 1), (1, 0), (0, 2), (1, 1), (2, 0))


def round_sizes(slots):
    return [slots * r // sum(ROUNDS) for r in ROUNDS]


def pack_kernel(local_tiles, layers, slots, here, tiles, counts, obs_in, pix_in, *rest):
    sizes = round_sizes(slots)
    total = len(sizes)
    obs_out, pix_out = rest[: total * layers], rest[total * layers : (total + 1) * layers]
    obs, pix, obs_all, pix_all, fill, sems = rest[(total + 1) * layers :]
    loads = [
        pltpu.make_async_copy(obs_in, obs, sems.at[0]),
        pltpu.make_async_copy(pix_in, pix, sems.at[1]),
    ]
    for copy in loads:
        copy.start()
    my_layer, my_seat = lax.div(here[0], LAYER), lax.rem(here[0], LAYER)
    chunks = pix.shape[2] // CHUNK
    stride = slots + 1
    for x in range(layers):
        fill[x] = 0
    lane = lax.broadcasted_iota(jnp.int32, (8, CHUNK), 1)
    row = lax.broadcasted_iota(jnp.int32, (8, CHUNK), 0)
    for copy in loads:
        copy.wait()

    def put(b, infos):
        tile = tiles[b]
        count = counts[b]
        owner = lax.div(tile, local_tiles)
        x = lax.div(owner, LAYER) ^ my_layer
        seat = lax.rem(owner, LAYER) ^ my_seat
        spot = lax.rem(seat, PAIR) * PAIR + lax.div(seat, PAIR)
        screen = spot * local_tiles + lax.rem(tile, local_tiles)
        slot = fill[x]
        fill[x] = slot + lax.div(count + CHUNK - 1, CHUNK)
        for c in range(chunks):
            at = slot + c
            live = jnp.clip(count - c * CHUNK, 0, CHUNK)
            obs_all[x * stride + at] = obs[b, :, c * CHUNK : (c + 1) * CHUNK]
            pix_all[x * stride + at] = pix[b, :, c * CHUNK : (c + 1) * CHUNK]
            entry = jnp.where(row == 0, live, jnp.where(row == 1, tile, screen))
            here_only = (lane == at) & (row < 3)
            infos = tuple(
                jnp.where(here_only & (x == i), entry, info) for i, info in enumerate(infos)
            )
        return infos

    infos = lax.fori_loop(
        0, obs.shape[0], put, tuple(jnp.zeros((8, CHUNK), jnp.int32) for _ in range(layers))
    )
    copies = []
    for x in range(layers):
        at = x * stride
        pix_all[at + slots] = infos[x].astype(jnp.float32)
        copies.append((pix_all.at[pl.ds(at, stride)], pix_out[x]))
        for i, size in enumerate(sizes):
            copies.append((obs_all.at[pl.ds(at, size)], obs_out[i * layers + x]))
            at += size
    copies = [pltpu.make_async_copy(a, b, sems.at[i]) for i, (a, b) in enumerate(copies)]
    for copy in copies:
        copy.start()
    for copy in copies:
        copy.wait()


def pack(observations, pixel_geometry, block_counts, block_tiles, here, devices, local_tiles):
    blocks, epochs, width = observations.shape
    layers = devices // LAYER
    slots = LAYER * (2 * blocks // devices) * (width // CHUNK)
    sizes = round_sizes(slots)
    smem = pl.BlockSpec(memory_space=pltpu.SMEM)
    hbm = pl.BlockSpec(memory_space=pl.ANY)
    pix_part = jax.ShapeDtypeStruct((slots + 1, 8, CHUNK), jnp.float32)
    out = pl.pallas_call(
        functools.partial(pack_kernel, local_tiles, layers, slots),
        in_specs=[smem, smem, smem, hbm, hbm],
        out_specs=[hbm] * ((len(sizes) + 1) * layers),
        out_shape=[
            jax.ShapeDtypeStruct((size, epochs, CHUNK), observations.dtype)
            for size in sizes
            for _ in range(layers)
        ]
        + [pix_part] * layers,
        scratch_shapes=[
            pltpu.VMEM(observations.shape, observations.dtype),
            pltpu.VMEM(pixel_geometry.shape, jnp.float32),
            pltpu.VMEM((layers * (slots + 1), epochs, CHUNK), observations.dtype),
            pltpu.VMEM((layers * (slots + 1), 8, CHUNK), jnp.float32),
            pltpu.SMEM((layers,), jnp.int32),
            pltpu.SemaphoreType.DMA(((len(sizes) + 1) * layers,)),
        ],
        compiler_params=pltpu.CompilerParams(vmem_limit_bytes=10 * MIB),
        name="pack",
    )(here, block_tiles, block_counts, observations, pixel_geometry)
    rounds = len(sizes)
    return [out[i * layers : (i + 1) * layers] for i in range(rounds)], out[rounds * layers :]


def split(values):
    parts = []
    for _ in range(3):
        part = lax.reduce_precision(values, 8, 7)
        parts.append(part)
        values = values - part
    return parts


def kernel_split(values):
    parts = []
    for _ in range(3):
        part = values.astype(jnp.bfloat16).astype(jnp.float32)
        parts.append(part)
        values = values - part
    return parts


def fit_kernel(first, final, layers, slots, groups, *refs):
    info, cutoffs, places, spots, origin = refs[:5]
    rest = refs[5:]
    obs_in, pix_in = [], []
    for _ in groups:
        obs_in.append(rest[:layers])
        pix_in.append(rest[layers : 2 * layers])
        rest = rest[2 * layers :]
    patches, forms = rest[:2]
    rest = rest[1:]
    if first:
        screen_parts, stress_parts = rest[1 : 1 + LAYER], rest[1 + LAYER : 1 + 2 * LAYER]
        rest = rest[1 + 2 * LAYER :]
        grad, screen_grad, screens, stress = rest[:4]
        rest = rest[4:]
    else:
        screens, stress = rest[1:3]
        grad, screen_grad = rest[5:7]
        rest = rest[7:]
    outs = rest[:3] if final else ()
    rest = rest[len(outs) :]
    obs, pix = rest[:2]
    buffers = rest[2 : 2 + 15 * PAIR]
    items, sems = rest[2 + 15 * PAIR :]
    sets = [
        [buffers[5 * (PAIR * i + lane) : 5 * (PAIR * i + lane) + 5] for lane in range(PAIR)]
        for i in range(3)
    ]
    epochs = obs.shape[1]
    base = groups[0][0]
    span = sum(size for _, _, size in groups)
    local_tiles = screens.shape[0] // LAYER

    loads = []
    for x in range(layers):
        at = x * span
        for g, (_, low, size) in enumerate(groups):
            loads.append((obs_in[g][x], obs.at[pl.ds(at, size)]))
            loads.append((pix_in[g][x].at[pl.ds(low, size)], pix.at[pl.ds(at, size)]))
            at += size
    if first:
        for parts, whole in ((screen_parts, screens), (stress_parts, stress)):
            size = whole.shape[0] // LAYER
            for i, part in enumerate(parts):
                loads.append((part, whole.at[pl.ds(i * size, size)]))
    loads = [pltpu.make_async_copy(a, b, sems.at[i]) for i, (a, b) in enumerate(loads)]
    for copy in loads:
        copy.start()
    if first:
        grad[...] = jnp.zeros_like(grad)
        screen_grad[...] = jnp.zeros_like(screen_grad)

    def info_of(slot, kind):
        x = lax.div(slot, span)
        return info[(x * 3 + kind) * slots + base + lax.rem(slot, span)]

    def list_slot(slot, total):
        items[total] = slot
        return total + jnp.where(info_of(slot, 0) > 0, 1, 0)

    total = lax.fori_loop(0, layers * span, list_slot, 0)
    for copy in loads:
        copy.wait()

    def item_of(i):
        slot = items[jnp.minimum(i, total - 1)]
        tile = info_of(slot, 1)
        return slot, [cutoffs[tile * NEAR + k] for k in range(NEAR)]

    def spread(i, held):
        rows = pix[item_of(i)[0]]
        columns = rows.T
        for i in range(2):
            held[0][i] = jnp.broadcast_to(columns[:, i : i + 1], (CHUNK, CHUNK))
        le, ln = rows[4:5], rows[5:6]
        along = le * (rows[0:1] - origin[0]) + ln * (rows[1:2] - origin[1])
        row = lax.broadcasted_iota(jnp.int32, (8, CHUNK), 0)
        factors = jnp.where(
            row == 0, along, jnp.where(row == 1, le, jnp.where(row == 2, ln, rows[6:7]))
        )
        parts = kernel_split(factors)
        low = row < 4
        tiles = []
        for first_part, second_part in zip(CROSS[::2], CROSS[1::2]):
            upper = jnp.concatenate([parts[second_part[0]][:4]] * 2, axis=0)
            tiles.append(jnp.where(low, parts[first_part[0]], upper))
        tiles.append(jnp.zeros((8, CHUNK), jnp.float32))
        held[1][...] = jnp.concatenate(tiles, axis=0).T.astype(jnp.bfloat16)

    def make_strips(near, k, begin, end, held, green):
        patch = [
            jnp.broadcast_to(patches[near[k], r : r + 1], (8, PBLK)) for r in range(3)
        ]
        alongs = jnp.dot(
            held[1][begin:end], forms[near[k]], preferred_element_type=jnp.float32
        )
        for low in range(begin, end, 16):
            along = alongs[low - begin : low - begin + 16]
            inverses = []
            for at in (low, low + 8):
                east, north = (
                    jnp.concatenate([held[0][i, at : at + 8]] * (PBLK // CHUNK), axis=1)
                    for i in range(2)
                )
                dx = east - patch[0]
                dy = north - patch[1]
                inverses.append(lax.rsqrt(dx * dx + dy * dy + patch[2]))
            inverse = jnp.concatenate(inverses, axis=0)
            green[low : low + 16, k * PBLK : (k + 1) * PBLK] = (
                along * inverse * inverse * inverse
            ).astype(jnp.bfloat16)

    def make_hats(rows, hats):
        node = lax.broadcasted_iota(jnp.int32, (SG, CHUNK), 0).astype(jnp.float32)
        across = jnp.maximum(0.0, 1.0 - jnp.abs(rows[2:3] - node))
        upward = jnp.maximum(0.0, 1.0 - jnp.abs(rows[3:4] - node))
        for a in range(SG):
            hats[a * SG : (a + 1) * SG] = (across[a : a + 1] * upward).astype(jnp.bfloat16)

    def make_head(i, buffers):
        slot, near = item_of(i)
        make_hats(pix[slot], buffers[1])
        return near

    def predict(i, buffers):
        green, hats = buffers[:2]
        slot, near = item_of(i)
        model = jnp.dot(
            screens[info_of(slot, 2)], hats[...], preferred_element_type=jnp.float32
        )
        for k in range(NEAR):
            model += lax.dot_general(
                stress[pl.ds(pl.multiple_of(spots[near[k]], 16), epochs), :],
                green[:, k * PBLK : (k + 1) * PBLK],
                (((1,), (1,)), ((), ())),
                preferred_element_type=jnp.float32,
            )
        return model

    def weigh(i, model, buffers):
        slot, _ = item_of(i)
        live = jnp.where(i < total, info_of(slot, 0), 0)
        lane = lax.broadcasted_iota(jnp.int32, (1, CHUNK), 1)
        scale = jnp.where(lane < live, pix[slot, 7:8, :], 0.0)
        buffers[2][...] = ((model - obs[slot].astype(jnp.float32)) * scale).astype(jnp.bfloat16)

    def add_patch(near, k, buffers):
        grad[places[near[k]]] += jnp.dot(
            buffers[2][...],
            buffers[0][:, k * PBLK : (k + 1) * PBLK],
            preferred_element_type=jnp.float32,
        )

    def add_screen(slot, buffers):
        screen_grad[info_of(slot, 2)] += lax.dot_general(
            buffers[2][...],
            buffers[1][...],
            (((1,), (1,)), ((), ())),
            preferred_element_type=jnp.float32,
        )

    lanes = range(PAIR)
    half = CHUNK // 2

    def spread_pair(j, buffers):
        for lane in lanes:
            spread(PAIR * j + lane, buffers[lane][3:])

    def make_pair(j, buffers):
        for lane in lanes:
            near = make_head(PAIR * j + lane, buffers[lane])
            for k in range(NEAR):
                for low in (0, half):
                    make_strips(near, k, low, low + half, buffers[lane][3:], buffers[lane][0])

    def model_pair(j, buffers):
        for lane in lanes:
            model = predict(PAIR * j + lane, buffers[lane])
            weigh(PAIR * j + lane, model, buffers[lane])

    def turn(j, using, middle, making):
        now = [item_of(PAIR * j + lane) for lane in lanes]
        coming = [PAIR * (j + 1) + lane for lane in lanes]
        near = [make_head(PAIR * (j + 2) + lane, making[lane]) for lane in lanes]
        models = [predict(coming[lane], middle[lane]) for lane in lanes]

        def strips(k, lane):
            for low in (0, half):
                make_strips(
                    near[lane], k, low, low + half, making[lane][3:], making[lane][0]
                )

        def adds(k):
            for lane in lanes:
                add_patch(now[lane][1], k, using[lane])

        strips(0, 0)
        adds(0)
        spread_pair(j + 3, using)
        strips(0, 1)
        adds(1)
        strips(1, 0)
        for lane in lanes:
            weigh(coming[lane], models[lane], middle[lane])
        strips(1, 1)
        adds(2)
        strips(2, 0)
        for lane in lanes:
            add_screen(now[lane][0], using[lane])
        strips(2, 1)

    @pl.when(total > 0)
    def _():
        pairs = lax.div(total + PAIR - 1, PAIR)
        for j in range(3):
            spread_pair(j, sets[j])
        make_pair(0, sets[0])
        make_pair(1, sets[1])
        model_pair(0, sets[0])

        def step(i, _):
            for at in range(3):
                j = 3 * i + at

                @pl.when(j < pairs)
                def _():
                    turn(j, sets[at], sets[(at + 1) % 3], sets[(at + 2) % 3])

            return 0

        lax.fori_loop(0, lax.div(pairs + 2, 3), step, 0)

    if final:
        half = grad.shape[0] // 2
        outs[0][...] = grad[half:].astype(outs[0].dtype)
        for i, out in enumerate(outs[1:]):
            low = (PAIR + i) * local_tiles
            out[...] = screen_grad[low : low + local_tiles].astype(out.dtype)


def fit(tables, groups, patches, forms, screens, stress, state, first, final):
    layers = len(groups[0][1])
    slots = tables[0].shape[0] // (3 * layers)
    smem = pl.BlockSpec(memory_space=pltpu.SMEM)
    vmem = pl.BlockSpec(memory_space=pltpu.VMEM)
    hbm = pl.BlockSpec(memory_space=pl.ANY)
    spans = tuple((base, low, obs[0].shape[0]) for base, obs, _, low in groups)
    arrays = [a for _, obs, pix, _ in groups for a in (*obs, *pix)]
    span = sum(size for _, _, size in spans)
    blocks, epochs = state[0].shape[0], state[0].shape[1]
    out_shape = [jax.ShapeDtypeStruct(a.shape, a.dtype) for a in state]
    if first:
        state = ()
        for parts in (screens, stress):
            shape = (LAYER * parts[0].shape[0],) + parts[0].shape[1:]
            out_shape.append(jax.ShapeDtypeStruct(shape, parts[0].dtype))
    else:
        screens, stress = [screens], [stress]
    if final:
        out_shape.append(jax.ShapeDtypeStruct((blocks // 2, epochs, PBLK), jnp.bfloat16))
        shape = (state[1].shape[0] // LAYER,) + state[1].shape[1:]
        out_shape += [jax.ShapeDtypeStruct(shape, jnp.bfloat16)] * 2
    before = len(tables) + len(arrays) + 2 + len(screens) + len(stress)
    return pl.pallas_call(
        functools.partial(fit_kernel, first, final, layers, slots, spans),
        in_specs=[smem] * len(tables)
        + [hbm] * len(arrays)
        + [vmem] * 2
        + [hbm if first else vmem] * (len(screens) + len(stress))
        + [vmem] * len(state),
        out_specs=[vmem] * len(out_shape),
        out_shape=out_shape,
        scratch_shapes=[
            pltpu.VMEM((layers * span, epochs, CHUNK), arrays[0].dtype),
            pltpu.VMEM((layers * span, 8, CHUNK), jnp.float32),
        ]
        + [
            pltpu.VMEM((CHUNK, NEAR * PBLK), jnp.bfloat16),
            pltpu.VMEM((SG * SG, CHUNK), jnp.bfloat16),
            pltpu.VMEM((epochs, CHUNK), jnp.bfloat16),
            pltpu.VMEM((2, CHUNK, CHUNK), jnp.float32),
            pltpu.VMEM((CHUNK, TERMS), jnp.bfloat16),
        ]
        * (3 * PAIR)
        + [
            pltpu.SMEM((layers * span + 1,), jnp.int32),
            pltpu.SemaphoreType.DMA((2 * layers * len(groups) + 2 * LAYER,)),
        ],
        input_output_aliases={} if first else {before: 0, before + 1: 1},
        compiler_params=pltpu.CompilerParams(vmem_limit_bytes=8 * MIB),
        cost_estimate=pl.CostEstimate(
            flops=layers * span * 4 * epochs * CHUNK * (NEAR + 1) * PBLK,
            bytes_accessed=1024,
            transcendentals=layers * span * CHUNK * NEAR * PBLK,
        ),
        name="fit",
    )(*tables, *arrays, patches, forms, *screens, *stress, *state)


def partner(values, devices, distance):
    return lax.ppermute(values, "tile", [(i, i ^ distance) for i in range(devices)])


def orders(devices):
    stages = devices.bit_length() - 1
    high = list(range(2, stages))
    return [1] + high, high + [1]


def block_places(devices, here, blocks, local, epochs):
    block = jnp.arange(blocks)
    other = (block // local) ^ here
    seat = block % local
    half = local // 2
    turned = []
    for order in orders(devices):
        spot = 0
        for bit in order:
            spot = spot * 2 + ((other >> bit) & 1)
        turned.append(spot)
    chips = devices // 2
    upper = seat // half
    spot = jnp.where(upper == 0, turned[0], turned[1])
    place = (((other & 1) * 2 + upper) * chips + spot) * half + seat % half
    stages = devices.bit_length() - 1
    held = sum(((other >> (stages - 1 - s)) & 1) << s for s in range(stages))
    return place.astype(jnp.int32), ((held * local + seat) * epochs).astype(jnp.int32)


def halve(kept, given, there, devices):
    total = kept + partner(given, devices, 1).astype(jnp.float32)
    middle = total.shape[0] // 2
    parts = [total[:middle], total[middle:]]
    both = orders(devices)
    stages = len(both[0])
    back = None
    for stage in range(stages):
        got = []
        for side in range(2):
            given = parts[side][parts[side].shape[0] // 2 :]
            if stages - stage <= NARROW:
                given = given.astype(jnp.bfloat16)
            got.append(partner(given, devices, 1 << both[side][stage]))
        for side in range(2):
            if side:
                _, got[1] = lax.optimization_barrier((parts[0], got[1]))
            size = parts[side].shape[0] // 2
            parts[side] = parts[side][:size] + got[side].astype(jnp.float32)
            if back is None:
                _, there = lax.optimization_barrier((parts[0], there))
                back = partner(there, devices, PAIR)
    return jnp.concatenate(parts, axis=0), back


def on_device(
    observations,
    pixel_geometry,
    block_counts,
    block_tiles,
    cutoff_lists,
    patch_geometry,
    stress,
    screens,
):
    devices = lax.axis_size("tile")
    here = lax.axis_index("tile")
    blocks, epochs, width = observations.shape
    local_tiles = screens.shape[0]
    layers = devices // LAYER
    local = stress.shape[1] // PBLK

    slots = LAYER * (2 * blocks // devices) * (width // CHUNK)
    sizes = round_sizes(slots)

    held = jnp.swapaxes(stress.reshape(epochs, local, PBLK), 0, 1).reshape(-1, PBLK)
    obs, pix = pack(
        observations,
        pixel_geometry,
        block_counts,
        block_tiles,
        jnp.reshape(here, (1,)).astype(jnp.int32),
        devices,
        local_tiles,
    )

    _, held = lax.optimization_barrier((pix, held))
    other = partner(held, devices, devices // 2)
    across_screens = partner(screens, devices, PAIR)
    def exchange(parts):
        got = [partner(parts[x], devices, x * LAYER) for x in range(layers - 1, 0, -1)]
        return [parts[0]] + got[::-1]

    pix = exchange(pix)
    distance = devices // 2
    while distance >= LAYER:
        if distance < devices // 2:
            other = partner(held, devices, distance)
        held = jnp.concatenate([held, other], axis=0)
        distance //= 2
    patch_blocks = devices * local
    east, north, depth, compliance = patch_geometry
    origin = patch_geometry[:2, 0]
    strength = compliance * depth * depth
    faces = split(
        jnp.stack(
            [
                strength,
                -strength * (east - origin[0]),
                -strength * (north - origin[1]),
                strength * depth,
            ]
        )
    )
    forms = jnp.concatenate(
        [faces[second] for _, second in CROSS] + [jnp.zeros((8,) + east.shape, jnp.float32)]
    ).astype(jnp.bfloat16)
    forms = jnp.swapaxes(forms.reshape(TERMS, patch_blocks, PBLK), 0, 1)
    patches = jnp.stack([east, north, depth * depth])
    patches = jnp.swapaxes(patches.reshape(3, patch_blocks, PBLK), 0, 1)
    cutoffs = cutoff_lists.reshape(-1)
    held, pix, across_screens = lax.optimization_barrier((held, pix, across_screens))
    places, spots = block_places(devices, here, patch_blocks, local, epochs)
    info = jnp.stack([p[slots, :3, :slots] for p in pix]).astype(jnp.int32).reshape(-1)
    across_screens, forms, patches, cutoffs, info, places, spots = lax.optimization_barrier(
        (across_screens, forms, patches, cutoffs, info, places, spots)
    )
    got = [exchange(o) for o in obs[:PAIR]]
    across = partner(held, devices, PAIR)
    across, got[0] = lax.optimization_barrier((across, got[0]))
    all_stress = [held, across, partner(held, devices, 1), partner(across, devices, 1)]
    all_screens = [
        screens,
        across_screens,
        partner(screens, devices, 1),
        partner(across_screens, devices, 1),
    ]

    tables = (info, cutoffs, places, spots, origin)

    state = (
        jax.ShapeDtypeStruct((patch_blocks, epochs, PBLK), jnp.float32),
        jax.ShapeDtypeStruct((LAYER * local_tiles,) + screens.shape[1:], jnp.float32),
    )
    base = 0
    for i, size in enumerate(sizes):
        first, final = i == 0, i == len(sizes) - 1
        groups = [(base, got[i], pix, base)]
        state = fit(
            tables,
            groups,
            patches,
            forms,
            all_screens,
            all_stress,
            state[:2],
            first,
            final,
        )
        if first:
            all_screens, all_stress = state[2:]
            for late in obs[PAIR:]:
                _, late = lax.optimization_barrier((all_screens, late))
                got.append(exchange(late))
        base += size
    grad, screen_grad, given, next_door, diagonal = state
    own, far = screen_grad[:local_tiles], screen_grad[local_tiles : PAIR * local_tiles]
    there = (far + partner(diagonal, devices, 1).astype(jnp.float32)).astype(jnp.bfloat16)
    grad, back = halve(grad[: grad.shape[0] // 2], given, there, devices)
    screen_gradient = (
        own + partner(next_door, devices, 1).astype(jnp.float32) + back.astype(jnp.float32)
    )
    return (jnp.swapaxes(grad, 0, 1).reshape(epochs, local * PBLK), screen_gradient)


def solution(mesh):
    return jax.shard_map(
        on_device,
        mesh=mesh,
        in_specs=(
            P(("groups", "tile"), None, None),
            P(("groups", "tile"), None, None),
            P(("groups", "tile")),
            P(("groups", "tile")),
            P(),
            P(),
            P(None, ("groups", "tile")),
            P(("groups", "tile"), None, None),
        ),
        out_specs=(P(None, ("groups", "tile")), P(("groups", "tile"), None, None)),
        check_vma=False,
    )
```

```python
import functools

import jax
import jax.numpy as jnp
from jax import lax
from jax.experimental import pallas as pl
from jax.experimental.pallas import tpu as pltpu
from jax.sharding import PartitionSpec as P

PBLK = 256
NEAR = 3
SG = 16
CHUNK = 128
LAYER = 4
PAIR = 2
NARROW = 3
ROUNDS = (4, 6, 6)
MIB = 1 << 20
TERMS = 32
CROSS = ((0, 0), (0, 1), (1, 0), (0, 2), (1, 1), (2, 0))


def round_sizes(slots):
    return [slots * r // sum(ROUNDS) for r in ROUNDS]


def pack_kernel(local_tiles, layers, slots, here, tiles, counts, obs_in, pix_in, *rest):
    sizes = round_sizes(slots)
    total = len(sizes)
    obs_out, pix_out = rest[: total * layers], rest[total * layers : (total + 1) * layers]
    obs, pix, obs_all, pix_all, fill, sems = rest[(total + 1) * layers :]
    loads = [
        pltpu.make_async_copy(obs_in, obs, sems.at[0]),
        pltpu.make_async_copy(pix_in, pix, sems.at[1]),
    ]
    for copy in loads:
        copy.start()
    my_layer, my_seat = lax.div(here[0], LAYER), lax.rem(here[0], LAYER)
    chunks = pix.shape[2] // CHUNK
    stride = slots + 1
    for x in range(layers):
        fill[x] = 0
    lane = lax.broadcasted_iota(jnp.int32, (8, CHUNK), 1)
    row = lax.broadcasted_iota(jnp.int32, (8, CHUNK), 0)
    for copy in loads:
        copy.wait()

    def put(b, infos):
        tile = tiles[b]
        count = counts[b]
        owner = lax.div(tile, local_tiles)
        x = lax.div(owner, LAYER) ^ my_layer
        seat = lax.rem(owner, LAYER) ^ my_seat
        spot = lax.rem(seat, PAIR) * PAIR + lax.div(seat, PAIR)
        screen = spot * local_tiles + lax.rem(tile, local_tiles)
        slot = fill[x]
        fill[x] = slot + lax.div(count + CHUNK - 1, CHUNK)
        for c in range(chunks):
            at = slot + c
            live = jnp.clip(count - c * CHUNK, 0, CHUNK)
            obs_all[x * stride + at] = obs[b, :, c * CHUNK : (c + 1) * CHUNK]
            pix_all[x * stride + at] = pix[b, :, c * CHUNK : (c + 1) * CHUNK]
            entry = jnp.where(row == 0, live, jnp.where(row == 1, tile, screen))
            here_only = (lane == at) & (row < 3)
            infos = tuple(
                jnp.where(here_only & (x == i), entry, info) for i, info in enumerate(infos)
            )
        return infos

    infos = lax.fori_loop(
        0, obs.shape[0], put, tuple(jnp.zeros((8, CHUNK), jnp.int32) for _ in range(layers))
    )
    copies = []
    for x in range(layers):
        at = x * stride
        pix_all[at + slots] = infos[x].astype(jnp.float32)
        copies.append((pix_all.at[pl.ds(at, stride)], pix_out[x]))
        for i, size in enumerate(sizes):
            copies.append((obs_all.at[pl.ds(at, size)], obs_out[i * layers + x]))
            at += size
    copies = [pltpu.make_async_copy(a, b, sems.at[i]) for i, (a, b) in enumerate(copies)]
    for copy in copies:
        copy.start()
    for copy in copies:
        copy.wait()


def pack(observations, pixel_geometry, block_counts, block_tiles, here, devices, local_tiles):
    blocks, epochs, width = observations.shape
    layers = devices // LAYER
    slots = LAYER * (2 * blocks // devices) * (width // CHUNK)
    sizes = round_sizes(slots)
    smem = pl.BlockSpec(memory_space=pltpu.SMEM)
    hbm = pl.BlockSpec(memory_space=pl.ANY)
    pix_part = jax.ShapeDtypeStruct((slots + 1, 8, CHUNK), jnp.float32)
    out = pl.pallas_call(
        functools.partial(pack_kernel, local_tiles, layers, slots),
        in_specs=[smem, smem, smem, hbm, hbm],
        out_specs=[hbm] * ((len(sizes) + 1) * layers),
        out_shape=[
            jax.ShapeDtypeStruct((size, epochs, CHUNK), observations.dtype)
            for size in sizes
            for _ in range(layers)
        ]
        + [pix_part] * layers,
        scratch_shapes=[
            pltpu.VMEM(observations.shape, observations.dtype),
            pltpu.VMEM(pixel_geometry.shape, jnp.float32),
            pltpu.VMEM((layers * (slots + 1), epochs, CHUNK), observations.dtype),
            pltpu.VMEM((layers * (slots + 1), 8, CHUNK), jnp.float32),
            pltpu.SMEM((layers,), jnp.int32),
            pltpu.SemaphoreType.DMA(((len(sizes) + 1) * layers,)),
        ],
        compiler_params=pltpu.CompilerParams(vmem_limit_bytes=10 * MIB),
        name="pack",
    )(here, block_tiles, block_counts, observations, pixel_geometry)
    rounds = len(sizes)
    return [out[i * layers : (i + 1) * layers] for i in range(rounds)], out[rounds * layers :]


def split(values):
    parts = []
    for _ in range(3):
        part = lax.reduce_precision(values, 8, 7)
        parts.append(part)
        values = values - part
    return parts


def kernel_split(values):
    parts = []
    for _ in range(3):
        part = values.astype(jnp.bfloat16).astype(jnp.float32)
        parts.append(part)
        values = values - part
    return parts


def fit_kernel(first, final, layers, slots, groups, *refs):
    info, cutoffs, places, spots, origin = refs[:5]
    rest = refs[5:]
    obs_in, pix_in = [], []
    for _ in groups:
        obs_in.append(rest[:layers])
        pix_in.append(rest[layers : 2 * layers])
        rest = rest[2 * layers :]
    patches, forms = rest[:2]
    rest = rest[1:]
    if first:
        screen_parts, stress_parts = rest[1 : 1 + LAYER], rest[1 + LAYER : 1 + 2 * LAYER]
        rest = rest[1 + 2 * LAYER :]
        grad, screen_grad, screens, stress = rest[:4]
        rest = rest[4:]
    else:
        screens, stress = rest[1:3]
        grad, screen_grad = rest[5:7]
        rest = rest[7:]
    outs = rest[:3] if final else ()
    rest = rest[len(outs) :]
    obs, pix = rest[:2]
    buffers = rest[2 : 2 + 15 * PAIR]
    items, sems = rest[2 + 15 * PAIR :]
    sets = [
        [buffers[5 * (PAIR * i + lane) : 5 * (PAIR * i + lane) + 5] for lane in range(PAIR)]
        for i in range(3)
    ]
    epochs = obs.shape[1]
    base = groups[0][0]
    span = sum(size for _, _, size in groups)
    local_tiles = screens.shape[0] // LAYER

    loads = []
    for x in range(layers):
        at = x * span
        for g, (_, low, size) in enumerate(groups):
            loads.append((obs_in[g][x], obs.at[pl.ds(at, size)]))
            loads.append((pix_in[g][x].at[pl.ds(low, size)], pix.at[pl.ds(at, size)]))
            at += size
    if first:
        for parts, whole in ((screen_parts, screens), (stress_parts, stress)):
            size = whole.shape[0] // LAYER
            for i, part in enumerate(parts):
                loads.append((part, whole.at[pl.ds(i * size, size)]))
    loads = [pltpu.make_async_copy(a, b, sems.at[i]) for i, (a, b) in enumerate(loads)]
    for copy in loads:
        copy.start()
    if first:
        grad[...] = jnp.zeros_like(grad)
        screen_grad[...] = jnp.zeros_like(screen_grad)

    def info_of(slot, kind):
        x = lax.div(slot, span)
        return info[(x * 3 + kind) * slots + base + lax.rem(slot, span)]

    def list_slot(slot, total):
        items[total] = slot
        return total + jnp.where(info_of(slot, 0) > 0, 1, 0)

    total = lax.fori_loop(0, layers * span, list_slot, 0)
    for copy in loads:
        copy.wait()

    def item_of(i):
        slot = items[jnp.minimum(i, total - 1)]
        tile = info_of(slot, 1)
        return slot, [cutoffs[tile * NEAR + k] for k in range(NEAR)]

    def spread(i, held):
        rows = pix[item_of(i)[0]]
        columns = rows.T
        for i in range(2):
            held[0][i] = jnp.broadcast_to(columns[:, i : i + 1], (CHUNK, CHUNK))
        le, ln = rows[4:5], rows[5:6]
        along = le * (rows[0:1] - origin[0]) + ln * (rows[1:2] - origin[1])
        row = lax.broadcasted_iota(jnp.int32, (8, CHUNK), 0)
        factors = jnp.where(
            row == 0, along, jnp.where(row == 1, le, jnp.where(row == 2, ln, rows[6:7]))
        )
        parts = kernel_split(factors)
        low = row < 4
        tiles = []
        for first_part, second_part in zip(CROSS[::2], CROSS[1::2]):
            upper = jnp.concatenate([parts[second_part[0]][:4]] * 2, axis=0)
            tiles.append(jnp.where(low, parts[first_part[0]], upper))
        tiles.append(jnp.zeros((8, CHUNK), jnp.float32))
        held[1][...] = jnp.concatenate(tiles, axis=0).T.astype(jnp.bfloat16)

    def make_strips(near, k, begin, end, held, green):
        patch = [
            jnp.broadcast_to(patches[near[k], r : r + 1], (8, PBLK)) for r in range(3)
        ]
        alongs = jnp.dot(
            held[1][begin:end], forms[near[k]], preferred_element_type=jnp.float32
        )
        for low in range(begin, end, 16):
            along = alongs[low - begin : low - begin + 16]
            inverses = []
            for at in (low, low + 8):
                east, north = (
                    jnp.concatenate([held[0][i, at : at + 8]] * (PBLK // CHUNK), axis=1)
                    for i in range(2)
                )
                dx = east - patch[0]
                dy = north - patch[1]
                inverses.append(lax.rsqrt(dx * dx + dy * dy + patch[2]))
            inverse = jnp.concatenate(inverses, axis=0)
            green[low : low + 16, k * PBLK : (k + 1) * PBLK] = (
                along * inverse * inverse * inverse
            ).astype(jnp.bfloat16)

    def make_hats(rows, hats):
        node = lax.broadcasted_iota(jnp.int32, (SG, CHUNK), 0).astype(jnp.float32)
        across = jnp.maximum(0.0, 1.0 - jnp.abs(rows[2:3] - node))
        upward = jnp.maximum(0.0, 1.0 - jnp.abs(rows[3:4] - node))
        for a in range(SG):
            hats[a * SG : (a + 1) * SG] = (across[a : a + 1] * upward).astype(jnp.bfloat16)

    def make_head(i, buffers):
        slot, near = item_of(i)
        make_hats(pix[slot], buffers[1])
        return near

    def predict(i, buffers):
        green, hats = buffers[:2]
        slot, near = item_of(i)
        model = jnp.dot(
            screens[info_of(slot, 2)], hats[...], preferred_element_type=jnp.float32
        )
        for k in range(NEAR):
            model += lax.dot_general(
                stress[pl.ds(pl.multiple_of(spots[near[k]], 16), epochs), :],
                green[:, k * PBLK : (k + 1) * PBLK],
                (((1,), (1,)), ((), ())),
                preferred_element_type=jnp.float32,
            )
        return model

    def weigh(i, model, buffers):
        slot, _ = item_of(i)
        live = jnp.where(i < total, info_of(slot, 0), 0)
        lane = lax.broadcasted_iota(jnp.int32, (1, CHUNK), 1)
        scale = jnp.where(lane < live, pix[slot, 7:8, :], 0.0)
        buffers[2][...] = ((model - obs[slot].astype(jnp.float32)) * scale).astype(jnp.bfloat16)

    def add_patch(near, k, buffers):
        grad[places[near[k]]] += jnp.dot(
            buffers[2][...],
            buffers[0][:, k * PBLK : (k + 1) * PBLK],
            preferred_element_type=jnp.float32,
        )

    def add_screen(slot, buffers):
        screen_grad[info_of(slot, 2)] += lax.dot_general(
            buffers[2][...],
            buffers[1][...],
            (((1,), (1,)), ((), ())),
            preferred_element_type=jnp.float32,
        )

    lanes = range(PAIR)
    half = CHUNK // 2

    def spread_pair(j, buffers):
        for lane in lanes:
            spread(PAIR * j + lane, buffers[lane][3:])

    def make_pair(j, buffers):
        for lane in lanes:
            near = make_head(PAIR * j + lane, buffers[lane])
            for k in range(NEAR):
                for low in (0, half):
                    make_strips(near, k, low, low + half, buffers[lane][3:], buffers[lane][0])

    def model_pair(j, buffers):
        for lane in lanes:
            model = predict(PAIR * j + lane, buffers[lane])
            weigh(PAIR * j + lane, model, buffers[lane])

    def turn(j, using, middle, making):
        now = [item_of(PAIR * j + lane) for lane in lanes]
        coming = [PAIR * (j + 1) + lane for lane in lanes]
        near = [make_head(PAIR * (j + 2) + lane, making[lane]) for lane in lanes]
        models = [predict(coming[lane], middle[lane]) for lane in lanes]

        def strips(k, lane):
            for low in (0, half):
                make_strips(
                    near[lane], k, low, low + half, making[lane][3:], making[lane][0]
                )

        def adds(k):
            for lane in lanes:
                add_patch(now[lane][1], k, using[lane])

        strips(0, 0)
        adds(0)
        spread_pair(j + 3, using)
        strips(0, 1)
        adds(1)
        strips(1, 0)
        for lane in lanes:
            weigh(coming[lane], models[lane], middle[lane])
        strips(1, 1)
        adds(2)
        strips(2, 0)
        for lane in lanes:
            add_screen(now[lane][0], using[lane])
        strips(2, 1)

    @pl.when(total > 0)
    def _():
        pairs = lax.div(total + PAIR - 1, PAIR)
        for j in range(3):
            spread_pair(j, sets[j])
        make_pair(0, sets[0])
        make_pair(1, sets[1])
        model_pair(0, sets[0])

        def step(i, _):
            for at in range(3):
                j = 3 * i + at

                @pl.when(j < pairs)
                def _():
                    turn(j, sets[at], sets[(at + 1) % 3], sets[(at + 2) % 3])

            return 0

        lax.fori_loop(0, lax.div(pairs + 2, 3), step, 0)

    if final:
        half = grad.shape[0] // 2
        outs[0][...] = grad[half:].astype(outs[0].dtype)
        for i, out in enumerate(outs[1:]):
            low = (PAIR + i) * local_tiles
            out[...] = screen_grad[low : low + local_tiles].astype(out.dtype)


def fit(tables, groups, patches, forms, screens, stress, state, first, final):
    layers = len(groups[0][1])
    slots = tables[0].shape[0] // (3 * layers)
    smem = pl.BlockSpec(memory_space=pltpu.SMEM)
    vmem = pl.BlockSpec(memory_space=pltpu.VMEM)
    hbm = pl.BlockSpec(memory_space=pl.ANY)
    spans = tuple((base, low, obs[0].shape[0]) for base, obs, _, low in groups)
    arrays = [a for _, obs, pix, _ in groups for a in (*obs, *pix)]
    span = sum(size for _, _, size in spans)
    blocks, epochs = state[0].shape[0], state[0].shape[1]
    out_shape = [jax.ShapeDtypeStruct(a.shape, a.dtype) for a in state]
    if first:
        state = ()
        for parts in (screens, stress):
            shape = (LAYER * parts[0].shape[0],) + parts[0].shape[1:]
            out_shape.append(jax.ShapeDtypeStruct(shape, parts[0].dtype))
    else:
        screens, stress = [screens], [stress]
    if final:
        out_shape.append(jax.ShapeDtypeStruct((blocks // 2, epochs, PBLK), jnp.bfloat16))
        shape = (state[1].shape[0] // LAYER,) + state[1].shape[1:]
        out_shape += [jax.ShapeDtypeStruct(shape, jnp.bfloat16)] * 2
    before = len(tables) + len(arrays) + 2 + len(screens) + len(stress)
    return pl.pallas_call(
        functools.partial(fit_kernel, first, final, layers, slots, spans),
        in_specs=[smem] * len(tables)
        + [hbm] * len(arrays)
        + [vmem] * 2
        + [hbm if first else vmem] * (len(screens) + len(stress))
        + [vmem] * len(state),
        out_specs=[vmem] * len(out_shape),
        out_shape=out_shape,
        scratch_shapes=[
            pltpu.VMEM((layers * span, epochs, CHUNK), arrays[0].dtype),
            pltpu.VMEM((layers * span, 8, CHUNK), jnp.float32),
        ]
        + [
            pltpu.VMEM((CHUNK, NEAR * PBLK), jnp.bfloat16),
            pltpu.VMEM((SG * SG, CHUNK), jnp.bfloat16),
            pltpu.VMEM((epochs, CHUNK), jnp.bfloat16),
            pltpu.VMEM((2, CHUNK, CHUNK), jnp.float32),
            pltpu.VMEM((CHUNK, TERMS), jnp.bfloat16),
        ]
        * (3 * PAIR)
        + [
            pltpu.SMEM((layers * span + 1,), jnp.int32),
            pltpu.SemaphoreType.DMA((2 * layers * len(groups) + 2 * LAYER,)),
        ],
        input_output_aliases={} if first else {before: 0, before + 1: 1},
        compiler_params=pltpu.CompilerParams(vmem_limit_bytes=8 * MIB),
        cost_estimate=pl.CostEstimate(
            flops=layers * span * 4 * epochs * CHUNK * (NEAR + 1) * PBLK,
            bytes_accessed=1024,
            transcendentals=layers * span * CHUNK * NEAR * PBLK,
        ),
        name="fit",
    )(*tables, *arrays, patches, forms, *screens, *stress, *state)


def partner(values, devices, distance):
    return lax.ppermute(values, "tile", [(i, i ^ distance) for i in range(devices)])


def orders(devices):
    stages = devices.bit_length() - 1
    high = list(range(2, stages))
    return [1] + high, high + [1]


def block_places(devices, here, blocks, local, epochs):
    block = jnp.arange(blocks)
    other = (block // local) ^ here
    seat = block % local
    half = local // 2
    turned = []
    for order in orders(devices):
        spot = 0
        for bit in order:
            spot = spot * 2 + ((other >> bit) & 1)
        turned.append(spot)
    chips = devices // 2
    upper = seat // half
    spot = jnp.where(upper == 0, turned[0], turned[1])
    place = (((other & 1) * 2 + upper) * chips + spot) * half + seat % half
    stages = devices.bit_length() - 1
    held = sum(((other >> (stages - 1 - s)) & 1) << s for s in range(stages))
    return place.astype(jnp.int32), ((held * local + seat) * epochs).astype(jnp.int32)


def halve(kept, given, there, devices):
    total = kept + partner(given, devices, 1).astype(jnp.float32)
    middle = total.shape[0] // 2
    parts = [total[:middle], total[middle:]]
    both = orders(devices)
    stages = len(both[0])
    back = None
    for stage in range(stages):
        got = []
        for side in range(2):
            given = parts[side][parts[side].shape[0] // 2 :]
            if stages - stage <= NARROW:
                given = given.astype(jnp.bfloat16)
            got.append(partner(given, devices, 1 << both[side][stage]))
        for side in range(2):
            if side:
                _, got[1] = lax.optimization_barrier((parts[0], got[1]))
            size = parts[side].shape[0] // 2
            parts[side] = parts[side][:size] + got[side].astype(jnp.float32)
            if back is None:
                _, there = lax.optimization_barrier((parts[0], there))
                back = partner(there, devices, PAIR)
    return jnp.concatenate(parts, axis=0), back


def on_device(
    observations,
    pixel_geometry,
    block_counts,
    block_tiles,
    cutoff_lists,
    patch_geometry,
    stress,
    screens,
):
    devices = lax.axis_size("tile")
    here = lax.axis_index("tile")
    blocks, epochs, width = observations.shape
    local_tiles = screens.shape[0]
    layers = devices // LAYER
    local = stress.shape[1] // PBLK

    slots = LAYER * (2 * blocks // devices) * (width // CHUNK)
    sizes = round_sizes(slots)

    held = jnp.swapaxes(stress.reshape(epochs, local, PBLK), 0, 1).reshape(-1, PBLK)
    other = partner(held, devices, devices // 2)
    across_screens = partner(screens, devices, PAIR)
    obs, pix = pack(
        observations,
        pixel_geometry,
        block_counts,
        block_tiles,
        jnp.reshape(here, (1,)).astype(jnp.int32),
        devices,
        local_tiles,
    )

    def exchange(parts):
        got = [partner(parts[x], devices, x * LAYER) for x in range(layers - 1, 0, -1)]
        return [parts[0]] + got[::-1]

    distance = devices // 2
    while distance >= LAYER:
        if distance < devices // 2:
            other = partner(held, devices, distance)
        held = jnp.concatenate([held, other], axis=0)
        if distance == devices // 2:
            _, pix = lax.optimization_barrier((held, pix))
            pix = exchange(pix)
        distance //= 2
    patch_blocks = devices * local
    east, north, depth, compliance = patch_geometry
    origin = patch_geometry[:2, 0]
    strength = compliance * depth * depth
    faces = split(
        jnp.stack(
            [
                strength,
                -strength * (east - origin[0]),
                -strength * (north - origin[1]),
                strength * depth,
            ]
        )
    )
    forms = jnp.concatenate(
        [faces[second] for _, second in CROSS] + [jnp.zeros((8,) + east.shape, jnp.float32)]
    ).astype(jnp.bfloat16)
    forms = jnp.swapaxes(forms.reshape(TERMS, patch_blocks, PBLK), 0, 1)
    patches = jnp.stack([east, north, depth * depth])
    patches = jnp.swapaxes(patches.reshape(3, patch_blocks, PBLK), 0, 1)
    cutoffs = cutoff_lists.reshape(-1)
    held, pix[1] = lax.optimization_barrier((held, pix[1]))
    places, spots = block_places(devices, here, patch_blocks, local, epochs)
    info = jnp.stack([p[slots, :3, :slots] for p in pix]).astype(jnp.int32).reshape(-1)
    across_screens, forms, patches, cutoffs, info, places, spots = lax.optimization_barrier(
        (across_screens, forms, patches, cutoffs, info, places, spots)
    )
    got = [exchange(o) for o in obs[:PAIR]]
    across = partner(held, devices, PAIR)
    across, got[0] = lax.optimization_barrier((across, got[0]))
    all_stress = [held, across, partner(held, devices, 1), partner(across, devices, 1)]
    all_screens = [
        screens,
        across_screens,
        partner(screens, devices, 1),
        partner(across_screens, devices, 1),
    ]

    tables = (info, cutoffs, places, spots, origin)

    state = (
        jax.ShapeDtypeStruct((patch_blocks, epochs, PBLK), jnp.float32),
        jax.ShapeDtypeStruct((LAYER * local_tiles,) + screens.shape[1:], jnp.float32),
    )
    base = 0
    for i, size in enumerate(sizes):
        first, final = i == 0, i == len(sizes) - 1
        groups = [(base, got[i], pix, base)]
        state = fit(
            tables,
            groups,
            patches,
            forms,
            all_screens,
            all_stress,
            state[:2],
            first,
            final,
        )
        if first:
            all_screens, all_stress = state[2:]
            for late in obs[PAIR:]:
                _, late = lax.optimization_barrier((all_screens, late))
                got.append(exchange(late))
        base += size
    grad, screen_grad, given, next_door, diagonal = state
    own, far = screen_grad[:local_tiles], screen_grad[local_tiles : PAIR * local_tiles]
    there = (far + partner(diagonal, devices, 1).astype(jnp.float32)).astype(jnp.bfloat16)
    grad, back = halve(grad[: grad.shape[0] // 2], given, there, devices)
    screen_gradient = (
        own + partner(next_door, devices, 1).astype(jnp.float32) + back.astype(jnp.float32)
    )
    return (jnp.swapaxes(grad, 0, 1).reshape(epochs, local * PBLK), screen_gradient)


def solution(mesh):
    return jax.shard_map(
        on_device,
        mesh=mesh,
        in_specs=(
            P(("groups", "tile"), None, None),
            P(("groups", "tile"), None, None),
            P(("groups", "tile")),
            P(("groups", "tile")),
            P(),
            P(),
            P(None, ("groups", "tile")),
            P(("groups", "tile"), None, None),
        ),
        out_specs=(P(None, ("groups", "tile")), P(("groups", "tile"), None, None)),
        check_vma=False,
    )
```
